128 devices in a mesh: dp: 16 (over y, z_lo, core), hid: 8 (over x, z_hi).
Axes of the slice: x: 4, y: 4, z: 4 (z_hi: 2, z_lo: 2; z = z_hi * 2 + z_lo), core: 2. Of those that a mesh axis runs over, the one named last changes fastest.
Arguments:
- block_in: bfloat16 [32, 256, 1152], P('dp'), may hold values from -6 to 6
- time_tokens: bfloat16 [32, 4, 1152], P('dp'), may hold values from -6 to 6
- layout: int32 [32], P('dp'), may hold values from 0 to 1
- norm_gain: float32 [2, 2, 1152], replicated, may hold values from 0.5 to 1.5
- norm_bias: float32 [2, 2, 1152], replicated, may hold values from -3 to 3
- w_qkv: bfloat16 [2, 1152, 3456], replicated, may hold values from -0.1875 to 0.1875
- w_time: bfloat16 [2, 1152, 3456], replicated, may hold values from -0.1875 to 0.1875
- rel_table: float32 [2, 16, 31, 31], replicated, may hold values from -4 to 4
- w_out: bfloat16 [2, 1152, 1152], replicated, may hold values from -0.5 to 0.5
- w_up: bfloat16 [2, 1152, 4608], P(None, None, 'hid'), may hold values from -0.1875 to 0.1875
- b_up: float32 [2, 4608], P(None, 'hid'), may hold values from -3 to 3
- w_down: bfloat16 [2, 4608, 1152], P(None, 'hid'), may hold values from -0.09375 to 0.09375
- b_down: float32 [2, 1152], replicated, may hold values from -3 to 3
- cotangent: bfloat16 [32, 256, 1152], P('dp'), may hold values from -6 to 6
Outputs:
- block_out: float32 [32, 256, 1152], P('dp')
- grad_in: float32 [32, 256, 1152], P('dp')
- grad_time: float32 [32, 4, 1152], P('dp')
- grad_gain: float32 [2, 2, 1152], replicated
- grad_norm_bias: float32 [2, 2, 1152], replicated
- grad_qkv: float32 [2, 1152, 3456], P(None, ('dp', 'hid'))
- grad_time_w: float32 [2, 1152, 3456], P(None, ('dp', 'hid'))
- grad_table: float32 [2, 16, 31, 31], replicated
- grad_out_w: float32 [2, 1152, 1152], P(None, ('dp', 'hid'))
- grad_up: float32 [2, 1152, 4608], P(None, 'dp', 'hid')
- grad_b_up: float32 [2, 4608], replicated
- grad_down: float32 [2, 4608, 1152], P(None, 'hid', 'dp')
- grad_b_down: float32 [2, 1152], replicated
The draws below stay inside these ranges and needn't reach their ends.
Inputs may be any that keep to these rules, and one draw needn't show every extreme that they name: `layout`: 0: the row holds one image of 16 x 16 tokens; 1: it holds 4 images of 8 x 8 tokens one after another.
All inputs are finite; a program needn't handle non-finite values.
Results may differ from the reference program's by a relative error of at most 0.02.
Values may be sent and summed in bfloat16 or wider, within the bound.
A program may use at most 256 MiB of HBM per device.

```python
import jax
import jax.numpy as jnp
from jax import lax

D = 1152
HEADS = 16
HEAD_DIM = 72
FF = 4608
LAYERS = 2
GRID = 16
SUB = 8
ROW_LEN = 256
SLOTS = 4
REL = 31
ROWS = 32


def place_ends(array, key, low, high):
    spot = [jax.random.randint(jax.random.fold_in(key, axis), (), 0, length) for axis, length in enumerate(array.shape)]
    longest = array.shape.index(max(array.shape))
    beside = spot[:longest] + [(spot[longest] + 1) % array.shape[longest]] + spot[longest + 1:]
    return array.at[tuple(spot)].set(low).at[tuple(beside)].set(high)


def block_levels(stream_key, dims, cuts, least, largest):
    def one(dim, shards_of):
        draws = jax.random.uniform(jax.random.fold_in(jax.random.fold_in(stream_key, 6), dim), (shards_of,), jnp.float32, least / len(cuts), largest / len(cuts))
        return jnp.repeat(jnp.exp(draws), dims[dim] // shards_of).reshape((-1,) + (1,) * (len(dims) - dim - 1))

    level = one(*cuts[0])
    for cut in cuts[1:]:
        level = level * one(*cut)
    return level


def normal_values(rng, extent, spread, reach, shards=(), kind=jnp.bfloat16):
    drawn = jax.random.normal(rng, extent, jnp.float32) * spread
    if len(shards) > 0:
        drawn = block_levels(rng, extent, shards, -0.22, 0.18) * drawn
    return jnp.clip(drawn, min=-reach, max=reach).astype(kind)


def setup_inputs(seed: int = 0) -> dict:
    key_of = jax.random.split(jax.random.key(seed), 15)
    return {
        "block_in": normal_values(key_of[0], (ROWS, ROW_LEN, D), 1.0, 6.0, ((0, 16),)),
        "time_tokens": normal_values(key_of[1], (ROWS, SLOTS, D), 1.0, 6.0, ((0, 16),)),
        "layout": place_ends(jax.random.randint(key_of[2], (ROWS,), 0, 2), jax.random.fold_in(key_of[2], 1), 0, 1).astype(jnp.int32),
        "norm_gain": jnp.clip(1.0 + 0.1 * jax.random.normal(key_of[3], (LAYERS, 2, D), jnp.float32), 0.5, 1.5),
        "norm_bias": normal_values(key_of[4], (LAYERS, 2, D), 0.5, 3.0, (), jnp.float32),
        "w_qkv": normal_values(key_of[5], (LAYERS, D, 3 * D), D ** -0.5, 0.1875),
        "w_time": normal_values(key_of[6], (LAYERS, D, 3 * D), D ** -0.5, 0.1875),
        "rel_table": normal_values(key_of[7], (LAYERS, HEADS, REL, REL), 1.0, 4.0, (), jnp.float32),
        "w_out": normal_values(key_of[8], (LAYERS, D, D), (D // 8) ** -0.5, 0.5),
        "w_up": normal_values(key_of[9], (LAYERS, D, FF), D ** -0.5, 0.1875, ((2, 8),)),
        "b_up": normal_values(key_of[10], (LAYERS, FF), 0.5, 3.0, ((1, 8),), jnp.float32),
        "w_down": normal_values(key_of[11], (LAYERS, FF, D), FF ** -0.5, 0.09375, ((1, 8),)),
        "b_down": normal_values(key_of[12], (LAYERS, D), 0.5, 3.0, (), jnp.float32),
        "cotangent": normal_values(key_of[13], (ROWS, ROW_LEN, D), 1.0, 6.0, ((0, 16),)),
    }


@jax.custom_vjp
def low(v):
    return lax.optimization_barrier(v.astype(jnp.bfloat16)).astype(jnp.float32)

@jax.custom_vjp
def low_back(v):
    return v

def low_keep(v):
    return (low(v), None)

def low_pass(kept, grad):
    return (grad,)

def back_keep(v):
    return (v, None)

def back_low(kept, grad):
    return (low(grad),)
low.defvjp(low_keep, low_pass)
low_back.defvjp(back_keep, back_low)
HIGHEST = lax.Precision.HIGHEST
MASKED_LOGIT = -1e+30
NORM_EPSILON = 1e-06

def layer_norm(values, gain_row, shift_row):
    centre = values - lax.optimization_barrier(jnp.mean(values, -1, keepdims=True))
    inverse = lax.rsqrt(lax.optimization_barrier(jnp.mean(centre * centre, -1, keepdims=True)) + NORM_EPSILON)
    return centre * inverse * gain_row + shift_row

def bias_tables(rel_bias):
    position = jnp.arange(ROW_LEN)
    wide_y = position // GRID
    wide_x = position % GRID
    inner = position % (SUB * SUB)
    narrow_y = inner // SUB
    narrow_x = inner % SUB
    bias_single = rel_bias[:, wide_y[:, None] - wide_y[None, :] + GRID - 1, wide_x[:, None] - wide_x[None, :] + GRID - 1]
    bias_quad = rel_bias[:, narrow_y[:, None] - narrow_y[None, :] + GRID - 1, narrow_x[:, None] - narrow_x[None, :] + GRID - 1]
    return (bias_single, bias_quad)

def row_attention(qkv_row, bias_row, allowed):
    queries = qkv_row[:, :D].reshape(ROW_LEN, HEADS, HEAD_DIM)
    key_heads = qkv_row[:, D:2 * D].reshape(ROW_LEN, HEADS, HEAD_DIM)
    values = qkv_row[:, 2 * D:].reshape(ROW_LEN, HEADS, HEAD_DIM)
    scores = jnp.einsum('qhd,khd->hqk', queries, key_heads, precision=HIGHEST) * HEAD_DIM ** (-0.5)
    scores = low_back(scores)
    logits = jnp.where(allowed, scores + bias_row, MASKED_LOGIT)
    row_top = lax.optimization_barrier(jnp.max(logits, -1, keepdims=True))
    expo_term = jnp.exp(logits - row_top)
    weights = low(expo_term / lax.optimization_barrier(jnp.sum(expo_term, -1, keepdims=True)))
    return jnp.einsum('hqk,khd->qhd', weights, values, precision=HIGHEST).reshape(ROW_LEN, D)

def forward(layout, block_in, time_tokens, norm_gain, norm_bias, w_qkv, w_time, rel_table, w_out, w_up, b_up, w_down, b_down):
    position = jnp.arange(ROW_LEN)
    image_of = position // (SUB * SUB)
    is_four = layout == 1
    image_slot = jnp.where(is_four[:, None], image_of[None, :], 0)
    slot_pick = (image_slot[:, :, None] == jnp.arange(SLOTS)[None, None, :]).astype(jnp.float32)
    same_image = image_of[:, None] == image_of[None, :]
    current = block_in
    for layer_idx in range(LAYERS):
        first = low(layer_norm(current, norm_gain[layer_idx, 0], norm_bias[layer_idx, 0]))
        time_proj = jnp.einsum('rsd,de->rse', time_tokens, w_time[layer_idx], precision=HIGHEST)
        mixed = jnp.einsum('rtd,de->rte', first, w_qkv[layer_idx], precision=HIGHEST) + jnp.einsum('rts,rse->rte', slot_pick, time_proj, precision=HIGHEST)
        mixed = low(low_back(mixed))
        bias_single, bias_quad = bias_tables(rel_table[layer_idx])

        def attend_row(packed):
            qkv_row, flag = packed
            bias_row = jnp.where(flag, bias_quad, bias_single)
            allowed = jnp.logical_or(jnp.logical_not(flag), same_image)
            return row_attention(qkv_row, bias_row, allowed)
        attended = lax.map(jax.checkpoint(attend_row), (mixed, is_four))
        attended = low(low_back(attended))
        middle = current + low_back(jnp.einsum('rtd,de->rte', attended, w_out[layer_idx], precision=HIGHEST))
        second = low(layer_norm(middle, norm_gain[layer_idx, 1], norm_bias[layer_idx, 1]))
        pre_act = low_back(jnp.einsum('rtd,df->rtf', second, w_up[layer_idx], precision=HIGHEST) + b_up[layer_idx])
        hidden = low(jax.nn.gelu(pre_act, approximate=True))
        current = middle + low_back(jnp.einsum('rtf,fd->rtd', hidden, w_down[layer_idx], precision=HIGHEST) + b_down[layer_idx])
    return current

def reference(block_in, time_tokens, layout, norm_gain, norm_bias, w_qkv, w_time, rel_table, w_out, w_up, b_up, w_down, b_down, cotangent):

    def wrapped(*params):
        return forward(layout, *params)
    primals = (block_in.astype(jnp.float32), time_tokens.astype(jnp.float32), norm_gain, norm_bias, w_qkv.astype(jnp.float32), w_time.astype(jnp.float32), rel_table, w_out.astype(jnp.float32), w_up.astype(jnp.float32), b_up, w_down.astype(jnp.float32), b_down)
    block_out, pullback = jax.vjp(wrapped, *primals)
    gradients = pullback(cotangent.astype(jnp.float32))
    return (block_out, gradients[0], gradients[1], gradients[2], gradients[3], gradients[4], gradients[5], gradients[6], gradients[7], gradients[8], gradients[9], gradients[10], gradients[11])
```

```python
import functools

import jax
import jax.numpy as jnp
from jax import lax
from jax.experimental import pallas as pl
from jax.experimental.pallas import tpu as pltpu
from jax.sharding import PartitionSpec as P

D = 1152
HEADS = 16
HEAD_DIM = 72
FF = 4608
LAYERS = 2
GRID = 16
SUB = 8
ROW_LEN = 256
SLOTS = 4
REL = 31
DP = 16
HID = 8
UNITS = FF // HID
KEPT = D // (DP * HID)
TOKENS = 512
OWN = ROW_LEN // HID
SCALE = HEAD_DIM ** (-0.5)
MASKED_LOGIT = -1e30
NORM_EPSILON = 1e-06
F32 = jnp.float32
BF16 = jnp.bfloat16
MESH = pl.DeviceIdType.MESH
VMEM_LIMIT = 60 * 1024 * 1024
HIGHEST = lax.Precision.HIGHEST


def contract(a, b, da, db, precision=None):
    return lax.dot_general(
        a, b, (((da,), (db,)), ((), ())), preferred_element_type=F32, precision=precision
    )


def dot(a, b):
    return contract(a, b, 1, 0)


def dot_nt(a, b):
    return contract(a, b, 1, 1)


def dot_tn(a, b):
    return contract(a, b, 0, 0)


def span(start, size, multiple):
    return pl.ds(pl.multiple_of(start, multiple), size)


def gelu_parts(v):
    c = 0.7978845608028654
    square = v * v
    t = jnp.tanh(c * v * (1.0 + 0.044715 * square))
    return t, square


def gelu(v):
    t, _ = gelu_parts(v)
    return 0.5 * v * (1.0 + t)


def gelu_slope(v):
    c = 0.7978845608028654
    t, square = gelu_parts(v)
    return 0.5 * (1.0 + t) + 0.5 * v * (1.0 - t * t) * (c * (1.0 + 3.0 * 0.044715 * square))


def skew_table(e, side, lanes):
    lane = lax.broadcasted_iota(jnp.int32, (side, lanes), 1) % side
    w = jnp.zeros((side, lanes), F32)
    for xk in range(side):
        w = jnp.where(lane == xk, e[15 - xk : 15 - xk + side], w)
    return w


def bias_kernel(layout_ref, te_ref, out_ref):
    te = te_ref[0, 0]
    col = lax.broadcasted_iota(jnp.int32, (32, 512), 1)
    row = lax.broadcasted_iota(jnp.int32, (32, 512), 0)
    wide = (row == 30 - col // GRID).astype(F32)
    narrow = ((row == 22 - col // SUB) & (col < 15 * SUB)).astype(F32)[:, :256]
    e_wide = contract(te, wide, 1, 0, HIGHEST)
    e_narrow = contract(te, narrow, 1, 0, HIGHEST)
    w_wide = skew_table(e_wide, GRID, 512)
    w_narrow = skew_table(e_narrow, SUB, 256)
    key_slot = lax.broadcasted_iota(jnp.int32, (SUB, ROW_LEN), 1) // (SUB * SUB)
    for r in range(2):

        @pl.when(layout_ref[r] != 1)
        def _():
            for y in range(GRID):
                out_ref[0, r, 0, pl.ds(GRID * y, GRID), :] = pltpu.roll(
                    w_wide, (512 - (15 - y) * GRID) % 512, 1
                )[:, :ROW_LEN]

        @pl.when(layout_ref[r] == 1)
        def _():
            for slot in range(SLOTS):
                for y in range(SUB):
                    moved = pltpu.roll(w_narrow, (256 + 64 * slot - (7 - y) * SUB) % 256, 1)
                    out_ref[0, r, 0, pl.ds(64 * slot + SUB * y, SUB), :] = jnp.where(
                        key_slot == slot, moved, MASKED_LOGIT
                    )


def bias_maps(layout, rel_table):
    te = jnp.pad(jnp.swapaxes(rel_table, 2, 3), ((0, 0), (0, 0), (0, 1), (0, 1)))
    return pl.pallas_call(
        bias_kernel,
        out_shape=jax.ShapeDtypeStruct((LAYERS, 2, HEADS, ROW_LEN, ROW_LEN), F32),
        grid_spec=pltpu.PrefetchScalarGridSpec(
            num_scalar_prefetch=1,
            grid=(LAYERS, HEADS),
            in_specs=[pl.BlockSpec((1, 1, 32, 32), lambda l, h, _: (l, h, 0, 0))],
            out_specs=pl.BlockSpec(
                (1, 2, 1, ROW_LEN, ROW_LEN), lambda l, h, _: (l, 0, h, 0, 0)
            ),
        ),
        compiler_params=pltpu.CompilerParams(vmem_limit_bytes=VMEM_LIMIT),
        name="bias_maps",
    )(layout, te)


def fold_kernel(sums_ref, out_ref):
    first = lax.axis_index("hid")
    col = lax.broadcasted_iota(jnp.int32, (512, 32), 0)
    row = lax.broadcasted_iota(jnp.int32, (512, 32), 1)
    wide = (row == 30 - col // GRID).astype(F32)
    narrow = ((row == 22 - col // SUB) & (col < 15 * SUB)).astype(F32)[:256]

    def unskew(w, side, lanes):
        lane = lax.broadcasted_iota(jnp.int32, (side, lanes), 1) % side
        e = jnp.zeros((32, lanes), F32)
        for xk in range(side):
            part = jnp.where(lane == xk, w, 0.0)
            low = 15 - xk
            pieces = []
            if low:
                pieces.append(jnp.zeros((low, lanes), F32))
            pieces.append(part)
            if 32 - low - side:
                pieces.append(jnp.zeros((32 - low - side, lanes), F32))
            e = e + jnp.concatenate(pieces, axis=0)
        return e

    single = sums_ref[0, 0]
    quad = sums_ref[1, 0]
    w_wide = jnp.zeros((GRID, 512), F32)
    for i in range(2):
        y = 2 * first + i
        block = jnp.concatenate(
            [single[GRID * i : GRID * (i + 1)], jnp.zeros((GRID, 256), F32)], axis=1
        )
        w_wide = w_wide + pltpu.roll(block, (15 - y) * GRID, 1)
    slot = first // 2
    lane_slot = lax.broadcasted_iota(jnp.int32, (SUB, ROW_LEN), 1) // (SUB * SUB)
    w_narrow = jnp.zeros((SUB, 256), F32)
    for i in range(4):
        y = lax.rem(first, 2) * 4 + i
        block = jnp.where(lane_slot == slot, quad[SUB * i : SUB * (i + 1)], 0.0)
        w_narrow = w_narrow + pltpu.roll(block, lax.rem((7 - y) * SUB + 256 - 64 * slot, 256), 1)
    e_wide = unskew(w_wide, GRID, 512)
    e_narrow = unskew(w_narrow, SUB, 256)
    out_ref[0] = contract(e_wide, wide, 1, 0, HIGHEST) + contract(e_narrow, narrow, 1, 0, HIGHEST)


def table_grads(sums):
    both = pl.pallas_call(
        fold_kernel,
        out_shape=jax.ShapeDtypeStruct((HEADS, 32, 32), F32),
        grid=(HEADS,),
        in_specs=[pl.BlockSpec((2, 1, OWN, ROW_LEN), lambda h: (0, h, 0, 0))],
        out_specs=pl.BlockSpec((1, 32, 32), lambda h: (h, 0, 0)),
        compiler_params=pltpu.CompilerParams(vmem_limit_bytes=VMEM_LIMIT),
        name="table_fold",
    )(sums)
    return jnp.swapaxes(both[:, :REL, :REL], 1, 2)


def head_window(h):
    tile = jnp.minimum((h * 9) // 16, 7)
    start = tile * 128
    offset = h * HEAD_DIM - start
    lane = lax.broadcasted_iota(jnp.int32, (1, 256), 1)
    mask = ((lane >= offset) & (lane < offset + HEAD_DIM)).astype(F32).astype(BF16)
    return start, mask


def layer_norm_rows(x, gain, shift):
    centre = x - jnp.mean(x, -1, keepdims=True)
    inverse = lax.rsqrt(jnp.mean(centre * centre, -1, keepdims=True) + NORM_EPSILON)
    unit = centre * inverse
    return (unit * gain + shift).astype(BF16), unit.astype(BF16), inverse


CHUNK = 32


def forward_kernel(
    has_sum,
    *refs,
):
    if has_sum:
        x_ref, sum_ref, bdown_ref, *refs = refs
    else:
        x_ref, *refs = refs
    (
        tp_ref,
        gain_ref,
        shift_ref,
        bup_ref,
        wqkv_ref,
        wout_ref,
        wup_ref,
        wdown_ref,
        bias_hbm,
        h_ref,
        part_ref,
        first_ref,
        unit1_ref,
        inv1_ref,
        qkv_ref,
        att_ref,
        second_ref,
        unit2_ref,
        inv2_ref,
        u_ref,
        g_ref,
        p_hbm,
        bias_buf,
        p_buf,
        o_acc,
        bias_sem,
        p_sem,
    ) = refs

    def bias_copy(i):
        return pltpu.make_async_copy(
            bias_hbm.at[i // HEADS, lax.rem(i, HEADS)],
            bias_buf.at[lax.rem(i, 4)],
            bias_sem.at[lax.rem(i, 4)],
        )

    def p_copy(i):
        return pltpu.make_async_copy(
            p_buf.at[lax.rem(i, 2)],
            p_hbm.at[i // HEADS, lax.rem(i, HEADS)],
            p_sem.at[lax.rem(i, 2)],
        )

    for i in range(3):
        bias_copy(i).start()

    def row(r, _):
        base = r * ROW_LEN
        rows = span(base, ROW_LEN, ROW_LEN)

        def norm_one(i, _):
            rr = span(base + i * CHUNK, CHUNK, CHUNK)
            x = x_ref[rr].astype(F32)
            if has_sum:
                x = x + (sum_ref[rr].astype(F32) + bdown_ref[...])
            h_ref[rr] = x
            low, unit, inverse = layer_norm_rows(x, gain_ref[0:1], shift_ref[0:1])
            first_ref[rr] = low
            unit1_ref[rr] = unit
            inv1_ref[rr] = inverse
            return 0

        lax.fori_loop(0, ROW_LEN // CHUNK, norm_one, 0)

        def project(n, _):
            cols = span(n * D, D, 128)
            wide = dot(first_ref[rows], wqkv_ref[:, cols])
            for s in range(SLOTS):
                qkv_ref[span(base + 64 * s, 64, 64), cols] = (
                    wide[64 * s : 64 * (s + 1)] + tp_ref[r, s : s + 1, cols]
                ).astype(BF16)
            return 0

        lax.fori_loop(0, 3, project, 0)
        o_acc[...] = jnp.zeros_like(o_acc)

        def head(h, _):
            i = r * HEADS + h
            start, mask = head_window(h)
            q = qkv_ref[rows, span(start, 256, 128)] * mask
            k = qkv_ref[rows, span(D + start, 256, 128)]
            v = qkv_ref[rows, span(2 * D + start, 256, 128)] * mask

            @pl.when(i + 3 < 2 * HEADS)
            def _():
                bias_copy(i + 3).start()

            bias_copy(i).wait()
            logits = dot_nt(q, k) * SCALE + bias_buf[lax.rem(i, 4)]
            expo = jnp.exp(logits - jnp.max(logits, -1, keepdims=True))
            p = (expo * (1.0 / jnp.sum(expo, -1, keepdims=True))).astype(BF16)

            @pl.when(i >= 2)
            def _():
                p_copy(i - 2).wait()

            p_buf[lax.rem(i, 2)] = p
            p_copy(i).start()
            o_acc[:, span(start, 256, 128)] += dot(p, v)
            return 0

        lax.fori_loop(0, HEADS, head, 0)
        att_ref[rows] = o_acc[...].astype(BF16)
        h_ref[rows] = h_ref[rows] + dot(att_ref[rows], wout_ref[...])

        def norm_two(i, _):
            rr = span(base + i * CHUNK, CHUNK, CHUNK)
            low, unit, inverse = layer_norm_rows(h_ref[rr], gain_ref[1:2], shift_ref[1:2])
            second_ref[rr] = low
            unit2_ref[rr] = unit
            inv2_ref[rr] = inverse
            return 0

        lax.fori_loop(0, ROW_LEN // CHUNK, norm_two, 0)
        u_ref[rows] = dot(second_ref[rows], wup_ref[...]) + bup_ref[...]
        g_ref[rows] = gelu(u_ref[rows]).astype(BF16)
        part_ref[rows] = dot(g_ref[rows], wdown_ref[...]).astype(BF16)
        return 0

    lax.fori_loop(0, 2, row, 0)
    p_copy(2 * HEADS - 2).wait()
    p_copy(2 * HEADS - 1).wait()


IN_VMEM = pl.BlockSpec(memory_space=pltpu.VMEM)
IN_ANY = pl.BlockSpec(memory_space=pl.ANY)


def forward_layer(x, added, tp, gain, shift, b_up, w_qkv, w_out, w_up, w_down, bias):
    args = [x] if added is None else [x, *added]
    n_vmem = len(args) + 8
    s = jax.ShapeDtypeStruct
    shapes = [
        s((TOKENS, D), F32),
        s((TOKENS, D), BF16),
        s((TOKENS, D), BF16),
        s((TOKENS, D), BF16),
        s((TOKENS, 1), F32),
        s((TOKENS, 3 * D), BF16),
        s((TOKENS, D), BF16),
        s((TOKENS, D), BF16),
        s((TOKENS, D), BF16),
        s((TOKENS, 1), F32),
        s((TOKENS, UNITS), F32),
        s((TOKENS, UNITS), BF16),
        s((2, HEADS, ROW_LEN, ROW_LEN), BF16),
    ]
    return pl.pallas_call(
        functools.partial(forward_kernel, added is not None),
        out_shape=shapes,
        in_specs=[IN_VMEM] * n_vmem + [IN_ANY],
        out_specs=[IN_VMEM] * 12 + [IN_ANY],
        scratch_shapes=[
            pltpu.VMEM((4, ROW_LEN, ROW_LEN), F32),
            pltpu.VMEM((2, ROW_LEN, ROW_LEN), BF16),
            pltpu.VMEM((ROW_LEN, D), F32),
            pltpu.SemaphoreType.DMA((4,)),
            pltpu.SemaphoreType.DMA((2,)),
        ],
        compiler_params=pltpu.CompilerParams(vmem_limit_bytes=VMEM_LIMIT),
        name="forward_layer",
    )(*args, tp, gain, shift, b_up, w_qkv, w_out, w_up, w_down, bias)


def ff_backward_kernel(
    dy_ref,
    u_ref,
    g_ref,
    second_ref,
    wup_ref,
    wdown_ref,
    part_ref,
    grads_ref,
    bup_ref,
    bdown_ref,
    dyl_ref,
    du_ref,
):
    first = lax.axis_index("hid") * OWN

    def row(r, total):
        rows = span(r * ROW_LEN, ROW_LEN, ROW_LEN)
        dyl_ref[rows] = dy_ref[rows].astype(BF16)
        gh = dot_nt(dyl_ref[rows], wdown_ref[...])
        du = (gh * gelu_slope(u_ref[rows])).astype(BF16)
        du_ref[rows] = du
        part_ref[rows] = dot_nt(du, wup_ref[...]).astype(BF16)
        return total + jnp.sum(du.astype(F32), 0, keepdims=True)

    bup_ref[...] = lax.fori_loop(0, 2, row, jnp.zeros((1, UNITS), F32))
    own = jnp.zeros((1, D), F32)
    for r in range(2):
        own = own + jnp.sum(
            dyl_ref[span(r * ROW_LEN + first, OWN, OWN)].astype(F32), 0, keepdims=True
        )
    bdown_ref[...] = own
    up = dot_tn(second_ref[...], du_ref[...]).astype(BF16)
    for c in range(DP):
        grads_ref[c, 0:72, 0:UNITS] = up[72 * c : 72 * (c + 1)]
    down = dot_tn(dyl_ref[...], g_ref[...]).astype(BF16)
    for c in range(DP):
        grads_ref[c, 0:72, UNITS : 2 * UNITS] = down[72 * c : 72 * (c + 1)]
        grads_ref[c, 64:80] = jnp.where(
            lax.broadcasted_iota(jnp.int32, (16, D), 0) < 8, grads_ref[c, 64:80].astype(F32), 0.0
        ).astype(BF16)


def ff_backward(dy, u, g, second, w_up, w_down):
    s = jax.ShapeDtypeStruct
    return pl.pallas_call(
        ff_backward_kernel,
        out_shape=[
            s((TOKENS, D), BF16),
            s((DP, 80, D), BF16),
            s((1, UNITS), F32),
            s((1, D), F32),
        ],
        in_specs=[IN_VMEM] * 6,
        out_specs=[IN_VMEM] * 4,
        scratch_shapes=[pltpu.VMEM((TOKENS, D), BF16), pltpu.VMEM((TOKENS, UNITS), BF16)],
        compiler_params=pltpu.CompilerParams(vmem_limit_bytes=VMEM_LIMIT),
        name="ff_backward",
    )(dy, u, g, second, w_up, w_down)


def kept_matrix():
    feature = lax.broadcasted_iota(jnp.int32, (D, 256), 0)
    column = lax.broadcasted_iota(jnp.int32, (D, 256), 1)
    inner = column % 16
    chosen = (feature == (column // 16) * 72 + lax.axis_index("hid") * KEPT + inner) & (
        inner < KEPT
    )
    return chosen.astype(F32).astype(BF16)


def norm_slope(dn, unit, inverse, gain):
    scaled = dn * gain
    return inverse * (
        scaled
        - jnp.mean(scaled, -1, keepdims=True)
        - unit * jnp.mean(scaled * unit, -1, keepdims=True)
    )


def attn_backward_kernel(
    dy_ref,
    dn2_ref,
    unit2_ref,
    inv2_ref,
    gain_ref,
    unit1_ref,
    inv1_ref,
    qkv_ref,
    att_ref,
    first_ref,
    time_ref,
    pick_ref,
    kind_ref,
    wout_ref,
    wqkv_ref,
    p_hbm,
    dx_ref,
    gq_ref,
    gt_ref,
    go_ref,
    dproj_ref,
    sums_ref,
    gains_ref,
    shifts_ref,
    dh_low,
    do_ref,
    dqkv_ref,
    acc_ref,
    dn1_ref,
    ds_ref,
    p_buf,
    p_sem,
):
    own_first = lax.axis_index("hid") * OWN

    def p_copy(i):
        return pltpu.make_async_copy(
            p_hbm.at[i // HEADS, lax.rem(i, HEADS)],
            p_buf.at[lax.rem(i, 4)],
            p_sem.at[lax.rem(i, 4)],
        )

    for i in range(3):
        p_copy(i).start()
    sums_ref[...] = jnp.zeros_like(sums_ref)
    gains_ref[...] = jnp.zeros_like(gains_ref)
    shifts_ref[...] = jnp.zeros_like(shifts_ref)

    def row(r, _):
        base = r * ROW_LEN
        rows = span(base, ROW_LEN, ROW_LEN)

        def second_norm(i, _):
            rr = span(base + i * CHUNK, CHUNK, CHUNK)
            dn = dn2_ref[rr].astype(F32)
            dh = dy_ref[rr] + norm_slope(
                dn, unit2_ref[rr].astype(F32), inv2_ref[rr], gain_ref[1:2]
            )
            dx_ref[rr] = dh
            dh_low[rr] = dh.astype(BF16)
            return 0

        lax.fori_loop(0, ROW_LEN // CHUNK, second_norm, 0)
        mine = span(base + own_first, OWN, OWN)
        dn = dn2_ref[mine].astype(F32)
        gains_ref[1:2] += jnp.sum(dn * unit2_ref[mine].astype(F32), 0, keepdims=True)
        shifts_ref[1:2] += jnp.sum(dn, 0, keepdims=True)
        do_ref[...] = dot_nt(dh_low[rows], wout_ref[...]).astype(BF16)
        acc_ref[...] = jnp.zeros_like(acc_ref)

        def head(h, _):
            i = r * HEADS + h
            start, mask = head_window(h)
            cols = span(start, 256, 128)
            cols_k = span(D + start, 256, 128)
            cols_v = span(2 * D + start, 256, 128)
            q = qkv_ref[rows, cols] * mask
            k = qkv_ref[rows, cols_k] * mask
            v = qkv_ref[rows, cols_v] * mask
            do = do_ref[:, cols] * mask

            @pl.when(i + 3 < 2 * HEADS)
            def _():
                p_copy(i + 3).start()

            dp = dot_nt(do, v)
            p_copy(i).wait()
            p_low = p_buf[lax.rem(i, 4)]
            p = p_low.astype(F32)
            t = p * dp
            ds = t - p * jnp.sum(t, -1, keepdims=True)
            ds_ref[...] = ds
            ds_low = ds.astype(BF16)
            acc_ref[:, cols] += dot(ds_low, k) * SCALE
            acc_ref[:, cols_k] += dot_tn(ds_low, q) * SCALE
            acc_ref[:, cols_v] += dot_tn(p_low, do)
            mine = ds_ref[span(own_first, OWN, OWN)]
            sums_ref[0, h] += mine * kind_ref[r, 0:1]
            sums_ref[1, h] += mine * kind_ref[r, 1:2]
            return 0

        lax.fori_loop(0, HEADS, head, 0)
        dqkv_ref[rows] = acc_ref[...].astype(BF16)

        def back(n, _):
            cols = span(n * D, D, 128)
            got = dot_nt(dqkv_ref[rows, cols], wqkv_ref[:, cols])

            @pl.when(n == 0)
            def _():
                dn1_ref[...] = got

            @pl.when(n > 0)
            def _():
                dn1_ref[...] += got

            return 0

        lax.fori_loop(0, 3, back, 0)

        def first_norm(i, _):
            rr = span(base + i * CHUNK, CHUNK, CHUNK)
            dn = dn1_ref[span(i * CHUNK, CHUNK, CHUNK)]
            dx_ref[rr] = dx_ref[rr] + norm_slope(
                dn, unit1_ref[rr].astype(F32), inv1_ref[rr], gain_ref[0:1]
            )
            return 0

        lax.fori_loop(0, ROW_LEN // CHUNK, first_norm, 0)
        dn = dn1_ref[span(own_first, OWN, OWN)]
        gains_ref[0:1] += jnp.sum(dn * unit1_ref[mine].astype(F32), 0, keepdims=True)
        shifts_ref[0:1] += jnp.sum(dn, 0, keepdims=True)
        return 0

    lax.fori_loop(0, 2, row, 0)
    kept = kept_matrix()
    first_kept = dot(first_ref[...], kept).astype(BF16)
    att_kept = dot(att_ref[...], kept).astype(BF16)
    time_kept = dot(time_ref[...], kept).astype(BF16)

    def weights(n, _):
        cols = span(n * D, D, 128)
        dproj = dot(pick_ref[...], dqkv_ref[:, cols])
        dproj_ref[:, cols] = dproj
        gt = dot_tn(time_kept, dproj.astype(BF16)).astype(BF16)
        gq = dot_tn(first_kept, dqkv_ref[:, cols]).astype(BF16)
        for c in range(DP):
            gq_ref[c, :, cols] = gq[16 * c : 16 * (c + 1)]
            gt_ref[c, :, cols] = gt[16 * c : 16 * (c + 1)]
        return 0

    lax.fori_loop(0, 3, weights, 0)
    go = dot_tn(att_kept, dh_low[...]).astype(BF16)
    for c in range(DP):
        go_ref[c] = go[16 * c : 16 * (c + 1)]


def attn_backward(dy, dn2, saved, gain, time_tokens, pick, kind, w_out, w_qkv):
    first, unit1, inv1, qkv, att, unit2, inv2, p = saved
    s = jax.ShapeDtypeStruct
    return pl.pallas_call(
        attn_backward_kernel,
        out_shape=[
            s((TOKENS, D), F32),
            s((DP, 16, 3 * D), BF16),
            s((DP, 16, 3 * D), BF16),
            s((DP, 16, D), BF16),
            s((8, 3 * D), F32),
            s((2, HEADS, OWN, ROW_LEN), F32),
            s((2, D), F32),
            s((2, D), F32),
        ],
        in_specs=[IN_VMEM] * 15 + [IN_ANY],
        out_specs=[IN_VMEM] * 8,
        scratch_shapes=[
            pltpu.VMEM((TOKENS, D), BF16),
            pltpu.VMEM((ROW_LEN, D), BF16),
            pltpu.VMEM((TOKENS, 3 * D), BF16),
            pltpu.VMEM((ROW_LEN, 3 * D), F32),
            pltpu.VMEM((ROW_LEN, D), F32),
            pltpu.VMEM((ROW_LEN, ROW_LEN), F32),
            pltpu.VMEM((4, ROW_LEN, ROW_LEN), BF16),
            pltpu.SemaphoreType.DMA((4,)),
        ],
        compiler_params=pltpu.CompilerParams(vmem_limit_bytes=VMEM_LIMIT),
        name="attn_backward",
    )(
        dy,
        dn2,
        unit2,
        inv2,
        gain,
        unit1,
        inv1,
        qkv,
        att,
        first,
        time_tokens,
        pick,
        kind,
        w_out,
        w_qkv,
        p,
    )


HID_ORDER = (2, 6, 1, 4, 3, 7, 5)


def hid_peer(me, k):
    return lax.rem(me // 2 + k // 2, 4) * 2 + lax.rem(me + k, 2)


def hid_sum_kernel(x_ref, o_ref, recv, send1, recv1, send2, recv2):
    me = lax.axis_index("hid")
    n = TOKENS // HID
    barrier = pltpu.get_barrier_semaphore()
    for k in HID_ORDER:
        pl.semaphore_signal(
            barrier, inc=1, device_id={"hid": hid_peer(me, k)}, device_id_type=MESH
        )
    pl.semaphore_wait(barrier, HID - 1)
    first = []
    for k in HID_ORDER:
        peer = hid_peer(me, k)
        copy = pltpu.make_async_remote_copy(
            src_ref=x_ref.at[span(peer * n, n, n)],
            dst_ref=recv.at[k - 1],
            send_sem=send1.at[k - 1],
            recv_sem=recv1.at[k - 1],
            device_id={"hid": peer},
            device_id_type=MESH,
        )
        copy.start()
        first.append(copy)
    mine = span(me * n, n, n)
    for copy in first:
        copy.wait_recv()
    total = x_ref[mine].astype(F32)
    for k in range(HID - 1):
        total = total + recv[k].astype(F32)
    o_ref[mine] = total.astype(BF16)
    second = []
    for k in HID_ORDER:
        peer = hid_peer(me, k)
        copy = pltpu.make_async_remote_copy(
            src_ref=o_ref.at[mine],
            dst_ref=o_ref.at[mine],
            send_sem=send2.at[k - 1],
            recv_sem=recv2.at[k - 1],
            device_id={"hid": peer},
            device_id_type=MESH,
        )
        copy.start()
        second.append(copy)
    for k in HID_ORDER:
        source = lax.rem(me // 2 + 4 - k // 2, 4) * 2 + lax.rem(me + k, 2)
        pltpu.make_async_remote_copy(
            src_ref=o_ref.at[mine],
            dst_ref=o_ref.at[span(source * n, n, n)],
            send_sem=send2.at[k - 1],
            recv_sem=recv2.at[k - 1],
            device_id={"hid": source},
            device_id_type=MESH,
        ).wait_recv()
    for copy in first + second:
        copy.wait_send()


def hid_sum(x):
    return pl.pallas_call(
        hid_sum_kernel,
        out_shape=jax.ShapeDtypeStruct((TOKENS, D), BF16),
        in_specs=[IN_VMEM],
        out_specs=IN_VMEM,
        scratch_shapes=[pltpu.VMEM((HID - 1, TOKENS // HID, D), BF16)]
        + [pltpu.SemaphoreType.DMA((HID - 1,))] * 4,
        compiler_params=pltpu.CompilerParams(
            collective_id=1, has_side_effects=True, vmem_limit_bytes=VMEM_LIMIT
        ),
        name="hid_sum",
    )(x)


def dp_place(me):
    return me // 4, lax.rem(me // 2, 2), lax.rem(me, 2)


def dp_scatter_kernel(n, *refs):
    xs, outs, pair, mixed, recv = (refs[i * n : (i + 1) * n] for i in range(5))
    pair_send, pair_recv, send, got = refs[5 * n :]
    me = lax.axis_index("dp")
    y, z, core = dp_place(me)
    chip = me // 2
    partner = chip * 2 + (1 - core)

    def other(k):
        return lax.rem(y + k // 2, 4) * 2 + lax.rem(z + k, 2)

    barrier = pltpu.get_barrier_semaphore()
    pl.semaphore_signal(barrier, inc=1, device_id={"dp": partner}, device_id_type=MESH)
    for k in range(1, 8):
        pl.semaphore_signal(
            barrier, inc=1, device_id={"dp": other(k) * 2 + core}, device_id_type=MESH
        )
    pl.semaphore_wait(barrier, 8)
    copies = []
    for i in range(n):
        copy = pltpu.make_async_remote_copy(
            src_ref=xs[i].at[:, 1 - core],
            dst_ref=pair[i],
            send_sem=pair_send.at[i],
            recv_sem=pair_recv.at[i],
            device_id={"dp": partner},
            device_id_type=MESH,
        )
        copy.start()
        copies.append(copy)
    arrivals = []
    for i in range(n):
        copies[i].wait_recv()
        for k in HID_ORDER + (0,):
            c = other(k)
            block = xs[i][c, core].astype(F32) + pair[i][c].astype(F32)
            if k == 0:
                outs[i][...] = block
                continue
            mixed[i][c] = block.astype(BF16)
            copy = pltpu.make_async_remote_copy(
                src_ref=mixed[i].at[c],
                dst_ref=recv[i].at[k - 1],
                send_sem=send.at[i, k - 1],
                recv_sem=got.at[i, k - 1],
                device_id={"dp": c * 2 + core},
                device_id_type=MESH,
            )
            copy.start()
            copies.append(copy)
            arrivals.append((i, k, copy))
    for i, k, copy in arrivals:
        copy.wait_recv()
        outs[i][...] += recv[i][k - 1].astype(F32)
    for copy in copies:
        copy.wait_send()


def dp_scatter(collective, *xs):
    n = len(xs)
    xs = [x.reshape(8, 2, *x.shape[1:]) for x in xs]
    blocks = [x.shape[2:] for x in xs]
    return pl.pallas_call(
        functools.partial(dp_scatter_kernel, n),
        out_shape=[jax.ShapeDtypeStruct(b, F32) for b in blocks],
        in_specs=[IN_VMEM] * n,
        out_specs=[IN_VMEM] * n,
        scratch_shapes=[pltpu.VMEM((8, *b), BF16) for b in blocks]
        + [pltpu.VMEM((8, *b), BF16) for b in blocks]
        + [pltpu.VMEM((7, *b), BF16) for b in blocks]
        + [
            pltpu.SemaphoreType.DMA((n,)),
            pltpu.SemaphoreType.DMA((n,)),
            pltpu.SemaphoreType.DMA((n, 7)),
            pltpu.SemaphoreType.DMA((n, 7)),
        ],
        compiler_params=pltpu.CompilerParams(
            collective_id=collective, has_side_effects=True, vmem_limit_bytes=VMEM_LIMIT
        ),
        name="dp_scatter",
    )(*xs)


def shards(
    block_in,
    time_tokens,
    layout,
    norm_gain,
    norm_bias,
    w_qkv,
    w_time,
    rel_table,
    w_out,
    w_up,
    b_up,
    w_down,
    b_down,
    cotangent,
):
    hid_index = lax.axis_index("hid")
    is_four = layout == 1
    bias = bias_maps(layout, rel_table)
    slot = jnp.arange(SLOTS)
    quarter_slot = jnp.where(is_four[:, None], slot[None, :], 0)
    token_slot = jnp.repeat(quarter_slot, 64, axis=1)
    pick = (
        (jnp.arange(2)[:, None, None, None] == jnp.arange(2)[None, None, :, None])
        & (slot[None, :, None, None] == token_slot[None, None])
    ).reshape(8, TOKENS)
    pick = pick.astype(BF16)
    kind = jnp.broadcast_to(
        jnp.stack([~is_four, is_four], 1).astype(F32)[:, :, None], (2, 2, ROW_LEN)
    )
    time_flat = time_tokens.reshape(8, D)

    def time_part(layer):
        proj = jnp.dot(time_flat, w_time[layer], preferred_element_type=F32).reshape(2, 4, 3 * D)
        return jnp.where(is_four[:, None, None], proj, proj[:, :1])

    x = block_in.reshape(TOKENS, D)
    added = None
    stored = []
    for layer in range(LAYERS):
        h, part, first, unit1, inv1, qkv, att, second, unit2, inv2, u, g, p = forward_layer(
            x,
            added,
            time_part(layer),
            norm_gain[layer],
            norm_bias[layer],
            b_up[layer][None],
            w_qkv[layer],
            w_out[layer],
            w_up[layer],
            w_down[layer],
            bias[layer],
        )
        total = hid_sum(part)
        x, added = h, (total, b_down[layer][None])
        stored.append((second, u, g, (first, unit1, inv1, qkv, att, unit2, inv2, p)))
    block_out = x + (added[0].astype(F32) + added[1])

    dy = cotangent.reshape(TOKENS, D).astype(F32)
    grad_time = jnp.zeros((8, D), F32)
    gains, shifts, tables, bups, bdowns = [], [], [], [], []
    qkv_grads, time_grads, out_grads, up_grads, down_grads = [], [], [], [], []
    for layer in reversed(range(LAYERS)):
        second, u, g, saved = stored[layer]
        part, ff_grads, bup, bdown = ff_backward(dy, u, g, second, w_up[layer], w_down[layer])
        dn2 = hid_sum(part)
        dx, gq, gt, go, dproj, sums, gain, shift = attn_backward(
            dy,
            dn2,
            saved,
            norm_gain[layer],
            time_flat,
            pick,
            kind,
            w_out[layer],
            w_qkv[layer],
        )
        dy = dx
        grad_time = grad_time + contract(dproj.astype(BF16), w_time[layer], 1, 1)
        ff_own, q_own, t_own, o_own = dp_scatter(2, ff_grads, gq, gt, go)
        up_grads.insert(0, ff_own[:72, :UNITS])
        down_grads.insert(0, ff_own[:72, UNITS:].T)
        qkv_grads.insert(0, q_own[:KEPT])
        time_grads.insert(0, t_own[:KEPT])
        out_grads.insert(0, o_own[:KEPT])
        gains.insert(0, gain)
        shifts.insert(0, shift)
        tables.insert(0, table_grads(sums))
        bups.insert(
            0, lax.dynamic_update_slice(jnp.zeros((FF,), F32), bup[0], (hid_index * UNITS,))
        )
        bdowns.insert(0, bdown[0])
    small = lax.psum(
        tuple(jnp.stack(v) for v in (gains, shifts, tables, bups, bdowns)), ("dp", "hid")
    )
    return (
        block_out.reshape(2, ROW_LEN, D),
        dy.reshape(2, ROW_LEN, D),
        grad_time.reshape(2, SLOTS, D),
        small[0],
        small[1],
        jnp.stack(qkv_grads),
        jnp.stack(time_grads),
        small[2],
        jnp.stack(out_grads),
        jnp.stack(up_grads),
        small[3],
        jnp.stack(down_grads),
        small[4],
    )


def solution(mesh):
    in_specs = (
        P("dp", None, None),
        P("dp", None, None),
        P("dp"),
        P(),
        P(),
        P(),
        P(),
        P(),
        P(),
        P(None, None, "hid"),
        P(None, "hid"),
        P(None, "hid", None),
        P(),
        P("dp", None, None),
    )
    out_specs = (
        P("dp", None, None),
        P("dp", None, None),
        P("dp", None, None),
        P(),
        P(),
        P(None, ("dp", "hid"), None),
        P(None, ("dp", "hid"), None),
        P(),
        P(None, ("dp", "hid"), None),
        P(None, "dp", "hid"),
        P(),
        P(None, "hid", "dp"),
        P(),
    )
    return jax.shard_map(shards, mesh=mesh, in_specs=in_specs, out_specs=out_specs, check_vma=False)
```

```python
import functools

import jax
import jax.numpy as jnp
from jax import lax
from jax.experimental import pallas as pl
from jax.experimental.pallas import tpu as pltpu
from jax.sharding import PartitionSpec as P

D = 1152
HEADS = 16
HEAD_DIM = 72
FF = 4608
LAYERS = 2
GRID = 16
SUB = 8
ROW_LEN = 256
SLOTS = 4
REL = 31
DP = 16
HID = 8
UNITS = FF // HID
KEPT = D // (DP * HID)
TOKENS = 512
OWN = ROW_LEN // HID
SCALE = HEAD_DIM ** (-0.5)
MASKED_LOGIT = -1e30
NORM_EPSILON = 1e-06
F32 = jnp.float32
BF16 = jnp.bfloat16
MESH = pl.DeviceIdType.MESH
VMEM_LIMIT = 63 * 1024 * 1024
HIGHEST = lax.Precision.HIGHEST


def contract(a, b, da, db, precision=None):
    return lax.dot_general(
        a, b, (((da,), (db,)), ((), ())), preferred_element_type=F32, precision=precision
    )


def dot(a, b):
    return contract(a, b, 1, 0)


def dot_nt(a, b):
    return contract(a, b, 1, 1)


def dot_tn(a, b):
    return contract(a, b, 0, 0)


def span(start, size, multiple):
    return pl.ds(pl.multiple_of(start, multiple), size)


def gelu_parts(v):
    c = 0.7978845608028654
    square = v * v
    t = jnp.tanh(c * v * (1.0 + 0.044715 * square))
    return t, square


def gelu(v):
    t, _ = gelu_parts(v)
    return 0.5 * v * (1.0 + t)


def gelu_slope(v):
    c = 0.7978845608028654
    t, square = gelu_parts(v)
    return 0.5 * (1.0 + t) + 0.5 * v * (1.0 - t * t) * (c * (1.0 + 3.0 * 0.044715 * square))


def skew_table(e, side, lanes):
    lane = lax.broadcasted_iota(jnp.int32, (side, lanes), 1) % side
    w = jnp.zeros((side, lanes), F32)
    for xk in range(side):
        w = jnp.where(lane == xk, e[15 - xk : 15 - xk + side], w)
    return w


def prepare_kernel(layout_ref, te_ref, time_ref, wtime_ref, bias_ref, tp_ref):
    h = pl.program_id(1)

    @pl.when(h == 0)
    def _():
        tp_ref[...] = jnp.zeros_like(tp_ref)

    @pl.when(lax.rem(h, 2) == 0)
    def _():
        tp_ref[0] += dot(time_ref[0], wtime_ref[0])

    @pl.when(h == HEADS - 1)
    def _():
        for r in range(2):

            @pl.when(layout_ref[r] != 1)
            def _():
                tp_ref[0, 4 * r : 4 * r + 4] = jnp.broadcast_to(
                    tp_ref[0, 4 * r : 4 * r + 1], (SLOTS, 3 * D)
                )

    te = te_ref[0, 0]
    col = lax.broadcasted_iota(jnp.int32, (32, 512), 1)
    row = lax.broadcasted_iota(jnp.int32, (32, 512), 0)

    def single(r):
        wide = (row == 30 - col // GRID).astype(F32)
        w = skew_table(contract(te, wide, 1, 0, HIGHEST), GRID, 512)
        for y in range(GRID):
            bias_ref[0, r, 0, pl.ds(GRID * y, GRID), :] = pltpu.roll(
                w, (512 - (15 - y) * GRID) % 512, 1
            )[:, :ROW_LEN]

    def quad(r):
        narrow = ((row == 22 - col // SUB) & (col < 15 * SUB)).astype(F32)[:, :256]
        w = skew_table(contract(te, narrow, 1, 0, HIGHEST), SUB, 256)
        key_slot = lax.broadcasted_iota(jnp.int32, (SUB, ROW_LEN), 1) // (SUB * SUB)
        for slot in range(SLOTS):
            for y in range(SUB):
                moved = pltpu.roll(w, (256 + 64 * slot - (7 - y) * SUB) % 256, 1)
                bias_ref[0, r, 0, pl.ds(64 * slot + SUB * y, SUB), :] = jnp.where(
                    key_slot == slot, moved, MASKED_LOGIT
                )

    first, second = layout_ref[0], layout_ref[1]
    pl.when(first != 1)(lambda: single(0))
    pl.when(first == 1)(lambda: quad(0))

    @pl.when(first == second)
    def _():
        bias_ref[0, 1] = bias_ref[0, 0]

    pl.when((first != second) & (second != 1))(lambda: single(1))
    pl.when((first != second) & (second == 1))(lambda: quad(1))


def prepare(layout, rel_table, time_flat, w_time):
    te = jnp.pad(jnp.swapaxes(rel_table, 2, 3), ((0, 0), (0, 0), (0, 1), (0, 1)))
    time_parts = jnp.swapaxes(time_flat.reshape(8, 8, 144), 0, 1)
    return pl.pallas_call(
        prepare_kernel,
        out_shape=[
            jax.ShapeDtypeStruct((LAYERS, 2, HEADS, ROW_LEN, ROW_LEN), F32),
            jax.ShapeDtypeStruct((LAYERS, 8, 3 * D), F32),
        ],
        grid_spec=pltpu.PrefetchScalarGridSpec(
            num_scalar_prefetch=1,
            grid=(LAYERS, HEADS),
            in_specs=[
                pl.BlockSpec((1, 1, 32, 32), lambda l, h, _: (l, h, 0, 0)),
                pl.BlockSpec((1, 8, 144), lambda l, h, _: (h // 2, 0, 0)),
                pl.BlockSpec((1, 144, 3 * D), lambda l, h, _: (l, h // 2, 0)),
            ],
            out_specs=[
                pl.BlockSpec((1, 2, 1, ROW_LEN, ROW_LEN), lambda l, h, _: (l, 0, h, 0, 0)),
                pl.BlockSpec((1, 8, 3 * D), lambda l, h, _: (l, 0, 0)),
            ],
        ),
        compiler_params=pltpu.CompilerParams(vmem_limit_bytes=VMEM_LIMIT),
        name="prepare",
    )(layout, te, time_parts, w_time)


IN_VMEM = pl.BlockSpec(memory_space=pltpu.VMEM)
IN_ANY = pl.BlockSpec(memory_space=pl.ANY)
CHUNK = 128
HID_ORDER = (2, 6, 1, 4, 3, 7, 5)
SLICE = ROW_LEN // HID


def head_window(h):
    start = h * HEAD_DIM // 128 * 128
    offset = h * HEAD_DIM - start
    width = 128 if offset + HEAD_DIM <= 128 else 256
    lane = lax.broadcasted_iota(jnp.int32, (1, width), 1)
    mask = ((lane >= offset) & (lane < offset + HEAD_DIM)).astype(F32).astype(BF16)
    return start, width, mask


def hid_peer(me, k):
    return lax.rem(me // 2 + k // 2, 4) * 2 + lax.rem(me + k, 2)


def hid_source(me, k):
    return lax.rem(me // 2 + 4 - k // 2, 4) * 2 + lax.rem(me + k, 2)


def greet_hid(barrier, me):
    for k in HID_ORDER:
        pl.semaphore_signal(
            barrier, inc=1, device_id={"hid": hid_peer(me, k)}, device_id_type=MESH
        )


class HidSums:
    def __init__(self, part, recv, total, sems):
        self.part, self.recv, self.total = part, recv, total
        self.send1, self.recv1, self.send2, self.recv2 = sems
        self.me = lax.axis_index("hid")

    def scatter_copy(self, e, k):
        peer = hid_peer(self.me, k)
        return pltpu.make_async_remote_copy(
            src_ref=self.part.at[e, span(peer * SLICE, SLICE, SLICE)],
            dst_ref=self.recv.at[e, k - 1],
            send_sem=self.send1.at[e, k - 1],
            recv_sem=self.recv1.at[e, k - 1],
            device_id={"hid": peer},
            device_id_type=MESH,
        )

    def gather_copy(self, slot, e, k, outgoing):
        owner = self.me if outgoing else hid_source(self.me, k)
        rows = self.total.at[slot, span(owner * SLICE, SLICE, SLICE)]
        return pltpu.make_async_remote_copy(
            src_ref=rows,
            dst_ref=rows,
            send_sem=self.send2.at[e, k - 1],
            recv_sem=self.recv2.at[e, k - 1],
            device_id={"hid": hid_peer(self.me, k)},
            device_id_type=MESH,
        )

    def scatter(self, e):
        for k in HID_ORDER:
            self.scatter_copy(e, k).start()

    def add_and_gather(self, e):
        mine = span(self.me * SLICE, SLICE, SLICE)
        for k in HID_ORDER:
            self.scatter_copy(e, k).wait_recv()
        total = self.part[e, mine].astype(F32)
        for k in range(HID - 1):
            total = total + self.recv[e, k].astype(F32)
        self.total[e, mine] = total.astype(BF16)
        for k in HID_ORDER:
            self.gather_copy(e, e, k, True).start()

    def wait(self, e):
        for k in HID_ORDER:
            self.gather_copy(e, e, k, False).wait_recv()

    def drain(self, e):
        for k in HID_ORDER:
            self.scatter_copy(e, k).wait_send()
            self.gather_copy(e, e, k, True).wait_send()


def write_ff_grads(ffg, up_of, down_of):
    up = up_of()
    for c in range(DP):
        ffg[c // 2, c % 2, 0:72, 0:UNITS] = up[72 * c : 72 * (c + 1)].astype(BF16)
    down = down_of()
    for c in range(DP):
        ffg[c // 2, c % 2, 0:72, UNITS : 2 * UNITS] = down[72 * c : 72 * (c + 1)].astype(BF16)


def layer_norm_rows(x, gain, shift):
    centre = x - jnp.mean(x, -1, keepdims=True)
    inverse = lax.rsqrt(jnp.mean(centre * centre, -1, keepdims=True) + NORM_EPSILON)
    unit = centre * inverse
    return (unit * gain + shift).astype(BF16), unit.astype(BF16), inverse


def kept_matrix():
    feature = lax.broadcasted_iota(jnp.int32, (D, 256), 0)
    column = lax.broadcasted_iota(jnp.int32, (D, 256), 1)
    low = column < 128
    owner = jnp.where(low, column // 8, column - 128)
    inner = jnp.where(low, column % 8, 8)
    chosen = (feature == owner * 72 + lax.axis_index("hid") * KEPT + inner) & (column < 144)
    return chosen.astype(F32).astype(BF16)


def attend_forward(qkv, r, bias_ref, p_ref, o_acc):
    o_acc[...] = jnp.zeros_like(o_acc)

    def scores(h):
        start, width, mask = head_window(h)
        q = qkv[r, :, start : start + width] * mask
        return dot_nt(q, qkv[r, :, D + start : D + start + width])

    def mix(h, score):
        start, width, mask = head_window(h)
        logits = score * SCALE + bias_ref[h]
        expo = jnp.exp(logits - jnp.max(logits, -1, keepdims=True))
        p = (expo * (1.0 / jnp.sum(expo, -1, keepdims=True))).astype(BF16)
        p_ref[h] = p
        v = qkv[r, :, 2 * D + start : 2 * D + start + width] * mask
        o_acc[:, start : start + width] += dot(p, v)

    ready = {}
    for h in range(HEADS + 1):
        if h < HEADS:
            ready[h] = scores(h)
        if h:
            mix(h - 1, ready.pop(h - 1))


def forward_kernel(
    x_ref,
    cot_ref,
    tp_ref,
    gain_ref,
    shift_ref,
    bup_ref,
    bdown_ref,
    time_ref,
    wqkv_hbm,
    wout_hbm,
    wup_hbm,
    wdown_hbm,
    bias_hbm,
    gbup_ref,
    gbdown_ref,
    timek_ref,
    out_hbm,
    dn2_hbm,
    ffg_hbm,
    qkv_hbm,
    p_hbm,
    unit_hbm,
    inv_hbm,
    kept_hbm,
    second_hbm,
    u_hbm,
    g_hbm,
    wqkv,
    wout,
    wup,
    wdown,
    bias_ref,
    p_ref,
    qkv,
    part,
    recv,
    total,
    h_ref,
    first,
    att,
    o_acc,
    unit,
    inv,
    pick,
    kept,
    second,
    u_ref,
    g_ref,
    du_ref,
    ffg,
    w_sem,
    save_sem,
    send1,
    recv1,
    send2,
    recv2,
):
    me = lax.axis_index("hid")
    sums = HidSums(part, recv, total, (send1, recv1, send2, recv2))

    def load_qkv(l):
        return pltpu.make_async_copy(wqkv_hbm.at[l], wqkv, w_sem.at[0])

    def load_bias(i):
        return pltpu.make_async_copy(
            bias_hbm.at[i // 2, lax.rem(i, 2)], bias_ref, w_sem.at[1]
        )

    def load(hbm, ref, l, n):
        return pltpu.make_async_copy(hbm.at[l], ref.at[l], w_sem.at[2 + 2 * n + l])

    def load_out(l):
        return load(wout_hbm, wout, l, 0)

    def load_up(l):
        return load(wup_hbm, wup, l, 1)

    def load_down(l):
        return load(wdown_hbm, wdown, l, 2)

    load_qkv(0).start()
    load_bias(0).start()
    for l in range(LAYERS):
        load_out(l).start()
        load_up(l).start()
        load_down(l).start()
    barrier = pltpu.get_barrier_semaphore()
    greet_hid(barrier, me)
    pick[...] = kept_matrix()
    timek_ref[...] = dot(time_ref[...], pick[...]).astype(BF16)
    pl.semaphore_wait(barrier, HID - 1)

    def saves(l, r):
        rows = span(r * ROW_LEN, ROW_LEN, ROW_LEN)
        pairs = [
            (qkv.at[r], qkv_hbm.at[l, rows]),
            (unit.at[0, rows], unit_hbm.at[l, 0, rows]),
            (unit.at[1, rows], unit_hbm.at[l, 1, rows]),
            (inv.at[0, rows], inv_hbm.at[l, 0, rows]),
            (inv.at[1, rows], inv_hbm.at[l, 1, rows]),
            (kept.at[0, rows], kept_hbm.at[l, 0, rows]),
            (kept.at[1, rows], kept_hbm.at[l, 1, rows]),
        ]
        return [
            pltpu.make_async_copy(a, b, save_sem.at[r, n]) for n, (a, b) in enumerate(pairs)
        ]

    def feed_saves(r):
        rows = span(r * ROW_LEN, ROW_LEN, ROW_LEN)
        pairs = [(second, second_hbm), (u_ref, u_hbm), (g_ref, g_hbm)]
        return [
            pltpu.make_async_copy(a.at[rows], b.at[rows], save_sem.at[r, 7 + n])
            for n, (a, b) in enumerate(pairs)
        ]

    def save_p(l, r):
        return pltpu.make_async_copy(p_ref, p_hbm.at[l, r], save_sem.at[0, 10])

    def step(i, _):
        l = i // 2
        r = lax.rem(i, 2)
        base = r * ROW_LEN
        rows = span(base, ROW_LEN, ROW_LEN)

        @pl.when(l == 0)
        def _():
            h_ref[rows] = x_ref[rows].astype(F32)

        @pl.when(l == 1)
        def _():
            for copy in saves(0, r) + feed_saves(r):
                copy.wait()
            sums.wait(r)
            h_ref[rows] = h_ref[rows] + (total[r].astype(F32) + bdown_ref[0:1])

        def norm(which):
            def body(c, _):
                rr = span(base + c * CHUNK, CHUNK, CHUNK)
                low, value, inverse = layer_norm_rows(
                    h_ref[rr], gain_ref[l, which : which + 1], shift_ref[l, which : which + 1]
                )
                if which == 0:
                    first[span(c * CHUNK, CHUNK, CHUNK)] = low
                else:
                    second[rr] = low
                unit[which, rr] = value
                inv[which, rr] = jnp.broadcast_to(inverse, (CHUNK, 128))
                return 0

            lax.fori_loop(0, ROW_LEN // CHUNK, body, 0)

        norm(0)

        @pl.when(r == 0)
        def _():
            load_qkv(l).wait()

        def project(n, _):
            cols = span(n * D, D, 128)
            wide = dot(first[...], wqkv[:, cols])
            for s in range(SLOTS):
                qkv[r, 64 * s : 64 * (s + 1), cols] = (
                    wide[64 * s : 64 * (s + 1)] + tp_ref[l, pl.ds(4 * r + s, 1), cols]
                ).astype(BF16)
            return 0

        lax.fori_loop(0, 3, project, 0)

        @pl.when(i == 1)
        def _():
            load_qkv(1).start()

        @pl.when(i == 2)
        def _():
            sums.add_and_gather(1)

        @pl.when(i == 3)
        def _():
            sums.add_and_gather(4)

        kept[0, rows] = dot(first[...], pick[...]).astype(BF16)
        load_bias(i).wait()

        @pl.when(i > 0)
        def _():
            save_p(0, 0).wait()

        attend_forward(qkv, r, bias_ref, p_ref, o_acc)
        save_p(l, r).start()

        @pl.when(i < 3)
        def _():
            load_bias(i + 1).start()

        @pl.when(i == 1)
        def _():
            sums.add_and_gather(0)

        @pl.when(i == 3)
        def _():
            sums.add_and_gather(2)

        att[...] = o_acc[...].astype(BF16)
        kept[1, rows] = dot(att[...], pick[...]).astype(BF16)

        @pl.when(r == 0)
        def _():
            load_out(l).wait()
            load_up(l).wait()
            load_down(l).wait()

        h_ref[rows] = h_ref[rows] + dot(att[...], wout[l])
        norm(1)
        for copy in saves(l, r):
            copy.start()
        u_ref[rows] = dot(second[rows], wup[l]) + bup_ref[l]
        g_ref[rows] = gelu(u_ref[rows]).astype(BF16)

        @pl.when(l == 0)
        def _():
            for copy in feed_saves(r):
                copy.start()

        @pl.when(l == 1)
        def _():
            gh = dot_nt(cot_ref[rows], wdown[1])
            du = (gh * gelu_slope(u_ref[rows])).astype(BF16)
            du_ref[rows] = du
            part[4 + r] = dot_nt(du, wup[1]).astype(BF16)
            sums.scatter(4 + r)

        part[i] = dot(g_ref[rows], wdown[l]).astype(BF16)
        sums.scatter(i)
        return 0

    lax.fori_loop(0, 4, step, 0)
    write_ff_grads(
        ffg,
        lambda: dot_tn(second[...], du_ref[...]),
        lambda: dot_tn(cot_ref[...], g_ref[...]),
    )
    ffg_copy = pltpu.make_async_copy(ffg, ffg_hbm, w_sem.at[8])
    ffg_copy.start()
    sums.add_and_gather(5)
    gbup_ref[...] = jnp.sum(du_ref[...].astype(F32), 0, keepdims=True)
    own = jnp.zeros((1, D), F32)
    for r in range(2):
        own = own + jnp.sum(
            cot_ref[span(r * ROW_LEN + me * OWN, OWN, OWN)].astype(F32), 0, keepdims=True
        )
    gbdown_ref[...] = own
    sums.add_and_gather(3)
    results = []
    for r in range(2):
        rows = pl.ds(r * ROW_LEN, ROW_LEN)
        sums.wait(2 + r)
        h_ref[rows] = h_ref[rows] + (total[2 + r].astype(F32) + bdown_ref[1:2])
        results.append(
            pltpu.make_async_copy(h_ref.at[rows], out_hbm.at[rows], w_sem.at[9 + r])
        )
        results[-1].start()
        sums.wait(4 + r)
        results.append(
            pltpu.make_async_copy(total.at[4 + r], dn2_hbm.at[rows], w_sem.at[11 + r])
        )
        results[-1].start()
        for copy in saves(1, r):
            copy.wait()
    save_p(0, 0).wait()
    ffg_copy.wait()
    for copy in results:
        copy.wait()
    for e in range(6):
        sums.drain(e)


def forward(x, cot, tp, gain, shift, b_up, b_down, time_flat, w_qkv, w_out, w_up, w_down, bias):
    s = jax.ShapeDtypeStruct
    v = pltpu.VMEM
    dma = pltpu.SemaphoreType.DMA
    return pl.pallas_call(
        forward_kernel,
        out_shape=[
            s((1, UNITS), F32),
            s((1, D), F32),
            s((8, 256), BF16),
            s((TOKENS, D), F32),
            s((TOKENS, D), BF16),
            s((8, 2, 80, D), BF16),
            s((LAYERS, TOKENS, 3 * D), BF16),
            s((LAYERS, 2, HEADS, ROW_LEN, ROW_LEN), BF16),
            s((LAYERS, 2, TOKENS, D), BF16),
            s((LAYERS, 2, TOKENS, 128), F32),
            s((LAYERS, 2, TOKENS, 256), BF16),
            s((TOKENS, D), BF16),
            s((TOKENS, UNITS), F32),
            s((TOKENS, UNITS), BF16),
        ],
        in_specs=[IN_VMEM] * 8 + [IN_ANY] * 5,
        out_specs=[IN_VMEM] * 3 + [IN_ANY] * 11,
        scratch_shapes=[
            v((D, 3 * D), BF16),
            v((LAYERS, D, D), BF16),
            v((LAYERS, D, UNITS), BF16),
            v((LAYERS, UNITS, D), BF16),
            v((HEADS, ROW_LEN, ROW_LEN), F32),
            v((HEADS, ROW_LEN, ROW_LEN), BF16),
            v((2, ROW_LEN, 3 * D), BF16),
            v((6, ROW_LEN, D), BF16),
            v((6, HID - 1, SLICE, D), BF16),
            v((6, ROW_LEN, D), BF16),
            v((TOKENS, D), F32),
            v((ROW_LEN, D), BF16),
            v((ROW_LEN, D), BF16),
            v((ROW_LEN, D), F32),
            v((2, TOKENS, D), BF16),
            v((2, TOKENS, 128), F32),
            v((D, 256), BF16),
            v((2, TOKENS, 256), BF16),
            v((TOKENS, D), BF16),
            v((TOKENS, UNITS), F32),
            v((TOKENS, UNITS), BF16),
            v((TOKENS, UNITS), BF16),
            v((8, 2, 80, D), BF16),
            dma((13,)),
            dma((2, 11)),
            dma((6, HID - 1)),
            dma((6, HID - 1)),
            dma((6, HID - 1)),
            dma((6, HID - 1)),
        ],
        compiler_params=pltpu.CompilerParams(
            collective_id=1, has_side_effects=True, vmem_limit_bytes=VMEM_LIMIT
        ),
        name="forward",
    )(x, cot, tp, gain, shift, b_up, b_down, time_flat, w_qkv, w_out, w_up, w_down, bias)


class DpSums:
    def __init__(self, x, pair, recv, sems, free):
        self.x, self.pair, self.recv, self.free = x, pair, recv, free
        self.pair_send, self.pair_recv, self.send, self.got = sems
        me = lax.axis_index("dp")
        self.y, self.z, self.core = me // 4, lax.rem(me // 2, 2), lax.rem(me, 2)
        self.chip = me // 2
        self.partner = self.chip * 2 + (1 - self.core)

    def other(self, k):
        return lax.rem(self.y + k // 2, 4) * 2 + lax.rem(self.z + k, 2)

    def peer(self, k):
        return {"dp": self.other(k) * 2 + self.core}

    def pair_copy(self):
        return pltpu.make_async_remote_copy(
            src_ref=self.x.at[:, 1 - self.core],
            dst_ref=self.pair,
            send_sem=self.pair_send,
            recv_sem=self.pair_recv,
            device_id={"dp": self.partner},
            device_id_type=MESH,
        )

    def chip_copy(self, k):
        return pltpu.make_async_remote_copy(
            src_ref=self.pair.at[self.other(k)],
            dst_ref=self.recv.at[k - 1],
            send_sem=self.send.at[k - 1],
            recv_sem=self.got.at[k - 1],
            device_id=self.peer(k),
            device_id_type=MESH,
        )

    def start(self):
        self.pair_copy().start()

    def exchange(self):
        self.pair_copy().wait_recv()
        for k in HID_ORDER + (0,):
            c = self.other(k)
            both = self.x[c, self.core].astype(F32) + self.pair[c].astype(F32)
            self.pair[c] = both.astype(BF16)
            if k:
                self.chip_copy(k).start()
        self.pair_copy().wait_send()

    def finish(self):
        total = self.pair[self.chip].astype(F32)
        for k in HID_ORDER:
            self.chip_copy(k).wait_recv()
            total = total + self.recv[k - 1].astype(F32)
        for k in HID_ORDER:
            self.chip_copy(k).wait_send()
        return total

    def release(self):
        pl.semaphore_signal(
            self.free, inc=1, device_id={"dp": self.partner}, device_id_type=MESH
        )
        for k in HID_ORDER:
            pl.semaphore_signal(self.free, inc=1, device_id=self.peer(k), device_id_type=MESH)

    def acquire(self):
        pl.semaphore_wait(self.free, 8)


def norm_slope(dn, unit, inverse, gain):
    scaled = dn * gain
    return inverse * (
        scaled
        - jnp.mean(scaled, -1, keepdims=True)
        - unit * jnp.mean(scaled * unit, -1, keepdims=True)
    )


def attend_backward(qkv, r, do_ref, p_ref, acc, ds_ref, fold, kind_ref, own_first):
    acc[...] = jnp.zeros_like(acc)

    def slopes(h):
        start, width, mask = head_window(h)
        v = qkv[r, :, 2 * D + start : 2 * D + start + width] * mask
        return dot_nt(do_ref[:, start : start + width], v)

    def spread(h, dp):
        start, width, mask = head_window(h)
        p_low = p_ref[h]
        p = p_low.astype(F32)
        t = p * dp
        ds = t - p * jnp.sum(t, -1, keepdims=True)
        ds_ref[h % 2] = ds
        low = ds.astype(BF16)
        k = qkv[r, :, D + start : D + start + width] * mask
        q = qkv[r, :, start : start + width] * mask
        do = do_ref[:, start : start + width] * mask
        acc[:, start : start + width] += dot(low, k)
        acc[:, D + start : D + start + width] += dot_tn(low, q)
        acc[:, 2 * D + start : 2 * D + start + width] += dot_tn(p_low, do)
        mine = ds_ref[h % 2, span(own_first, OWN, OWN)]
        fold[0, h] += mine * kind_ref[r, 0:1]
        fold[1, h] += mine * kind_ref[r, 1:2]

    ready = {}
    depth = 2
    for h in range(HEADS + depth):
        if h < HEADS:
            ready[h] = slopes(h)
        if h >= depth:
            spread(h - depth, ready.pop(h - depth))


def two_part_dot(a, b):
    high = a.astype(BF16)
    low = (a - high.astype(F32)).astype(BF16)
    return dot(high, b) + dot(low, b)


def fold_tables(fold, me):
    lane = lax.broadcasted_iota(jnp.int32, (ROW_LEN, 512), 0)
    place = lax.broadcasted_iota(jnp.int32, (ROW_LEN, 512), 1)
    wide = (place == (lane // GRID) * 32 + 15 - lane % GRID).astype(F32).astype(BF16)
    inner = lane % (SUB * SUB)
    narrow = (place == (inner // SUB) * 32 + 15 - inner % SUB).astype(F32).astype(BF16)
    single = two_part_dot(fold[0].reshape(HEADS * OWN, ROW_LEN), wide)
    single = single.reshape(HEADS * 2, GRID, 512)
    quad = two_part_dot(fold[1].reshape(HEADS * OWN, ROW_LEN), narrow)
    quad = quad.reshape(HEADS * 4, SUB, 512)
    out = jnp.zeros((HEADS, 1024), F32)
    single = sum(pltpu.roll(single[:, x], x, 1) for x in range(GRID)).reshape(HEADS, 2, 512)
    quad = sum(pltpu.roll(quad[:, x], x, 1) for x in range(SUB)).reshape(HEADS, 4, 512)
    rest = jnp.zeros((HEADS, 512), F32)
    for i in range(2):
        y = 2 * me + i
        row = jnp.concatenate([single[:, i], rest], axis=1)
        out = out + pltpu.roll(row, (15 - y) * 32, 1)
    for i in range(4):
        y = lax.rem(me, 2) * 4 + i
        row = jnp.concatenate([quad[:, i], rest], axis=1)
        out = out + pltpu.roll(row, (15 - y) * 32, 1)
    return out


def backward_kernel(
    gain_ref,
    pick_ref,
    kind_ref,
    timek_ref,
    gbup_ref,
    gbdown_ref,
    dn2_hbm,
    cot_hbm,
    ffg_hbm,
    qkv_hbm,
    p_hbm,
    unit_hbm,
    inv_hbm,
    kept_hbm,
    second_hbm,
    u_hbm,
    g_hbm,
    wqkv_hbm,
    wout_hbm,
    wup_hbm,
    wdown_hbm,
    wtime_hbm,
    gtime_ref,
    gq_ref,
    gt_ref,
    go_ref,
    ffo_ref,
    small_out,
    dx_hbm,
    wqkv,
    wout,
    wup,
    wdown,
    qkv,
    p_ref,
    unit,
    inv,
    kept,
    second,
    u_ref,
    g_ref,
    total,
    part,
    recv,
    dy,
    dhl,
    dxl,
    do_ref,
    acc,
    dqkv,
    du_ref,
    ds_ref,
    x2,
    pair2,
    recv2,
    x3,
    pair3,
    recv3,
    stage,
    ninth,
    fold,
    dproj,
    small,
    small_recv,
    small_sum,
    small_pair,
    small_chip,
    load_sem,
    row_sem,
    hid_sems,
    dp_sems,
    chip_sems,
    free2,
    free3,
    small_sems,
    small_one,
):
    me = lax.axis_index("hid")
    own_first = me * OWN
    sums = HidSums(part, recv, total, tuple(hid_sems.at[n] for n in range(4)))
    ff_sum = DpSums(
        x2,
        pair2,
        recv2,
        (dp_sems.at[0], dp_sems.at[1], chip_sems.at[0], chip_sems.at[1]),
        free2,
    )
    at_sum = DpSums(
        x3,
        pair3,
        recv3,
        (dp_sems.at[2], dp_sems.at[3], chip_sems.at[2], chip_sems.at[3]),
        free3,
    )

    def load(n, src, dst):
        return pltpu.make_async_copy(src, dst, load_sem.at[n])

    def load_dn2(r):
        return load(r, dn2_hbm.at[pl.ds(r * ROW_LEN, ROW_LEN)], total.at[2 + r])

    def load_cot():
        return load(2, cot_hbm, dxl)

    def load_out(l):
        return load(3, wout_hbm.at[l], wout)

    def load_qkv_weight(l):
        return load(4, wqkv_hbm.at[l], wqkv)

    def load_time_weight(l):
        return load(4, wtime_hbm.at[l], wqkv)

    def load_p(j):
        return load(5, p_hbm.at[1 - j // 2, lax.rem(j, 2)], p_ref)

    def load_ffg():
        return load(6, ffg_hbm, x2)

    def load_kept():
        return load(7, kept_hbm, kept)

    def load_feed():
        return [
            load(8, second_hbm, second),
            load(9, u_hbm, u_ref),
            load(10, g_hbm, g_ref),
            load(11, wup_hbm.at[0], wup),
            load(12, wdown_hbm.at[0], wdown),
        ]

    def load_qkv(l, r):
        rows = span(r * ROW_LEN, ROW_LEN, ROW_LEN)
        return pltpu.make_async_copy(qkv_hbm.at[l, rows], qkv.at[r], row_sem.at[r, 0])

    def load_norms(l, r):
        rows = span(r * ROW_LEN, ROW_LEN, ROW_LEN)
        return [
            pltpu.make_async_copy(
                unit_hbm.at[l, 0, rows], unit.at[0, rows], row_sem.at[r, 1]
            ),
            pltpu.make_async_copy(
                unit_hbm.at[l, 1, rows], unit.at[1, rows], row_sem.at[r, 2]
            ),
            pltpu.make_async_copy(inv_hbm.at[l, 0, rows], inv.at[0, rows], row_sem.at[r, 3]),
            pltpu.make_async_copy(inv_hbm.at[l, 1, rows], inv.at[1, rows], row_sem.at[r, 4]),
        ]

    def save_dx(r):
        rows = span(r * ROW_LEN, ROW_LEN, ROW_LEN)
        return pltpu.make_async_copy(dy.at[rows], dx_hbm.at[rows], row_sem.at[r, 5])

    load_dn2(0).start()
    load_cot().start()
    for copy in load_norms(1, 0):
        copy.start()
    load_out(1).start()
    load_qkv(1, 0).start()
    load_p(0).start()
    load_ffg().start()
    load_qkv_weight(1).start()
    for copy in load_feed():
        copy.start()
    load_dn2(1).start()
    for copy in load_norms(1, 1):
        copy.start()
    load_qkv(1, 1).start()
    load_kept().start()
    barrier = pltpu.get_barrier_semaphore()
    greet_hid(barrier, me)
    pl.semaphore_signal(
        barrier, inc=1, device_id={"dp": ff_sum.partner}, device_id_type=MESH
    )
    for k in HID_ORDER:
        pl.semaphore_signal(barrier, inc=1, device_id=ff_sum.peer(k), device_id_type=MESH)
    small[...] = jnp.zeros_like(small)
    ninth[...] = jnp.zeros_like(ninth)
    gtime_ref[...] = jnp.zeros_like(gtime_ref)
    pl.semaphore_wait(barrier, 15)
    load_ffg().wait()
    ff_sum.start()
    load_cot().wait()

    def attention_results(l, block):
        for n in range(3):
            cols = pl.ds(n * D, D)
            gq_ref[l, 0:8, cols] = block[8 * n : 8 * n + 8]
            gq_ref[l, 8:9, cols] = block[56 + n : 57 + n]
            gt_ref[l, 0:8, cols] = block[24 + 8 * n : 32 + 8 * n]
            gt_ref[l, 8:9, cols] = block[59 + n : 60 + n]
        go_ref[l, 0:8] = block[48:56]
        go_ref[l, 8:9] = block[62:63]

    def place(p, grad):
        half = lax.rem(p, 2)
        for c in range(DP):
            stage[c, span(8 * half, 8, 8)] = grad[8 * c : 8 * c + 8]
            ninth[c, pl.ds(p, 1)] = grad[128 + c : 129 + c]

    def flush(pair):
        for c in range(DP):
            x3[c // 2, c % 2, span(16 * pair, 16, 16)] = stage[c].astype(BF16)

    def attention_weights(l):
        def project(n, _):
            cols = span(n * D, D, 128)
            dproj[l, :, cols] = dot(pick_ref[...], dqkv[:, cols])
            return 0

        lax.fori_loop(0, 3, project, 0)

        def token_piece(n, _):
            cols = span(n * D, D, 128)
            place(n, dot_tn(kept[l, 0, :, 0:144], dqkv[:, cols]))
            pl.when(n == 1)(lambda: flush(0))
            return 0

        lax.fori_loop(0, 3, token_piece, 0)

        def time_piece(n, _):
            cols = span(n * D, D, 128)
            place(3 + n, dot_tn(timek_ref[:, 0:144], dproj[l, :, cols].astype(BF16)))
            pl.when(n == 0)(lambda: flush(1))
            pl.when(n == 2)(lambda: flush(2))
            return 0

        lax.fori_loop(0, 3, time_piece, 0)
        place(6, dot_tn(kept[l, 1, :, 0:144], dhl[...]))
        for c in range(DP):
            stage[c, 8:16] = ninth[c]
        flush(3)
        small[span(l * 16, 16, 16), 0:1024] = fold_tables(fold, me)

    def time_gradient(l):
        load_time_weight(l).wait()
        got = gtime_ref[...]
        for n in range(3):
            cols = pl.ds(n * D, D)
            got = got + dot_nt(dproj[l, :, cols].astype(BF16), wqkv[:, cols])
        gtime_ref[...] = got

    def step(j, _):
        l = 1 - j // 2
        r = lax.rem(j, 2)
        base = r * ROW_LEN
        rows = span(base, ROW_LEN, ROW_LEN)
        slot = 2 * l + r

        for copy in load_norms(1, r):
            copy.wait()

        @pl.when(l == 1)
        def _():
            pl.when(r == 0)(lambda: load_dn2(0).wait())
            pl.when(r == 1)(lambda: load_dn2(1).wait())
            dy[rows] = dxl[rows].astype(F32)

        @pl.when(l == 0)
        def _():
            sums.wait(r)

        @pl.when(r == 0)
        def _():
            fold[...] = jnp.zeros_like(fold)

        def second_norm(c, _):
            rr = span(base + c * CHUNK, CHUNK, CHUNK)
            dn = total[slot, span(c * CHUNK, CHUNK, CHUNK)].astype(F32)
            dh = dy[rr] + norm_slope(
                dn, unit[1, rr].astype(F32), inv[1, rr, 0:1], gain_ref[l, 1:2]
            )
            dy[rr] = dh
            dhl[rr] = dh.astype(BF16)
            return 0

        lax.fori_loop(0, ROW_LEN // CHUNK, second_norm, 0)
        mine = span(base + own_first, OWN, OWN)

        def norm_sums(which, dn):
            value = jnp.sum(dn * unit[which, mine].astype(F32), 0, keepdims=True)
            small[pl.ds(32 + 2 * l + which, 1)] += value
            small[pl.ds(36 + 2 * l + which, 1)] += jnp.sum(dn, 0, keepdims=True)

        norm_sums(1, total[slot, span(own_first, OWN, OWN)].astype(F32))

        @pl.when(r == 0)
        def _():
            load_out(1).wait()

        do_ref[...] = dot_nt(dhl[rows], wout[...]).astype(BF16)

        @pl.when(j == 1)
        def _():
            load_out(0).start()

        load_qkv(1, r).wait()
        load_p(j).wait()
        attend_backward(qkv, r, do_ref, p_ref, acc, ds_ref, fold, kind_ref, own_first)

        @pl.when(j < 3)
        def _():
            load_p(j + 1).start()

        @pl.when(l == 1)
        def _():
            load_qkv(0, r).start()

        @pl.when(j == 0)
        def _():
            ff_sum.exchange()

        @pl.when(j == 1)
        def _():
            sums.add_and_gather(0)
            ffo_ref[1] = ff_sum.finish()
            ff_sum.release()

        @pl.when(j == 2)
        def _():
            ff_sum.exchange()
            at_sum.exchange()

        @pl.when(j == 3)
        def _():
            ffo_ref[0] = ff_sum.finish()
            attention_results(1, at_sum.finish())
            at_sum.release()

        dqkv[rows, 0:D] = (acc[:, 0:D] * SCALE).astype(BF16)
        dqkv[rows, D : 2 * D] = (acc[:, D : 2 * D] * SCALE).astype(BF16)
        dqkv[rows, 2 * D :] = acc[:, 2 * D :].astype(BF16)

        @pl.when(r == 0)
        def _():
            load_qkv_weight(1).wait()

        def back(n, _):
            cols = span(n * D, D, 128)
            got = dot_nt(dqkv[rows, cols], wqkv[:, cols])

            @pl.when(n == 0)
            def _():
                acc[:, 0:D] = got

            @pl.when(n > 0)
            def _():
                acc[:, 0:D] += got

            return 0

        lax.fori_loop(0, 3, back, 0)

        @pl.when(r == 1)
        def _():
            load_time_weight(l).start()

        def first_norm(c, _):
            rr = span(base + c * CHUNK, CHUNK, CHUNK)
            dn = acc[span(c * CHUNK, CHUNK, CHUNK), 0:D]
            dy[rr] = dy[rr] + norm_slope(
                dn, unit[0, rr].astype(F32), inv[0, rr, 0:1], gain_ref[l, 0:1]
            )
            return 0

        lax.fori_loop(0, ROW_LEN // CHUNK, first_norm, 0)
        norm_sums(0, acc[span(own_first, OWN, OWN), 0:D])

        @pl.when(l == 0)
        def _():
            save_dx(r).start()

        @pl.when(l == 1)
        def _():
            for copy in load_norms(0, r):
                copy.start()

            @pl.when(r == 0)
            def _():
                for copy in load_feed():
                    copy.wait()

            dxl[rows] = dy[rows].astype(BF16)
            gh = dot_nt(dxl[rows], wdown[...])
            du = (gh * gelu_slope(u_ref[rows])).astype(BF16)
            du_ref[rows] = du
            part[r] = dot_nt(du, wup[...]).astype(BF16)
            sums.scatter(r)
            small[40:41] += jnp.sum(dxl[mine].astype(F32), 0, keepdims=True)

        @pl.when(j == 1)
        def _():
            write_ff_grads(
                x2,
                lambda: dot_tn(second[...], du_ref[...]),
                lambda: dot_tn(dxl[...], g_ref[...]),
            )
            ff_sum.acquire()
            ff_sum.start()
            load_kept().wait()

        @pl.when(r == 1)
        def _():
            attention_weights(l)

            @pl.when(l == 0)
            def _():
                at_sum.acquire()

            at_sum.start()

        @pl.when(j == 1)
        def _():
            sums.add_and_gather(1)
            time_gradient(1)
            load_qkv_weight(0).start()

        return 0

    lax.fori_loop(0, 4, step, 0)

    odd = lax.rem(me, 2).astype(F32)
    for l, value in enumerate(
        (jnp.sum(du_ref[...].astype(F32), 0, keepdims=True), gbup_ref[...])
    ):
        small[pl.ds(42 + 4 * l + me // 2, 1)] = jnp.concatenate(
            [value * (1.0 - odd), value * odd], axis=1
        )
    small[41:42] = gbdown_ref[...]

    def small_scatter(k):
        peer = hid_peer(me, k)
        return pltpu.make_async_remote_copy(
            src_ref=small.at[span(peer * 8, 8, 8)],
            dst_ref=small_recv.at[k - 1],
            send_sem=small_sems.at[0, k - 1],
            recv_sem=small_sems.at[1, k - 1],
            device_id={"hid": peer},
            device_id_type=MESH,
        )

    def small_swap():
        return pltpu.make_async_remote_copy(
            src_ref=small_sum.at[0],
            dst_ref=small_pair,
            send_sem=small_one.at[0],
            recv_sem=small_one.at[1],
            device_id={"dp": ff_sum.partner},
            device_id_type=MESH,
        )

    def small_spread(k, outgoing):
        chip = ff_sum.chip
        if not outgoing:
            chip = lax.rem(ff_sum.y + 4 - k // 2, 4) * 2 + lax.rem(ff_sum.z + k, 2)
        return pltpu.make_async_remote_copy(
            src_ref=small_chip.at[chip],
            dst_ref=small_chip.at[chip],
            send_sem=small_sems.at[2, k - 1],
            recv_sem=small_sems.at[3, k - 1],
            device_id=ff_sum.peer(k),
            device_id_type=MESH,
        )

    def small_gather(k, outgoing):
        owner = me if outgoing else hid_source(me, k)
        rows = small_out.at[span(owner * 8, 8, 8)]
        return pltpu.make_async_remote_copy(
            src_ref=rows,
            dst_ref=rows,
            send_sem=small_sems.at[4, k - 1],
            recv_sem=small_sems.at[5, k - 1],
            device_id={"hid": hid_peer(me, k)},
            device_id_type=MESH,
        )

    for k in HID_ORDER:
        small_scatter(k).start()
    at_sum.exchange()
    for k in HID_ORDER:
        small_scatter(k).wait_recv()
    value = small[span(me * 8, 8, 8)]
    for k in range(HID - 1):
        value = value + small_recv[k]
    small_sum[0] = value
    small_swap().start()
    time_gradient(0)
    small_swap().wait_recv()
    small_chip[ff_sum.chip] = small_sum[0] + small_pair[...]
    for k in HID_ORDER:
        small_spread(k, True).start()
    for k in HID_ORDER:
        small_spread(k, False).wait_recv()
    value = small_chip[0]
    for c in range(1, 8):
        value = value + small_chip[c]
    small_out[span(me * 8, 8, 8)] = value
    for k in HID_ORDER:
        small_gather(k, True).start()
    attention_results(0, at_sum.finish())
    for k in HID_ORDER:
        small_gather(k, False).wait_recv()
    for k in HID_ORDER:
        small_scatter(k).wait_send()
        small_spread(k, True).wait_send()
        small_gather(k, True).wait_send()
    small_swap().wait_send()
    for r in range(2):
        save_dx(r).wait()
        sums.drain(r)


def backward(vmem_args, hbm_args):
    s = jax.ShapeDtypeStruct
    v = pltpu.VMEM
    dma = pltpu.SemaphoreType.DMA
    return pl.pallas_call(
        backward_kernel,
        out_shape=[
            s((8, D), F32),
            s((LAYERS, KEPT, 3 * D), F32),
            s((LAYERS, KEPT, 3 * D), F32),
            s((LAYERS, KEPT, D), F32),
            s((LAYERS, 80, D), F32),
            s((64, D), F32),
            s((TOKENS, D), F32),
        ],
        in_specs=[IN_VMEM] * len(vmem_args) + [IN_ANY] * len(hbm_args),
        out_specs=[IN_VMEM] * 6 + [IN_ANY],
        scratch_shapes=[
            v((D, 3 * D), BF16),
            v((D, D), BF16),
            v((D, UNITS), BF16),
            v((UNITS, D), BF16),
            v((2, ROW_LEN, 3 * D), BF16),
            v((HEADS, ROW_LEN, ROW_LEN), BF16),
            v((2, TOKENS, D), BF16),
            v((2, TOKENS, 128), F32),
            v((LAYERS, 2, TOKENS, 256), BF16),
            v((TOKENS, D), BF16),
            v((TOKENS, UNITS), F32),
            v((TOKENS, UNITS), BF16),
            v((4, ROW_LEN, D), BF16),
            v((2, ROW_LEN, D), BF16),
            v((2, HID - 1, SLICE, D), BF16),
            v((TOKENS, D), F32),
            v((TOKENS, D), BF16),
            v((TOKENS, D), BF16),
            v((ROW_LEN, D), BF16),
            v((ROW_LEN, 3 * D), F32),
            v((TOKENS, 3 * D), BF16),
            v((TOKENS, UNITS), BF16),
            v((2, ROW_LEN, ROW_LEN), F32),
            v((8, 2, 80, D), BF16),
            v((8, 80, D), BF16),
            v((7, 80, D), BF16),
            v((8, 2, 64, D), BF16),
            v((8, 64, D), BF16),
            v((7, 64, D), BF16),
            v((DP, 16, D), F32),
            v((DP, 8, D), F32),
            v((2, HEADS, OWN, ROW_LEN), F32),
            v((LAYERS, 8, 3 * D), F32),
            v((64, D), F32),
            v((7, 8, D), F32),
            v((1, 8, D), F32),
            v((8, D), F32),
            v((8, 8, D), F32),
            dma((13,)),
            dma((2, 6)),
            dma((4, 2, HID - 1)),
            dma((4,)),
            dma((4, 7)),
            pltpu.SemaphoreType.REGULAR,
            pltpu.SemaphoreType.REGULAR,
            dma((6, HID - 1)),
            dma((2,)),
        ],
        compiler_params=pltpu.CompilerParams(
            collective_id=2, has_side_effects=True, vmem_limit_bytes=VMEM_LIMIT
        ),
        name="backward",
    )(*vmem_args, *hbm_args)


def shards(
    block_in,
    time_tokens,
    layout,
    norm_gain,
    norm_bias,
    w_qkv,
    w_time,
    rel_table,
    w_out,
    w_up,
    b_up,
    w_down,
    b_down,
    cotangent,
):
    is_four = layout == 1
    slot = jnp.arange(SLOTS)
    quarter_slot = jnp.where(is_four[:, None], slot[None, :], 0)
    token_slot = jnp.repeat(quarter_slot, 64, axis=1)
    pick = (
        (jnp.arange(2)[:, None, None, None] == jnp.arange(2)[None, None, :, None])
        & (slot[None, :, None, None] == token_slot[None, None])
    ).reshape(8, TOKENS)
    kind = jnp.broadcast_to(
        jnp.stack([~is_four, is_four], 1).astype(F32)[:, :, None], (2, 2, ROW_LEN)
    )
    time_flat = time_tokens.reshape(8, D)
    cot = cotangent.reshape(TOKENS, D)
    bias, tp = prepare(layout, rel_table, time_flat, w_time)
    (
        gbup,
        gbdown,
        timek,
        block_out,
        dn2,
        ffg,
        qkv,
        p,
        unit,
        inv,
        kept,
        second,
        u,
        g,
    ) = forward(
        block_in.reshape(TOKENS, D),
        cot,
        tp,
        norm_gain,
        norm_bias,
        b_up[:, None],
        b_down,
        time_flat,
        w_qkv,
        w_out,
        w_up,
        w_down,
        bias,
    )
    gtime, gq, gt, go, ffo, small, dx = backward(
        (norm_gain, pick.astype(BF16), kind, timek, gbup, gbdown),
        (
            dn2,
            cot,
            ffg,
            qkv,
            p,
            unit,
            inv,
            kept,
            second,
            u,
            g,
            w_qkv,
            w_out,
            w_up,
            w_down,
            w_time,
        ),
    )
    table = small[:32, :1024].reshape(LAYERS, HEADS, 32, 32)[:, :, REL - 1 :: -1, :REL]
    return (
        block_out.reshape(2, ROW_LEN, D),
        dx.reshape(2, ROW_LEN, D),
        gtime.reshape(2, SLOTS, D),
        small[32:36].reshape(LAYERS, 2, D),
        small[36:40].reshape(LAYERS, 2, D),
        gq,
        gt,
        table,
        go,
        ffo[:, :72, :UNITS],
        small[42:50].reshape(LAYERS, FF),
        jnp.swapaxes(ffo[:, :72, UNITS:], 1, 2),
        small[40:42],
    )


def solution(mesh):
    in_specs = (
        P("dp", None, None),
        P("dp", None, None),
        P("dp"),
        P(),
        P(),
        P(),
        P(),
        P(),
        P(),
        P(None, None, "hid"),
        P(None, "hid"),
        P(None, "hid", None),
        P(),
        P("dp", None, None),
    )
    out_specs = (
        P("dp", None, None),
        P("dp", None, None),
        P("dp", None, None),
        P(),
        P(),
        P(None, ("dp", "hid"), None),
        P(None, ("dp", "hid"), None),
        P(),
        P(None, ("dp", "hid"), None),
        P(None, "dp", "hid"),
        P(),
        P(None, "hid", "dp"),
        P(),
    )
    return jax.shard_map(shards, mesh=mesh, in_specs=in_specs, out_specs=out_specs, check_vma=False)
```

```python
import functools

import jax
import jax.numpy as jnp
from jax import lax
from jax.experimental import pallas as pl
from jax.experimental.pallas import tpu as pltpu
from jax.sharding import PartitionSpec as P

D = 1152
HEADS = 16
HEAD_DIM = 72
FF = 4608
LAYERS = 2
GRID = 16
SUB = 8
ROW_LEN = 256
SLOTS = 4
REL = 31
DP = 16
HID = 8
UNITS = FF // HID
KEPT = D // (DP * HID)
TOKENS = 512
OWN = ROW_LEN // HID
SCALE = HEAD_DIM ** (-0.5)
MASKED_LOGIT = -1e30
NORM_EPSILON = 1e-06
F32 = jnp.float32
BF16 = jnp.bfloat16
MESH = pl.DeviceIdType.MESH
VMEM_LIMIT = 63 * 1024 * 1024
HIGHEST = lax.Precision.HIGHEST


def contract(a, b, da, db, precision=None):
    return lax.dot_general(
        a, b, (((da,), (db,)), ((), ())), preferred_element_type=F32, precision=precision
    )


def dot(a, b):
    return contract(a, b, 1, 0)


def dot_nt(a, b):
    return contract(a, b, 1, 1)


def dot_tn(a, b):
    return contract(a, b, 0, 0)


def span(start, size, multiple):
    return pl.ds(pl.multiple_of(start, multiple), size)


def gelu_parts(v):
    c = 0.7978845608028654
    square = v * v
    t = jnp.tanh(c * v * (1.0 + 0.044715 * square))
    return t, square


def gelu(v):
    t, _ = gelu_parts(v)
    return 0.5 * v * (1.0 + t)


def gelu_slope(v):
    c = 0.7978845608028654
    t, square = gelu_parts(v)
    return 0.5 * (1.0 + t) + 0.5 * v * (1.0 - t * t) * (c * (1.0 + 3.0 * 0.044715 * square))


def prepare_kernel(
    layout_ref, rel_ref, time_ref, wtime_ref, bias_ref, tp_ref, kind_ref, rows_ref, skew_ref, turned_ref
):
    g = pl.program_id(1)
    first, second = layout_ref[0], layout_ref[1]

    @pl.when(g == 0)
    def _():
        tp_ref[...] = jnp.zeros_like(tp_ref)
        for r in range(2):
            four = jnp.where(layout_ref[r] == 1, 1.0, 0.0)
            kind_ref[r, 0:1] = jnp.full((1, ROW_LEN), 1.0 - four, F32)
            kind_ref[r, 1:2] = jnp.full((1, ROW_LEN), four, F32)

    @pl.when(g < 3)
    def _():
        tp_ref[0] += dot(time_ref[:, span(384 * g, 384, 128)], wtime_ref[0])

    @pl.when(g == 3)
    def _():
        for r in range(2):

            @pl.when(layout_ref[r] != 1)
            def _():
                tp_ref[0, 4 * r : 4 * r + 4] = jnp.broadcast_to(
                    tp_ref[0, 4 * r : 4 * r + 1], (SLOTS, 3 * D)
                )

    rows_ref[...] = jnp.zeros_like(rows_ref)
    rows_ref[:, 0:4, 0:REL] = rel_ref[0, :, pl.ds(4 * g, 4), :]
    table = rows_ref[:, 0]
    for i in range(1, 4):
        table = table + pltpu.roll(rows_ref[:, i], 32 * i, 1)

    def skewed(side, count, top):
        skew_ref[...] = jnp.zeros_like(skew_ref)
        for j in range(count):
            block = jnp.broadcast_to(table[top - j : top - j + 1], (side, 128))
            skew_ref[pl.ds(side * j, side)] = pltpu.roll(
                block, 113, 1, stride=1, stride_axis=0
            )

    def single(r):
        skewed(GRID, REL, REL - 1)
        turned_ref[...] = skew_ref[...].T
        for i in range(4):
            w = turned_ref[32 * i : 32 * i + GRID]
            for m in range(8):
                moved = w if m == 0 else pltpu.roll(w, 512 - 16 * m, 1)
                for t in range(2):
                    y = 15 - 8 * t - m
                    bias_ref[0, r, i, pl.ds(GRID * y, GRID), :] = moved[
                        :, 128 * t : 128 * t + ROW_LEN
                    ]

    def quad(r):
        skewed(SUB, 15, 22)
        turned_ref[:, 0:128] = skew_ref[0:128].T
        half = lax.broadcasted_iota(jnp.int32, (SUB, 128), 1) // 64
        closed = jnp.full((SUB, 128), MASKED_LOGIT, F32)
        for i in range(4):
            w = turned_ref[32 * i : 32 * i + SUB, 0:128]
            for y in range(SUB):
                for odd in range(2):
                    moved = pltpu.roll(w, (128 + 64 * odd - (7 - y) * SUB) % 128, 1)
                    moved = jnp.where(half == odd, moved, MASKED_LOGIT)
                    for tile in range(2):
                        rows = pl.ds(64 * (2 * tile + odd) + SUB * y, SUB)
                        bias_ref[0, r, i, rows, 128 * tile : 128 * tile + 128] = moved
                        bias_ref[0, r, i, rows, 128 - 128 * tile : 256 - 128 * tile] = closed

    pl.when(first != 1)(lambda: single(0))
    pl.when(first == 1)(lambda: quad(0))

    @pl.when(first == second)
    def _():
        for i in range(4):
            bias_ref[0, 1, i] = bias_ref[0, 0, i]

    pl.when((first != second) & (second != 1))(lambda: single(1))
    pl.when((first != second) & (second == 1))(lambda: quad(1))


def prepare(layout, rel_table, time_flat, w_time):
    return pl.pallas_call(
        prepare_kernel,
        out_shape=[
            jax.ShapeDtypeStruct((LAYERS, 2, HEADS, ROW_LEN, ROW_LEN), F32),
            jax.ShapeDtypeStruct((LAYERS, 8, 3 * D), F32),
            jax.ShapeDtypeStruct((2, 2, ROW_LEN), F32),
        ],
        grid_spec=pltpu.PrefetchScalarGridSpec(
            num_scalar_prefetch=1,
            grid=(LAYERS, 4),
            in_specs=[
                pl.BlockSpec((1, REL, HEADS, REL), lambda l, g, _: (l, 0, 0, 0)),
                pl.BlockSpec((8, D), lambda l, g, _: (0, 0)),
                pl.BlockSpec((1, 384, 3 * D), lambda l, g, _: (l, jnp.minimum(g, 2), 0)),
            ],
            out_specs=[
                pl.BlockSpec((1, 2, 4, ROW_LEN, ROW_LEN), lambda l, g, _: (l, 0, g, 0, 0)),
                pl.BlockSpec((1, 8, 3 * D), lambda l, g, _: (l, 0, 0)),
                pl.BlockSpec((2, 2, ROW_LEN), lambda l, g, _: (0, 0, 0)),
            ],
            scratch_shapes=[
                pltpu.VMEM((REL, 8, 128), F32),
                pltpu.VMEM((512, 128), F32),
                pltpu.VMEM((128, 512), F32),
            ],
        ),
        compiler_params=pltpu.CompilerParams(vmem_limit_bytes=VMEM_LIMIT),
        name="prepare",
    )(layout, jnp.swapaxes(rel_table, 1, 2), time_flat, w_time)


IN_VMEM = pl.BlockSpec(memory_space=pltpu.VMEM)
IN_ANY = pl.BlockSpec(memory_space=pl.ANY)
CHUNK = 128
HID_ORDER = (2, 6, 1, 4, 3, 7, 5)
SLICE = ROW_LEN // HID


def head_window(h):
    start = h * HEAD_DIM // 128 * 128
    offset = h * HEAD_DIM - start
    width = 128 if offset + HEAD_DIM <= 128 else 256
    lane = lax.broadcasted_iota(jnp.int32, (1, width), 1)
    mask = ((lane >= offset) & (lane < offset + HEAD_DIM)).astype(F32).astype(BF16)
    return start, width, mask


def hid_peer(me, k):
    return lax.rem(me // 2 + k // 2, 4) * 2 + lax.rem(me + k, 2)


def hid_source(me, k):
    return lax.rem(me // 2 + 4 - k // 2, 4) * 2 + lax.rem(me + k, 2)


def greet_hid(barrier, me):
    for k in HID_ORDER:
        pl.semaphore_signal(
            barrier, inc=1, device_id={"hid": hid_peer(me, k)}, device_id_type=MESH
        )


class HidSums:
    def __init__(self, part, recv, total, sems):
        self.part, self.recv, self.total = part, recv, total
        self.send1, self.recv1, self.send2, self.recv2 = sems
        self.me = lax.axis_index("hid")

    def scatter_copy(self, e, k):
        peer = hid_peer(self.me, k)
        return pltpu.make_async_remote_copy(
            src_ref=self.part.at[e, span(peer * SLICE, SLICE, SLICE)],
            dst_ref=self.recv.at[e, k - 1],
            send_sem=self.send1.at[e, k - 1],
            recv_sem=self.recv1.at[e, k - 1],
            device_id={"hid": peer},
            device_id_type=MESH,
        )

    def gather_copy(self, slot, e, k, outgoing):
        owner = self.me if outgoing else hid_source(self.me, k)
        rows = self.total.at[slot, span(owner * SLICE, SLICE, SLICE)]
        return pltpu.make_async_remote_copy(
            src_ref=rows,
            dst_ref=rows,
            send_sem=self.send2.at[e, k - 1],
            recv_sem=self.recv2.at[e, k - 1],
            device_id={"hid": hid_peer(self.me, k)},
            device_id_type=MESH,
        )

    def scatter(self, e):
        for k in HID_ORDER:
            self.scatter_copy(e, k).start()

    def add_and_gather(self, e):
        mine = span(self.me * SLICE, SLICE, SLICE)
        for k in HID_ORDER:
            self.scatter_copy(e, k).wait_recv()
        total = self.part[e, mine].astype(F32)
        for k in range(HID - 1):
            total = total + self.recv[e, k].astype(F32)
        self.total[e, mine] = total.astype(BF16)
        for k in HID_ORDER:
            self.gather_copy(e, e, k, True).start()

    def wait(self, e):
        for k in HID_ORDER:
            self.gather_copy(e, e, k, False).wait_recv()

    def drain(self, e):
        for k in HID_ORDER:
            self.scatter_copy(e, k).wait_send()
            self.gather_copy(e, e, k, True).wait_send()


def write_ff_grads(ffg, up_of, down_of):
    up = up_of()
    for c in range(DP):
        ffg[c // 2, c % 2, 0:72, 0:UNITS] = up[72 * c : 72 * (c + 1)].astype(BF16)
    down = down_of()
    for c in range(DP):
        ffg[c // 2, c % 2, 0:72, UNITS : 2 * UNITS] = down[72 * c : 72 * (c + 1)].astype(BF16)


def layer_norm_rows(x, gain, shift):
    centre = x - jnp.mean(x, -1, keepdims=True)
    inverse = lax.rsqrt(jnp.mean(centre * centre, -1, keepdims=True) + NORM_EPSILON)
    unit = centre * inverse
    return (unit * gain + shift).astype(BF16), unit.astype(BF16), inverse


def kept_matrix():
    feature = lax.broadcasted_iota(jnp.int32, (D, 256), 0)
    column = lax.broadcasted_iota(jnp.int32, (D, 256), 1)
    low = column < 128
    owner = jnp.where(low, column // 8, column - 128)
    inner = jnp.where(low, column % 8, 8)
    chosen = (feature == owner * 72 + lax.axis_index("hid") * KEPT + inner) & (column < 144)
    return chosen.astype(F32).astype(BF16)


def attend_forward(qkv, r, bias_ref, p_ref, o_acc):
    o_acc[...] = jnp.zeros_like(o_acc)

    def scores(h):
        start, width, mask = head_window(h)
        q = qkv[r, :, start : start + width] * mask
        return dot_nt(q, qkv[r, :, D + start : D + start + width])

    def mix(h, score):
        start, width, mask = head_window(h)
        logits = score * SCALE + bias_ref[h]
        expo = jnp.exp(logits - jnp.max(logits, -1, keepdims=True))
        p = (expo * (1.0 / jnp.sum(expo, -1, keepdims=True))).astype(BF16)
        p_ref[h] = p
        v = qkv[r, :, 2 * D + start : 2 * D + start + width] * mask
        o_acc[:, start : start + width] += dot(p, v)

    ready = {}
    for h in range(HEADS + 1):
        if h < HEADS:
            ready[h] = scores(h)
        if h:
            mix(h - 1, ready.pop(h - 1))


def forward_kernel(
    x_ref,
    cot_ref,
    tp_ref,
    gain_ref,
    shift_ref,
    bup_ref,
    bdown_ref,
    time_ref,
    wqkv_hbm,
    wout_hbm,
    wup_hbm,
    wdown_hbm,
    bias_hbm,
    gbup_ref,
    gbdown_ref,
    timek_ref,
    h_hbm,
    fpart_hbm,
    dn2_hbm,
    ffg_hbm,
    qkv_hbm,
    p_hbm,
    unit_hbm,
    inv_hbm,
    kept_hbm,
    second_hbm,
    u_hbm,
    g_hbm,
    wqkv,
    wout,
    wup,
    wdown,
    bias_ref,
    p_ref,
    qkv,
    part,
    fpart,
    recv,
    total,
    h_ref,
    first,
    att,
    o_acc,
    unit,
    inv,
    pick,
    kept,
    second,
    u_ref,
    g_ref,
    du_ref,
    ffg,
    w_sem,
    save_sem,
    send1,
    recv1,
    send2,
    recv2,
):
    me = lax.axis_index("hid")
    sums = HidSums(part, recv, total, (send1, recv1, send2, recv2))

    def load_qkv(l, n):
        cols = pl.ds(n * D, D)
        return pltpu.make_async_copy(
            wqkv_hbm.at[l, :, cols], wqkv.at[:, cols], w_sem.at[13 + n]
        )

    def load_bias(i):
        return pltpu.make_async_copy(
            bias_hbm.at[i // 2, lax.rem(i, 2)], bias_ref, w_sem.at[16]
        )

    def load(hbm, ref, l, n):
        return pltpu.make_async_copy(hbm.at[l], ref.at[l], w_sem.at[2 + 2 * n + l])

    def load_out(l):
        return load(wout_hbm, wout, l, 0)

    def load_up(l):
        return load(wup_hbm, wup, l, 1)

    def load_down(l):
        return load(wdown_hbm, wdown, l, 2)

    for n in range(3):
        load_qkv(0, n).start()
    load_bias(0).start()
    for l in range(LAYERS):
        load_out(l).start()
        load_up(l).start()
        load_down(l).start()
    barrier = pltpu.get_barrier_semaphore()
    greet_hid(barrier, me)
    pick[...] = kept_matrix()
    timek_ref[...] = dot(time_ref[...], pick[...]).astype(BF16)
    pl.semaphore_wait(barrier, HID - 1)

    def saves(l, r):
        rows = span(r * ROW_LEN, ROW_LEN, ROW_LEN)
        pairs = [
            (qkv.at[r], qkv_hbm.at[l, rows]),
            (unit.at[0, rows], unit_hbm.at[l, 0, rows]),
            (unit.at[1, rows], unit_hbm.at[l, 1, rows]),
            (inv.at[0, rows], inv_hbm.at[l, 0, rows]),
            (inv.at[1, rows], inv_hbm.at[l, 1, rows]),
            (kept.at[0, rows], kept_hbm.at[l, 0, rows]),
            (kept.at[1, rows], kept_hbm.at[l, 1, rows]),
        ]
        return [
            pltpu.make_async_copy(a, b, save_sem.at[r, n]) for n, (a, b) in enumerate(pairs)
        ]

    def feed_saves(r):
        rows = span(r * ROW_LEN, ROW_LEN, ROW_LEN)
        pairs = [(second, second_hbm), (u_ref, u_hbm), (g_ref, g_hbm)]
        return [
            pltpu.make_async_copy(a.at[rows], b.at[rows], save_sem.at[r, 7 + n])
            for n, (a, b) in enumerate(pairs)
        ]

    def results(r):
        rows = span(r * ROW_LEN, ROW_LEN, ROW_LEN)
        return [
            pltpu.make_async_copy(h_ref.at[rows], h_hbm.at[rows], w_sem.at[9 + r]),
            pltpu.make_async_copy(fpart.at[r], fpart_hbm.at[r], w_sem.at[11 + r]),
        ]

    def save_dn2(r):
        rows = pl.ds(r * ROW_LEN, ROW_LEN)
        return pltpu.make_async_copy(total.at[2 + r], dn2_hbm.at[rows], w_sem.at[r])

    def save_p(l, r):
        return pltpu.make_async_copy(p_ref, p_hbm.at[l, r], save_sem.at[0, 10])

    def step(i, _):
        l = i // 2
        r = lax.rem(i, 2)
        base = r * ROW_LEN
        rows = span(base, ROW_LEN, ROW_LEN)

        @pl.when(l == 0)
        def _():
            h_ref[rows] = x_ref[rows].astype(F32)

        @pl.when(l == 1)
        def _():
            for copy in saves(0, r) + feed_saves(r):
                copy.wait()
            sums.wait(r)
            h_ref[rows] = h_ref[rows] + (total[r].astype(F32) + bdown_ref[0:1])

        def norm(which):
            def body(c, _):
                rr = span(base + c * CHUNK, CHUNK, CHUNK)
                low, value, inverse = layer_norm_rows(
                    h_ref[rr], gain_ref[l, which : which + 1], shift_ref[l, which : which + 1]
                )
                if which == 0:
                    first[span(c * CHUNK, CHUNK, CHUNK)] = low
                else:
                    second[rr] = low
                unit[which, rr] = value
                inv[which, rr] = jnp.broadcast_to(inverse, (CHUNK, 128))
                return 0

            lax.fori_loop(0, ROW_LEN // CHUNK, body, 0)

        norm(0)

        for n in range(3):

            @pl.when(r == 0)
            def _():
                load_qkv(l, n).wait()

            cols = pl.ds(n * D, D)
            wide = dot(first[...], wqkv[:, cols])
            for s in range(SLOTS):
                qkv[r, 64 * s : 64 * (s + 1), cols] = (
                    wide[64 * s : 64 * (s + 1)] + tp_ref[l, pl.ds(4 * r + s, 1), cols]
                ).astype(BF16)

        @pl.when(i == 1)
        def _():
            for n in range(3):
                load_qkv(1, n).start()

        @pl.when(i == 2)
        def _():
            sums.add_and_gather(1)

        kept[0, rows] = dot(first[...], pick[...]).astype(BF16)
        load_bias(i).wait()

        @pl.when(i > 0)
        def _():
            save_p(0, 0).wait()

        attend_forward(qkv, r, bias_ref, p_ref, o_acc)
        save_p(l, r).start()

        @pl.when(i < 3)
        def _():
            load_bias(i + 1).start()

        @pl.when(i == 1)
        def _():
            sums.add_and_gather(0)

        @pl.when(i == 3)
        def _():
            sums.add_and_gather(2)

        att[...] = o_acc[...].astype(BF16)
        kept[1, rows] = dot(att[...], pick[...]).astype(BF16)

        @pl.when(r == 0)
        def _():
            load_out(l).wait()
            load_up(l).wait()
            load_down(l).wait()

        h_ref[rows] = h_ref[rows] + dot(att[...], wout[l])
        norm(1)
        for copy in saves(l, r):
            copy.start()
        u_ref[rows] = dot_nt(second[rows], wup[l]) + bup_ref[pl.ds(l, 1)]
        g_ref[rows] = gelu(u_ref[rows]).astype(BF16)

        @pl.when(l == 0)
        def _():
            for copy in feed_saves(r):
                copy.start()

        @pl.when(l == 1)
        def _():
            gh = dot_nt(cot_ref[rows], wdown[1])
            du = (gh * gelu_slope(u_ref[rows])).astype(BF16)
            du_ref[rows] = du
            part[2 + r] = dot(du, wup[1]).astype(BF16)
            sums.scatter(2 + r)
            fpart[r] = dot(g_ref[rows], wdown[1]).astype(BF16)
            for copy in results(r):
                copy.start()

        @pl.when(l == 0)
        def _():
            part[r] = dot(g_ref[rows], wdown[0]).astype(BF16)
            sums.scatter(r)

        return 0

    lax.fori_loop(0, 4, step, 0)
    write_ff_grads(
        ffg,
        lambda: dot_tn(second[...], du_ref[...]),
        lambda: dot_tn(cot_ref[...], g_ref[...]),
    )
    ffg_copy = pltpu.make_async_copy(ffg, ffg_hbm, w_sem.at[8])
    ffg_copy.start()
    gbup_ref[...] = jnp.sum(du_ref[...].astype(F32), 0, keepdims=True)
    own = jnp.zeros((1, D), F32)
    for r in range(2):
        own = own + jnp.sum(
            cot_ref[span(r * ROW_LEN + me * OWN, OWN, OWN)].astype(F32), 0, keepdims=True
        )
    gbdown_ref[...] = own
    sums.add_and_gather(3)
    for r in range(2):
        sums.wait(2 + r)
        save_dn2(r).start()
        for copy in saves(1, r) + results(r):
            copy.wait()
    save_p(0, 0).wait()
    ffg_copy.wait()
    for r in range(2):
        save_dn2(r).wait()
    for e in range(4):
        sums.drain(e)


def forward(x, cot, tp, gain, shift, b_up, b_down, time_flat, w_qkv, w_out, w_up, w_down, bias):
    s = jax.ShapeDtypeStruct
    v = pltpu.VMEM
    dma = pltpu.SemaphoreType.DMA
    return pl.pallas_call(
        forward_kernel,
        out_shape=[
            s((1, UNITS), F32),
            s((1, D), F32),
            s((8, 256), BF16),
            s((TOKENS, D), F32),
            s((2, ROW_LEN, D), BF16),
            s((TOKENS, D), BF16),
            s((8, 2, 80, D), BF16),
            s((LAYERS, TOKENS, 3 * D), BF16),
            s((LAYERS, 2, HEADS, ROW_LEN, ROW_LEN), BF16),
            s((LAYERS, 2, TOKENS, D), BF16),
            s((LAYERS, 2, TOKENS, 128), F32),
            s((LAYERS, 2, TOKENS, 256), BF16),
            s((TOKENS, D), BF16),
            s((TOKENS, UNITS), F32),
            s((TOKENS, UNITS), BF16),
        ],
        in_specs=[IN_VMEM] * 8 + [IN_ANY] * 5,
        out_specs=[IN_VMEM] * 3 + [IN_ANY] * 12,
        scratch_shapes=[
            v((D, 3 * D), BF16),
            v((LAYERS, D, D), BF16),
            v((LAYERS, UNITS, D), BF16),
            v((LAYERS, UNITS, D), BF16),
            v((HEADS, ROW_LEN, ROW_LEN), F32),
            v((HEADS, ROW_LEN, ROW_LEN), BF16),
            v((2, ROW_LEN, 3 * D), BF16),
            v((4, ROW_LEN, D), BF16),
            v((2, ROW_LEN, D), BF16),
            v((4, HID - 1, SLICE, D), BF16),
            v((4, ROW_LEN, D), BF16),
            v((TOKENS, D), F32),
            v((ROW_LEN, D), BF16),
            v((ROW_LEN, D), BF16),
            v((ROW_LEN, D), F32),
            v((2, TOKENS, D), BF16),
            v((2, TOKENS, 128), F32),
            v((D, 256), BF16),
            v((2, TOKENS, 256), BF16),
            v((TOKENS, D), BF16),
            v((TOKENS, UNITS), F32),
            v((TOKENS, UNITS), BF16),
            v((TOKENS, UNITS), BF16),
            v((8, 2, 80, D), BF16),
            dma((17,)),
            dma((2, 11)),
            dma((4, HID - 1)),
            dma((4, HID - 1)),
            dma((4, HID - 1)),
            dma((4, HID - 1)),
        ],
        compiler_params=pltpu.CompilerParams(
            collective_id=1, has_side_effects=True, vmem_limit_bytes=VMEM_LIMIT
        ),
        name="forward",
    )(x, cot, tp, gain, shift, b_up, b_down, time_flat, w_qkv, w_out, w_up, w_down, bias)


class DpSums:
    def __init__(self, x, pair, recv, sems, free):
        self.x, self.pair, self.recv, self.free = x, pair, recv, free
        self.pair_send, self.pair_recv, self.send, self.got = sems
        me = lax.axis_index("dp")
        self.y, self.z, self.core = me // 4, lax.rem(me // 2, 2), lax.rem(me, 2)
        self.chip = me // 2
        self.partner = self.chip * 2 + (1 - self.core)

    def other(self, k):
        return lax.rem(self.y + k // 2, 4) * 2 + lax.rem(self.z + k, 2)

    def peer(self, k):
        return {"dp": self.other(k) * 2 + self.core}

    def pair_copy(self):
        return pltpu.make_async_remote_copy(
            src_ref=self.x.at[:, 1 - self.core],
            dst_ref=self.pair,
            send_sem=self.pair_send,
            recv_sem=self.pair_recv,
            device_id={"dp": self.partner},
            device_id_type=MESH,
        )

    def start(self):
        self.pair_copy().start()

    def add_pair(self, c):
        both = self.x[c, self.core].astype(F32) + self.pair[c].astype(F32)
        self.pair[c] = both.astype(BF16)

    def release(self):
        pl.semaphore_signal(
            self.free, inc=1, device_id={"dp": self.partner}, device_id_type=MESH
        )
        for k in HID_ORDER:
            pl.semaphore_signal(self.free, inc=1, device_id=self.peer(k), device_id_type=MESH)

    def acquire(self):
        pl.semaphore_wait(self.free, 8)


class DirectSums(DpSums):
    def chip_copy(self, k):
        return pltpu.make_async_remote_copy(
            src_ref=self.pair.at[self.other(k)],
            dst_ref=self.recv.at[k - 1],
            send_sem=self.send.at[k - 1],
            recv_sem=self.got.at[k - 1],
            device_id=self.peer(k),
            device_id_type=MESH,
        )

    def exchange(self):
        self.pair_copy().wait_recv()
        for k in HID_ORDER + (0,):
            self.add_pair(self.other(k))
            if k:
                self.chip_copy(k).start()
        self.pair_copy().wait_send()

    def finish(self):
        total = self.pair[self.chip].astype(F32)
        for k in HID_ORDER:
            self.chip_copy(k).wait_recv()
            total = total + self.recv[k - 1].astype(F32)
        for k in HID_ORDER:
            self.chip_copy(k).wait_send()
        return total


class SteppedSums(DpSums):
    def y_copy(self, k):
        target = lax.rem(self.y + k, 4)
        return pltpu.make_async_remote_copy(
            src_ref=self.pair.at[pl.ds(2 * target, 2)],
            dst_ref=self.recv.at[pl.ds(2 * k - 2, 2)],
            send_sem=self.send.at[k - 1],
            recv_sem=self.got.at[k - 1],
            device_id=self.peer(2 * k),
            device_id_type=MESH,
        )

    def z_copy(self):
        return pltpu.make_async_remote_copy(
            src_ref=self.pair.at[2 * self.y + 1 - self.z],
            dst_ref=self.recv.at[6],
            send_sem=self.send.at[3],
            recv_sem=self.got.at[3],
            device_id=self.peer(1),
            device_id_type=MESH,
        )

    def exchange_y(self):
        self.pair_copy().wait_recv()
        for k in (2, 1, 3, 0):
            target = lax.rem(self.y + k, 4)
            for z in range(2):
                self.add_pair(2 * target + z)
            if k:
                self.y_copy(k).start()
        self.pair_copy().wait_send()

    def exchange_z(self):
        for k in (1, 3, 2):
            self.y_copy(k).wait_recv()
        for own in (False, True):
            z = self.z if own else 1 - self.z
            c = 2 * self.y + z
            block = self.pair[c].astype(F32)
            for k in (1, 2, 3):
                block = block + self.recv[2 * k - 2 + z].astype(F32)
            self.pair[c] = block.astype(BF16)
            if not own:
                self.z_copy().start()

    def finish(self):
        self.z_copy().wait_recv()
        total = self.pair[self.chip].astype(F32) + self.recv[6].astype(F32)
        for k in (1, 2, 3):
            self.y_copy(k).wait_send()
        self.z_copy().wait_send()
        return total


def norm_slope(dn, unit, inverse, gain):
    scaled = dn * gain
    return inverse * (
        scaled
        - jnp.mean(scaled, -1, keepdims=True)
        - unit * jnp.mean(scaled * unit, -1, keepdims=True)
    )


def attend_backward(qkv, r, do_ref, p_ref, acc, ds_ref, fold, kind_ref, own_first):
    acc[...] = jnp.zeros_like(acc)

    def slopes(h):
        start, width, mask = head_window(h)
        v = qkv[:, 2 * D + start : 2 * D + start + width] * mask
        return dot_nt(do_ref[:, start : start + width], v)

    def spread(h, dp):
        start, width, mask = head_window(h)
        p_low = p_ref[h]
        p = p_low.astype(F32)
        t = p * dp
        ds = t - p * jnp.sum(t, -1, keepdims=True)
        ds_ref[h % 2] = ds
        low = ds.astype(BF16)
        k = qkv[:, D + start : D + start + width] * mask
        q = qkv[:, start : start + width] * mask
        do = do_ref[:, start : start + width] * mask
        acc[:, start : start + width] += dot(low, k)
        acc[:, D + start : D + start + width] += dot_tn(low, q)
        acc[:, 2 * D + start : 2 * D + start + width] += dot_tn(p_low, do)
        mine = ds_ref[h % 2, span(own_first, OWN, OWN)]
        fold[0, h] += mine * kind_ref[r, 0:1]
        fold[1, h] += mine * kind_ref[r, 1:2]

    ready = {}
    depth = 2
    for h in range(HEADS + depth):
        if h < HEADS:
            ready[h] = slopes(h)
        if h >= depth:
            spread(h - depth, ready.pop(h - depth))


def two_part_dot(a, b):
    high = a.astype(BF16)
    low = (a - high.astype(F32)).astype(BF16)
    return dot(high, b) + dot(low, b)


def fold_tables(fold, me):
    lane = lax.broadcasted_iota(jnp.int32, (ROW_LEN, 512), 0)
    place = lax.broadcasted_iota(jnp.int32, (ROW_LEN, 512), 1)
    wide = (place == (lane // GRID) * 32 + 15 - lane % GRID).astype(F32).astype(BF16)
    inner = lane % (SUB * SUB)
    narrow = (place == (inner // SUB) * 32 + 15 - inner % SUB).astype(F32).astype(BF16)
    single = two_part_dot(fold[0].reshape(HEADS * OWN, ROW_LEN), wide)
    single = single.reshape(HEADS * 2, GRID, 512)
    quad = two_part_dot(fold[1].reshape(HEADS * OWN, ROW_LEN), narrow)
    quad = quad.reshape(HEADS * 4, SUB, 512)
    out = jnp.zeros((HEADS, 1024), F32)
    single = sum(pltpu.roll(single[:, x], x, 1) for x in range(GRID)).reshape(HEADS, 2, 512)
    quad = sum(pltpu.roll(quad[:, x], x, 1) for x in range(SUB)).reshape(HEADS, 4, 512)
    rest = jnp.zeros((HEADS, 512), F32)
    for i in range(2):
        y = 2 * me + i
        row = jnp.concatenate([single[:, i], rest], axis=1)
        out = out + pltpu.roll(row, (15 - y) * 32, 1)
    for i in range(4):
        y = lax.rem(me, 2) * 4 + i
        row = jnp.concatenate([quad[:, i], rest], axis=1)
        out = out + pltpu.roll(row, (15 - y) * 32, 1)
    return out


def backward_kernel(
    gain_ref,
    kind_ref,
    timek_ref,
    gbup_ref,
    gbdown_ref,
    dn2_hbm,
    fpart_hbm,
    cot_hbm,
    ffg_hbm,
    qkv_hbm,
    p_hbm,
    unit_hbm,
    inv_hbm,
    kept_hbm,
    second_hbm,
    u_hbm,
    g_hbm,
    wqkv_hbm,
    wout_hbm,
    wup_hbm,
    wdown_hbm,
    wtime_hbm,
    gtime_ref,
    gq_ref,
    gt_ref,
    go_ref,
    gup_ref,
    gdown_ref,
    ggain_ref,
    gshift_ref,
    gtable_ref,
    gbup_out,
    gbdown_out,
    dx_hbm,
    fsum_hbm,
    wqkv,
    wout,
    wup,
    wdown,
    qkv,
    p_ref,
    unit,
    inv,
    kept,
    second,
    u_ref,
    g_ref,
    total,
    part,
    recv,
    dy,
    dhl,
    dxl,
    do_ref,
    acc,
    dqkv,
    du_ref,
    ds_ref,
    x2,
    pair2,
    recv2,
    x3,
    pair3,
    recv3,
    stage,
    ninth,
    fold,
    dproj,
    pick_ref,
    small,
    small_out,
    small_recv,
    small_sum,
    small_pair,
    small_chip,
    load_sem,
    row_sem,
    hid_sems,
    dp_sems,
    chip_sems,
    free2,
    free3,
    small_sems,
    small_one,
):
    me = lax.axis_index("hid")
    own_first = me * OWN
    sums = HidSums(part, recv, total, tuple(hid_sems.at[n] for n in range(4)))
    ff_sum = SteppedSums(
        x2,
        pair2,
        recv2,
        (dp_sems.at[0], dp_sems.at[1], chip_sems.at[0], chip_sems.at[1]),
        free2,
    )
    at_sum = DirectSums(
        x3,
        pair3,
        recv3,
        (dp_sems.at[2], dp_sems.at[3], chip_sems.at[2], chip_sems.at[3]),
        free3,
    )

    def load(n, src, dst):
        return pltpu.make_async_copy(src, dst, load_sem.at[n])

    def load_dn2(r):
        return load(r, dn2_hbm.at[pl.ds(r * ROW_LEN, ROW_LEN)], total.at[4 + r])

    def load_cot():
        return load(2, cot_hbm, dxl)

    def load_out(l):
        return load(3, wout_hbm.at[l], wout)

    def load_qkv_weight(l):
        return load(4, wqkv_hbm.at[l], wqkv)

    def load_time_weight(l):
        return load(4, wtime_hbm.at[l], wqkv)

    def place_of(j):
        return 1 - j // 2, span(lax.rem(j, 2) * ROW_LEN, ROW_LEN, ROW_LEN)

    def load_p(j):
        return load(5, p_hbm.at[1 - j // 2, lax.rem(j, 2)], p_ref)

    def load_ffg():
        return load(6, ffg_hbm, x2)

    def load_kept():
        return load(7, kept_hbm, kept)

    def load_feed():
        return [
            load(8, second_hbm, second),
            load(9, u_hbm, u_ref),
            load(10, g_hbm, g_ref),
            load(11, wup_hbm.at[0], wup),
            load(12, wdown_hbm.at[0], wdown),
        ]

    def load_fpart():
        return load(13, fpart_hbm, part.at[pl.ds(2, 2)])

    def load_qkv(j):
        l, rows = place_of(j)
        return load(14, qkv_hbm.at[l, rows], qkv)

    def load_norm(which, j):
        l, rows = place_of(j)
        return [
            load(15 + 2 * which, unit_hbm.at[l, which, rows], unit.at[which]),
            load(16 + 2 * which, inv_hbm.at[l, which, rows], inv.at[which]),
        ]

    def save_dx(r):
        rows = span(r * ROW_LEN, ROW_LEN, ROW_LEN)
        return pltpu.make_async_copy(dy.at[rows], dx_hbm.at[rows], row_sem.at[r])

    def save_fsum(r):
        return pltpu.make_async_copy(total.at[2 + r], fsum_hbm.at[r], row_sem.at[2 + r])

    load_dn2(0).start()
    load_cot().start()
    for copy in load_norm(1, 0):
        copy.start()
    load_out(1).start()
    load_ffg().start()
    load_fpart().start()
    load_qkv(0).start()
    load_p(0).start()
    load_qkv_weight(1).start()
    for copy in load_norm(0, 0) + load_feed():
        copy.start()
    load_dn2(1).start()
    load_kept().start()
    barrier = pltpu.get_barrier_semaphore()
    greet_hid(barrier, me)
    pl.semaphore_signal(
        barrier, inc=1, device_id={"dp": ff_sum.partner}, device_id_type=MESH
    )
    for k in HID_ORDER:
        pl.semaphore_signal(barrier, inc=1, device_id=ff_sum.peer(k), device_id_type=MESH)
    small[...] = jnp.zeros_like(small)
    ninth[...] = jnp.zeros_like(ninth)
    gtime_ref[...] = jnp.zeros_like(gtime_ref)
    quarter = lax.broadcasted_iota(jnp.int32, (8, ROW_LEN), 1) // 64
    owner = lax.broadcasted_iota(jnp.int32, (8, ROW_LEN), 0)
    for r in range(2):
        whole = (owner == 4 * r).astype(F32) * kind_ref[r, 0:1]
        parts = (owner == 4 * r + quarter).astype(F32) * kind_ref[r, 1:2]
        pick_ref[:, pl.ds(r * ROW_LEN, ROW_LEN)] = (whole + parts).astype(BF16)
    pl.semaphore_wait(barrier, 15)
    load_ffg().wait()
    ff_sum.start()
    load_fpart().wait()
    sums.scatter(2)
    sums.scatter(3)
    load_cot().wait()

    def attention_results(l, block):
        for j in range(KEPT):
            for n in range(7):
                at = 8 * n + j if j < 8 else 56 + n
                ref = gq_ref if n < 3 else gt_ref if n < 6 else go_ref
                ref[j, l : l + 1, pl.ds(n % 3 * D, D)] = block[at : at + 1]

    def feed_results(l, block):
        gup_ref[l] = block[0:72, 0:UNITS]
        gdown_ref[l] = block[0:72, UNITS : 2 * UNITS]

    def place(p, grad):
        half = lax.rem(p, 2)
        for c in range(DP):
            stage[c, span(8 * half, 8, 8)] = grad[8 * c : 8 * c + 8]
            ninth[c, pl.ds(p, 1)] = grad[128 + c : 129 + c]

    def flush(pair):
        for c in range(DP):
            x3[c // 2, c % 2, span(16 * pair, 16, 16)] = stage[c].astype(BF16)

    def attention_weights(l):
        def project(n, _):
            cols = span(n * D, D, 128)
            dproj[l, :, cols] = dot(pick_ref[...], dqkv[:, cols])
            return 0

        lax.fori_loop(0, 3, project, 0)

        def token_piece(n, _):
            cols = span(n * D, D, 128)
            place(n, dot_tn(kept[l, 0, :, 0:144], dqkv[:, cols]))
            pl.when(n == 1)(lambda: flush(0))
            return 0

        lax.fori_loop(0, 3, token_piece, 0)

        def time_piece(n, _):
            cols = span(n * D, D, 128)
            place(3 + n, dot_tn(timek_ref[:, 0:144], dproj[l, :, cols].astype(BF16)))
            pl.when(n == 0)(lambda: flush(1))
            pl.when(n == 2)(lambda: flush(2))
            return 0

        lax.fori_loop(0, 3, time_piece, 0)
        place(6, dot_tn(kept[l, 1, :, 0:144], dhl[...]))
        for c in range(DP):
            stage[c, 8:16] = ninth[c]
        flush(3)
        small[span(l * 16, 16, 16), 0:1024] = fold_tables(fold, me)

    def time_gradient(l):
        load_time_weight(l).wait()
        got = jnp.zeros((8, D), F32)
        for n in range(3):
            cols = pl.ds(n * D, D)
            got = got + dot_nt(dproj[l, :, cols].astype(BF16), wqkv[:, cols])
        for r in range(2):
            gtime_ref[r] += got[4 * r : 4 * r + 4]

    def step(j, _):
        l = 1 - j // 2
        r = lax.rem(j, 2)
        base = r * ROW_LEN
        rows = span(base, ROW_LEN, ROW_LEN)
        slot = 4 * l + r
        more = j < 3

        for copy in load_norm(1, j):
            copy.wait()

        @pl.when(l == 1)
        def _():
            pl.when(r == 0)(lambda: load_dn2(0).wait())
            pl.when(r == 1)(lambda: load_dn2(1).wait())
            dy[rows] = dxl[rows].astype(F32)

        @pl.when(l == 0)
        def _():
            sums.wait(r)

        @pl.when(r == 0)
        def _():
            fold[...] = jnp.zeros_like(fold)

        def second_norm(c, _):
            here = span(c * CHUNK, CHUNK, CHUNK)
            rr = span(base + c * CHUNK, CHUNK, CHUNK)
            dn = total[slot, here].astype(F32)
            dh = dy[rr] + norm_slope(
                dn, unit[1, here].astype(F32), inv[1, here, 0:1], gain_ref[l, 1:2]
            )
            dy[rr] = dh
            dhl[rr] = dh.astype(BF16)
            return 0

        lax.fori_loop(0, ROW_LEN // CHUNK, second_norm, 0)
        mine = span(own_first, OWN, OWN)

        def norm_sums(which, dn):
            value = jnp.sum(dn * unit[which, mine].astype(F32), 0, keepdims=True)
            small[pl.ds(32 + 2 * l + which, 1)] += value
            small[pl.ds(36 + 2 * l + which, 1)] += jnp.sum(dn, 0, keepdims=True)

        norm_sums(1, total[slot, mine].astype(F32))

        @pl.when(more)
        def _():
            for copy in load_norm(1, j + 1):
                copy.start()

        @pl.when(r == 0)
        def _():
            load_out(1).wait()

        do_ref[...] = dot_nt(dhl[rows], wout[...]).astype(BF16)

        @pl.when(j == 1)
        def _():
            load_out(0).start()

        load_qkv(j).wait()
        load_p(j).wait()
        attend_backward(qkv, r, do_ref, p_ref, acc, ds_ref, fold, kind_ref, own_first)

        @pl.when(more)
        def _():
            load_p(j + 1).start()
            load_qkv(j + 1).start()

        @pl.when(j == 0)
        def _():
            ff_sum.exchange_y()

        @pl.when(j == 1)
        def _():
            sums.add_and_gather(0)

        @pl.when(j == 2)
        def _():
            at_sum.exchange()
            for e in range(2):
                sums.wait(2 + e)
                save_fsum(e).start()

        @pl.when(j == 3)
        def _():
            ff_sum.exchange_z()

        dqkv[rows, 0:D] = (acc[:, 0:D] * SCALE).astype(BF16)
        dqkv[rows, D : 2 * D] = (acc[:, D : 2 * D] * SCALE).astype(BF16)
        dqkv[rows, 2 * D :] = acc[:, 2 * D :].astype(BF16)

        @pl.when(j == 3)
        def _():
            attention_weights(0)
            attention_results(1, at_sum.finish())
            at_sum.release()
            at_sum.acquire()
            at_sum.start()

        @pl.when(r == 0)
        def _():
            load_qkv_weight(1).wait()

        def back(n, _):
            cols = span(n * D, D, 128)
            got = dot_nt(dqkv[rows, cols], wqkv[:, cols])

            @pl.when(n == 0)
            def _():
                acc[:, 0:D] = got

            @pl.when(n > 0)
            def _():
                acc[:, 0:D] += got

            return 0

        lax.fori_loop(0, 3, back, 0)

        @pl.when(r == 1)
        def _():
            load_time_weight(l).start()

        for copy in load_norm(0, j):
            copy.wait()

        def first_norm(c, _):
            here = span(c * CHUNK, CHUNK, CHUNK)
            rr = span(base + c * CHUNK, CHUNK, CHUNK)
            dn = acc[here, 0:D]
            dy[rr] = dy[rr] + norm_slope(
                dn, unit[0, here].astype(F32), inv[0, here, 0:1], gain_ref[l, 0:1]
            )
            return 0

        lax.fori_loop(0, ROW_LEN // CHUNK, first_norm, 0)
        norm_sums(0, acc[mine, 0:D])

        @pl.when(more)
        def _():
            for copy in load_norm(0, j + 1):
                copy.start()

        @pl.when(l == 0)
        def _():
            save_dx(r).start()

        @pl.when(l == 1)
        def _():
            @pl.when(r == 0)
            def _():
                for copy in load_feed():
                    copy.wait()

            dxl[rows] = dy[rows].astype(BF16)
            gh = dot_nt(dxl[rows], wdown[...])
            du = (gh * gelu_slope(u_ref[rows])).astype(BF16)
            du_ref[rows] = du
            part[r] = dot(du, wup[...]).astype(BF16)
            sums.scatter(r)
            small[40:41] += jnp.sum(
                dxl[span(base + own_first, OWN, OWN)].astype(F32), 0, keepdims=True
            )

        @pl.when(j == 0)
        def _():
            sums.add_and_gather(2)
            sums.add_and_gather(3)

        @pl.when(j == 1)
        def _():
            ff_sum.exchange_z()
            write_ff_grads(
                x2,
                lambda: dot_tn(second[...], du_ref[...]),
                lambda: dot_tn(dxl[...], g_ref[...]),
            )
            feed_results(1, ff_sum.finish())
            ff_sum.release()
            ff_sum.acquire()
            ff_sum.start()
            load_kept().wait()
            attention_weights(1)
            at_sum.start()
            ff_sum.exchange_y()
            sums.add_and_gather(1)
            time_gradient(1)
            load_qkv_weight(0).start()

        return 0

    lax.fori_loop(0, 4, step, 0)

    odd = lax.rem(me, 2).astype(F32)
    for l, value in enumerate(
        (jnp.sum(du_ref[...].astype(F32), 0, keepdims=True), gbup_ref[...])
    ):
        small[pl.ds(42 + 4 * l + me // 2, 1)] = jnp.concatenate(
            [value * (1.0 - odd), value * odd], axis=1
        )
    small[41:42] = gbdown_ref[...]

    def small_scatter(k):
        peer = hid_peer(me, k)
        return pltpu.make_async_remote_copy(
            src_ref=small.at[span(peer * 8, 8, 8)],
            dst_ref=small_recv.at[k - 1],
            send_sem=small_sems.at[0, k - 1],
            recv_sem=small_sems.at[1, k - 1],
            device_id={"hid": peer},
            device_id_type=MESH,
        )

    def small_swap():
        return pltpu.make_async_remote_copy(
            src_ref=small_sum.at[0],
            dst_ref=small_pair,
            send_sem=small_one.at[0],
            recv_sem=small_one.at[1],
            device_id={"dp": ff_sum.partner},
            device_id_type=MESH,
        )

    def small_spread(k, outgoing):
        chip = ff_sum.chip
        if not outgoing:
            chip = lax.rem(ff_sum.y + 4 - k // 2, 4) * 2 + lax.rem(ff_sum.z + k, 2)
        return pltpu.make_async_remote_copy(
            src_ref=small_chip.at[chip],
            dst_ref=small_chip.at[chip],
            send_sem=small_sems.at[2, k - 1],
            recv_sem=small_sems.at[3, k - 1],
            device_id=ff_sum.peer(k),
            device_id_type=MESH,
        )

    def small_gather(k, outgoing):
        owner = me if outgoing else hid_source(me, k)
        rows = small_out.at[span(owner * 8, 8, 8)]
        return pltpu.make_async_remote_copy(
            src_ref=rows,
            dst_ref=rows,
            send_sem=small_sems.at[4, k - 1],
            recv_sem=small_sems.at[5, k - 1],
            device_id={"hid": hid_peer(me, k)},
            device_id_type=MESH,
        )

    for k in HID_ORDER:
        small_scatter(k).start()
    at_sum.exchange()
    for k in HID_ORDER:
        small_scatter(k).wait_recv()
    value = small[span(me * 8, 8, 8)]
    for k in range(HID - 1):
        value = value + small_recv[k]
    small_sum[0] = value
    small_swap().start()
    feed_results(0, ff_sum.finish())
    small_swap().wait_recv()
    small_chip[ff_sum.chip] = small_sum[0] + small_pair[...]
    for k in HID_ORDER:
        small_spread(k, True).start()
    time_gradient(0)
    for k in HID_ORDER:
        small_spread(k, False).wait_recv()
    value = small_chip[0]
    for c in range(1, 8):
        value = value + small_chip[c]
    small_out[span(me * 8, 8, 8)] = value
    for k in HID_ORDER:
        small_gather(k, True).start()
    attention_results(0, at_sum.finish())
    for k in HID_ORDER:
        small_gather(k, False).wait_recv()
    for l in range(LAYERS):
        for a in range(REL):
            at = (REL - 1 - a) * 32
            gtable_ref[l, a] = small_out[16 * l : 16 * l + 16, at : at + REL]
        for n in range(2):
            ggain_ref[l, n : n + 1] = small_out[32 + 2 * l + n : 33 + 2 * l + n]
            gshift_ref[l, n : n + 1] = small_out[36 + 2 * l + n : 37 + 2 * l + n]
        for n in range(4):
            gbup_out[l : l + 1, n * D : (n + 1) * D] = small_out[42 + 4 * l + n : 43 + 4 * l + n]
        gbdown_out[l : l + 1] = small_out[40 + l : 41 + l]
    for k in HID_ORDER:
        small_scatter(k).wait_send()
        small_spread(k, True).wait_send()
        small_gather(k, True).wait_send()
    small_swap().wait_send()
    for r in range(2):
        save_dx(r).wait()
        save_fsum(r).wait()
    for e in range(4):
        sums.drain(e)


def backward(vmem_args, hbm_args):
    s = jax.ShapeDtypeStruct
    v = pltpu.VMEM
    dma = pltpu.SemaphoreType.DMA
    return pl.pallas_call(
        backward_kernel,
        out_shape=[
            s((2, SLOTS, D), F32),
            s((KEPT, LAYERS, 3 * D), F32),
            s((KEPT, LAYERS, 3 * D), F32),
            s((KEPT, LAYERS, D), F32),
            s((LAYERS, 72, UNITS), F32),
            s((LAYERS, 72, UNITS), F32),
            s((LAYERS, 2, D), F32),
            s((LAYERS, 2, D), F32),
            s((LAYERS, REL, HEADS, REL), F32),
            s((LAYERS, FF), F32),
            s((LAYERS, D), F32),
            s((TOKENS, D), F32),
            s((2, ROW_LEN, D), BF16),
        ],
        in_specs=[IN_VMEM] * len(vmem_args) + [IN_ANY] * len(hbm_args),
        out_specs=[IN_VMEM] * 11 + [IN_ANY] * 2,
        scratch_shapes=[
            v((D, 3 * D), BF16),
            v((D, D), BF16),
            v((UNITS, D), BF16),
            v((UNITS, D), BF16),
            v((ROW_LEN, 3 * D), BF16),
            v((HEADS, ROW_LEN, ROW_LEN), BF16),
            v((2, ROW_LEN, D), BF16),
            v((2, ROW_LEN, 128), F32),
            v((LAYERS, 2, TOKENS, 256), BF16),
            v((TOKENS, D), BF16),
            v((TOKENS, UNITS), F32),
            v((TOKENS, UNITS), BF16),
            v((6, ROW_LEN, D), BF16),
            v((4, ROW_LEN, D), BF16),
            v((4, HID - 1, SLICE, D), BF16),
            v((TOKENS, D), F32),
            v((TOKENS, D), BF16),
            v((TOKENS, D), BF16),
            v((ROW_LEN, D), BF16),
            v((ROW_LEN, 3 * D), F32),
            v((TOKENS, 3 * D), BF16),
            v((TOKENS, UNITS), BF16),
            v((2, ROW_LEN, ROW_LEN), F32),
            v((8, 2, 80, D), BF16),
            v((8, 80, D), BF16),
            v((7, 80, D), BF16),
            v((8, 2, 64, D), BF16),
            v((8, 64, D), BF16),
            v((7, 64, D), BF16),
            v((DP, 16, D), F32),
            v((DP, 8, D), F32),
            v((2, HEADS, OWN, ROW_LEN), F32),
            v((LAYERS, 8, 3 * D), F32),
            v((8, TOKENS), BF16),
            v((64, D), F32),
            v((64, D), F32),
            v((7, 8, D), F32),
            v((1, 8, D), F32),
            v((8, D), F32),
            v((8, 8, D), F32),
            dma((19,)),
            dma((4,)),
            dma((4, 4, HID - 1)),
            dma((4,)),
            dma((4, 7)),
            pltpu.SemaphoreType.REGULAR,
            pltpu.SemaphoreType.REGULAR,
            dma((6, HID - 1)),
            dma((2,)),
        ],
        compiler_params=pltpu.CompilerParams(
            collective_id=2, has_side_effects=True, vmem_limit_bytes=VMEM_LIMIT
        ),
        name="backward",
    )(*vmem_args, *hbm_args)


def shards(
    block_in,
    time_tokens,
    layout,
    norm_gain,
    norm_bias,
    w_qkv,
    w_time,
    rel_table,
    w_out,
    w_up,
    b_up,
    w_down,
    b_down,
    cotangent,
):
    time_flat = time_tokens.reshape(8, D)
    cot = cotangent.reshape(TOKENS, D)
    wup_turned = jnp.swapaxes(w_up, 1, 2)
    bias, tp, kind = prepare(layout, rel_table, time_flat, w_time)
    gbup, gbdown, timek, h, fpart, dn2, ffg, qkv, p, unit, inv, kept, second, u, g = forward(
        block_in.reshape(TOKENS, D),
        cot,
        tp,
        norm_gain,
        norm_bias,
        b_up,
        b_down,
        time_flat,
        w_qkv,
        w_out,
        wup_turned,
        w_down,
        bias,
    )
    (
        gtime,
        gq,
        gt,
        go,
        gup,
        gdown,
        ggain,
        gshift,
        gtable,
        gbup_all,
        gbdown_all,
        dx,
        fsum,
    ) = backward(
        (norm_gain, kind, timek, gbup, gbdown),
        (
            dn2,
            fpart,
            cot,
            ffg,
            qkv,
            p,
            unit,
            inv,
            kept,
            second,
            u,
            g,
            w_qkv,
            w_out,
            wup_turned,
            w_down,
            w_time,
        ),
    )
    block_out = h.reshape(2, ROW_LEN, D) + (fsum.astype(F32) + b_down[1])
    return (
        block_out,
        dx.reshape(2, ROW_LEN, D),
        gtime,
        ggain,
        gshift,
        jnp.swapaxes(gq, 0, 1),
        jnp.swapaxes(gt, 0, 1),
        jnp.swapaxes(gtable, 1, 2),
        jnp.swapaxes(go, 0, 1),
        gup,
        gbup_all,
        jnp.swapaxes(gdown, 1, 2),
        gbdown_all,
    )


def solution(mesh):
    in_specs = (
        P("dp", None, None),
        P("dp", None, None),
        P("dp"),
        P(),
        P(),
        P(),
        P(),
        P(),
        P(),
        P(None, None, "hid"),
        P(None, "hid"),
        P(None, "hid", None),
        P(),
        P("dp", None, None),
    )
    out_specs = (
        P("dp", None, None),
        P("dp", None, None),
        P("dp", None, None),
        P(),
        P(),
        P(None, ("dp", "hid"), None),
        P(None, ("dp", "hid"), None),
        P(),
        P(None, ("dp", "hid"), None),
        P(None, "dp", "hid"),
        P(),
        P(None, "hid", "dp"),
        P(),
    )
    return jax.shard_map(shards, mesh=mesh, in_specs=in_specs, out_specs=out_specs, check_vma=False)
```

```python
import functools

import jax
import jax.numpy as jnp
from jax import lax
from jax.experimental import pallas as pl
from jax.experimental.pallas import tpu as pltpu
from jax.sharding import PartitionSpec as P

D = 1152
HEADS = 16
HEAD_DIM = 72
FF = 4608
LAYERS = 2
GRID = 16
SUB = 8
ROW_LEN = 256
SLOTS = 4
REL = 31
DP = 16
HID = 8
UNITS = FF // HID
KEPT = D // (DP * HID)
TOKENS = 512
OWN = ROW_LEN // HID
SCALE = HEAD_DIM ** (-0.5)
MASKED_LOGIT = -1e30
NORM_EPSILON = 1e-06
F32 = jnp.float32
BF16 = jnp.bfloat16
MESH = pl.DeviceIdType.MESH
VMEM_LIMIT = 63 * 1024 * 1024
HIGHEST = lax.Precision.HIGHEST


def contract(a, b, da, db, precision=None):
    return lax.dot_general(
        a, b, (((da,), (db,)), ((), ())), preferred_element_type=F32, precision=precision
    )


def dot(a, b):
    return contract(a, b, 1, 0)


def dot_nt(a, b):
    return contract(a, b, 1, 1)


def dot_tn(a, b):
    return contract(a, b, 0, 0)


def span(start, size, multiple):
    return pl.ds(pl.multiple_of(start, multiple), size)


def gelu_parts(v):
    c = 0.7978845608028654
    square = v * v
    t = jnp.tanh(c * v * (1.0 + 0.044715 * square))
    return t, square


def gelu(v):
    t, _ = gelu_parts(v)
    return 0.5 * v * (1.0 + t)


def gelu_slope(v):
    c = 0.7978845608028654
    t, square = gelu_parts(v)
    return 0.5 * (1.0 + t) + 0.5 * v * (1.0 - t * t) * (c * (1.0 + 3.0 * 0.044715 * square))


def prepare_kernel(
    layout_ref, rel_ref, time_ref, wtime_ref, bias_ref, tp_ref, kind_ref, rows_ref, skew_ref, turned_ref
):
    g = pl.program_id(1)
    first, second = layout_ref[0], layout_ref[1]

    @pl.when(g == 0)
    def _():
        tp_ref[...] = jnp.zeros_like(tp_ref)
        for r in range(2):
            four = jnp.where(layout_ref[r] == 1, 1.0, 0.0)
            kind_ref[r, 0:1] = jnp.full((1, ROW_LEN), 1.0 - four, F32)
            kind_ref[r, 1:2] = jnp.full((1, ROW_LEN), four, F32)

    @pl.when(g < 3)
    def _():
        cols = span(384 * g, 384, 128)
        tokens = [time_ref[r, :, cols].astype(F32) for r in range(2)]
        tp_ref[0] += dot(jnp.concatenate(tokens, axis=0).astype(BF16), wtime_ref[0])

    @pl.when(g == 3)
    def _():
        for r in range(2):

            @pl.when(layout_ref[r] != 1)
            def _():
                tp_ref[0, 4 * r : 4 * r + 4] = jnp.broadcast_to(
                    tp_ref[0, 4 * r : 4 * r + 1], (SLOTS, 3 * D)
                )

    rows_ref[...] = jnp.zeros_like(rows_ref)
    rows_ref[:, 0:4, 0:REL] = rel_ref[0, :, pl.ds(4 * g, 4), :]
    table = rows_ref[:, 0]
    for i in range(1, 4):
        table = table + pltpu.roll(rows_ref[:, i], 32 * i, 1)

    def skewed(side, count, top):
        skew_ref[...] = jnp.zeros_like(skew_ref)
        for j in range(count):
            block = jnp.broadcast_to(table[top - j : top - j + 1], (side, 128))
            skew_ref[pl.ds(side * j, side)] = pltpu.roll(
                block, 113, 1, stride=1, stride_axis=0
            )

    def single(r):
        skewed(GRID, REL, REL - 1)
        turned_ref[...] = skew_ref[...].T
        for i in range(4):
            w = turned_ref[32 * i : 32 * i + GRID]
            for m in range(8):
                moved = w if m == 0 else pltpu.roll(w, 512 - 16 * m, 1)
                for t in range(2):
                    y = 15 - 8 * t - m
                    bias_ref[0, r, i, pl.ds(GRID * y, GRID), :] = moved[
                        :, 128 * t : 128 * t + ROW_LEN
                    ].astype(BF16)

    def quad(r):
        skewed(SUB, 15, 22)
        turned_ref[:, 0:128] = skew_ref[0:128].T
        half = lax.broadcasted_iota(jnp.int32, (2 * SUB, 128), 1) // 64
        closed = jnp.full((2 * SUB, 128), MASKED_LOGIT, F32).astype(BF16)
        for i in range(4):
            w = turned_ref[32 * i : 32 * i + SUB, 0:128]
            for y in range(0, SUB, 2):
                for odd in range(2):
                    moved = jnp.concatenate(
                        [
                            pltpu.roll(w, (128 + 64 * odd - (7 - y - n) * SUB) % 128, 1)
                            for n in range(2)
                        ],
                        axis=0,
                    )
                    moved = jnp.where(half == odd, moved, MASKED_LOGIT).astype(BF16)
                    for tile in range(2):
                        rows = pl.ds(64 * (2 * tile + odd) + SUB * y, 2 * SUB)
                        bias_ref[0, r, i, rows, 128 * tile : 128 * tile + 128] = moved
                        bias_ref[0, r, i, rows, 128 - 128 * tile : 256 - 128 * tile] = closed

    pl.when(first != 1)(lambda: single(0))
    pl.when(first == 1)(lambda: quad(0))

    @pl.when(first == second)
    def _():
        for i in range(4):
            bias_ref[0, 1, i] = bias_ref[0, 0, i]

    pl.when((first != second) & (second != 1))(lambda: single(1))
    pl.when((first != second) & (second == 1))(lambda: quad(1))


def prepare(layout, rel_table, time_tokens, w_time):
    return pl.pallas_call(
        prepare_kernel,
        out_shape=[
            jax.ShapeDtypeStruct((LAYERS, 2, HEADS, ROW_LEN, ROW_LEN), BF16),
            jax.ShapeDtypeStruct((LAYERS, 8, 3 * D), F32),
            jax.ShapeDtypeStruct((2, 2, ROW_LEN), F32),
        ],
        grid_spec=pltpu.PrefetchScalarGridSpec(
            num_scalar_prefetch=1,
            grid=(LAYERS, 4),
            in_specs=[
                pl.BlockSpec((1, REL, HEADS, REL), lambda l, g, _: (l, 0, 0, 0)),
                pl.BlockSpec((2, SLOTS, D), lambda l, g, _: (0, 0, 0)),
                pl.BlockSpec((1, 384, 3 * D), lambda l, g, _: (l, jnp.minimum(g, 2), 0)),
            ],
            out_specs=[
                pl.BlockSpec((1, 2, 4, ROW_LEN, ROW_LEN), lambda l, g, _: (l, 0, g, 0, 0)),
                pl.BlockSpec((1, 8, 3 * D), lambda l, g, _: (l, 0, 0)),
                pl.BlockSpec((2, 2, ROW_LEN), lambda l, g, _: (0, 0, 0)),
            ],
            scratch_shapes=[
                pltpu.VMEM((REL, 8, 128), F32),
                pltpu.VMEM((512, 128), F32),
                pltpu.VMEM((128, 512), F32),
            ],
        ),
        compiler_params=pltpu.CompilerParams(vmem_limit_bytes=VMEM_LIMIT),
        name="prepare",
    )(layout, jnp.swapaxes(rel_table, 1, 2), time_tokens, w_time)


IN_VMEM = pl.BlockSpec(memory_space=pltpu.VMEM)
IN_ANY = pl.BlockSpec(memory_space=pl.ANY)
CHUNK = 128
HID_ORDER = (2, 6, 1, 4, 3, 7, 5)
SLICE = ROW_LEN // HID


def head_window(h):
    start = h * HEAD_DIM // 128 * 128
    offset = h * HEAD_DIM - start
    width = 128 if offset + HEAD_DIM <= 128 else 256
    lane = lax.broadcasted_iota(jnp.int32, (1, width), 1)
    mask = ((lane >= offset) & (lane < offset + HEAD_DIM)).astype(F32).astype(BF16)
    return start, width, mask


def hid_peer(me, k):
    return lax.rem(me // 2 + k // 2, 4) * 2 + lax.rem(me + k, 2)


def hid_source(me, k):
    return lax.rem(me // 2 + 4 - k // 2, 4) * 2 + lax.rem(me + k, 2)


def greet_hid(barrier, me):
    for k in HID_ORDER:
        pl.semaphore_signal(
            barrier, inc=1, device_id={"hid": hid_peer(me, k)}, device_id_type=MESH
        )


class HidSums:
    def __init__(self, part, recv, total, sems):
        self.part, self.recv, self.total = part, recv, total
        self.send1, self.recv1, self.send2, self.recv2 = sems
        self.me = lax.axis_index("hid")

    def scatter_copy(self, e, k):
        peer = hid_peer(self.me, k)
        return pltpu.make_async_remote_copy(
            src_ref=self.part.at[e, span(peer * SLICE, SLICE, SLICE)],
            dst_ref=self.recv.at[e, k - 1],
            send_sem=self.send1.at[e, k - 1],
            recv_sem=self.recv1.at[e, k - 1],
            device_id={"hid": peer},
            device_id_type=MESH,
        )

    def gather_copy(self, slot, e, k, outgoing):
        owner = self.me if outgoing else hid_source(self.me, k)
        rows = self.total.at[slot, span(owner * SLICE, SLICE, SLICE)]
        return pltpu.make_async_remote_copy(
            src_ref=rows,
            dst_ref=rows,
            send_sem=self.send2.at[e, k - 1],
            recv_sem=self.recv2.at[e, k - 1],
            device_id={"hid": hid_peer(self.me, k)},
            device_id_type=MESH,
        )

    def scatter(self, e):
        for k in HID_ORDER:
            self.scatter_copy(e, k).start()

    def add_and_gather(self, e):
        mine = span(self.me * SLICE, SLICE, SLICE)
        for k in HID_ORDER:
            self.scatter_copy(e, k).wait_recv()
        total = self.part[e, mine].astype(F32)
        for k in range(HID - 1):
            total = total + self.recv[e, k].astype(F32)
        self.total[e, mine] = total.astype(BF16)
        for k in HID_ORDER:
            self.gather_copy(e, e, k, True).start()

    def wait(self, e):
        for k in HID_ORDER:
            self.gather_copy(e, e, k, False).wait_recv()

    def drain(self, e):
        for k in HID_ORDER:
            self.scatter_copy(e, k).wait_send()
            self.gather_copy(e, e, k, True).wait_send()


def write_ff_grads(ffg, up_of, down_of):
    for n, of in enumerate((up_of, down_of)):
        for a, b in ((0, 128), (128, 256), (256, 384), (384, 512), (512, UNITS)):
            grad = of(a, b)
            for c in range(DP):
                ffg[c // 2, c % 2, 0:72, n * UNITS + a : n * UNITS + b] = grad[
                    72 * c : 72 * (c + 1)
                ].astype(BF16)


def layer_norm_rows(x, gain, shift):
    centre = x - jnp.mean(x, -1, keepdims=True)
    inverse = lax.rsqrt(jnp.mean(centre * centre, -1, keepdims=True) + NORM_EPSILON)
    unit = centre * inverse
    return (unit * gain + shift).astype(BF16), unit.astype(BF16), inverse


def kept_matrix():
    feature = lax.broadcasted_iota(jnp.int32, (D, 256), 0)
    column = lax.broadcasted_iota(jnp.int32, (D, 256), 1)
    low = column < 128
    owner = jnp.where(low, column // 8, column - 128)
    inner = jnp.where(low, column % 8, 8)
    chosen = (feature == owner * 72 + lax.axis_index("hid") * KEPT + inner) & (column < 144)
    return chosen.astype(F32).astype(BF16)


def attend_forward(qkv, bias_ref, p_ref, o_acc):
    o_acc[:, 0:D] = jnp.zeros((ROW_LEN, D), F32)

    def scores(h):
        start, width, mask = head_window(h)
        q = qkv[:, start : start + width] * mask
        return dot_nt(q, qkv[:, D + start : D + start + width])

    def mix(h, score):
        start, width, mask = head_window(h)
        logits = score * SCALE + bias_ref[h].astype(F32)
        expo = jnp.exp(logits - jnp.max(logits, -1, keepdims=True))
        p = (expo * (1.0 / jnp.sum(expo, -1, keepdims=True))).astype(BF16)
        p_ref[h] = p
        v = qkv[:, 2 * D + start : 2 * D + start + width] * mask
        o_acc[:, start : start + width] += dot(p, v)

    ready = {}
    for h in range(HEADS + 1):
        if h < HEADS:
            ready[h] = scores(h)
        if h:
            mix(h - 1, ready.pop(h - 1))


class DpSums:
    def __init__(self, x, pair, recv, sems, free):
        self.x, self.pair, self.recv, self.free = x, pair, recv, free
        self.pair_send, self.pair_recv, self.send, self.got = sems
        me = lax.axis_index("dp")
        self.y, self.z, self.core = me // 4, lax.rem(me // 2, 2), lax.rem(me, 2)
        self.chip = me // 2
        self.partner = self.chip * 2 + (1 - self.core)

    def other(self, k):
        return lax.rem(self.y + k // 2, 4) * 2 + lax.rem(self.z + k, 2)

    def peer(self, k):
        return {"dp": self.other(k) * 2 + self.core}

    def pair_copy(self):
        return pltpu.make_async_remote_copy(
            src_ref=self.x.at[:, 1 - self.core],
            dst_ref=self.pair,
            send_sem=self.pair_send,
            recv_sem=self.pair_recv,
            device_id={"dp": self.partner},
            device_id_type=MESH,
        )

    def start(self):
        self.pair_copy().start()

    def add_pair(self, c):
        both = self.x[c, self.core].astype(F32) + self.pair[c].astype(F32)
        self.pair[c] = both.astype(BF16)

    def release(self):
        pl.semaphore_signal(
            self.free, inc=1, device_id={"dp": self.partner}, device_id_type=MESH
        )
        for k in HID_ORDER:
            pl.semaphore_signal(self.free, inc=1, device_id=self.peer(k), device_id_type=MESH)

    def acquire(self):
        pl.semaphore_wait(self.free, 8)


class DirectSums(DpSums):
    def chip_copy(self, k):
        return pltpu.make_async_remote_copy(
            src_ref=self.pair.at[self.other(k)],
            dst_ref=self.recv.at[k - 1],
            send_sem=self.send.at[k - 1],
            recv_sem=self.got.at[k - 1],
            device_id=self.peer(k),
            device_id_type=MESH,
        )

    def exchange(self):
        self.pair_copy().wait_recv()
        for k in HID_ORDER + (0,):
            self.add_pair(self.other(k))
            if k:
                self.chip_copy(k).start()
        self.pair_copy().wait_send()

    def finish(self):
        total = self.pair[self.chip].astype(F32)
        for k in HID_ORDER:
            self.chip_copy(k).wait_recv()
            total = total + self.recv[k - 1].astype(F32)
        for k in HID_ORDER:
            self.chip_copy(k).wait_send()
        return total


class SteppedSums(DpSums):
    def y_copy(self, k):
        target = lax.rem(self.y + k, 4)
        return pltpu.make_async_remote_copy(
            src_ref=self.pair.at[pl.ds(2 * target, 2)],
            dst_ref=self.recv.at[pl.ds(2 * k - 2, 2)],
            send_sem=self.send.at[k - 1],
            recv_sem=self.got.at[k - 1],
            device_id=self.peer(2 * k),
            device_id_type=MESH,
        )

    def z_copy(self):
        return pltpu.make_async_remote_copy(
            src_ref=self.pair.at[2 * self.y + 1 - self.z],
            dst_ref=self.recv.at[6],
            send_sem=self.send.at[3],
            recv_sem=self.got.at[3],
            device_id=self.peer(1),
            device_id_type=MESH,
        )

    def exchange_y(self):
        self.pair_copy().wait_recv()
        for k in (2, 1, 3, 0):
            target = lax.rem(self.y + k, 4)
            for z in range(2):
                self.add_pair(2 * target + z)
            if k:
                self.y_copy(k).start()
        self.pair_copy().wait_send()

    def exchange_z(self):
        for k in (1, 3, 2):
            self.y_copy(k).wait_recv()
        for own in (False, True):
            z = self.z if own else 1 - self.z
            c = 2 * self.y + z
            block = self.pair[c].astype(F32)
            for k in (1, 2, 3):
                block = block + self.recv[2 * k - 2 + z].astype(F32)
            self.pair[c] = block.astype(BF16)
            if not own:
                self.z_copy().start()

    def finish(self):
        self.z_copy().wait_recv()
        total = self.pair[self.chip].astype(F32) + self.recv[6].astype(F32)
        for k in (1, 2, 3):
            self.y_copy(k).wait_send()
        self.z_copy().wait_send()
        return total


def norm_slope(dn, unit, inverse, gain):
    scaled = dn * gain
    return inverse * (
        scaled
        - jnp.mean(scaled, -1, keepdims=True)
        - unit * jnp.mean(scaled * unit, -1, keepdims=True)
    )


def attend_backward(qkv, r, do_ref, p_ref, acc, ds_ref, fold, kind_ref, own_first):
    acc[...] = jnp.zeros_like(acc)

    def slopes(h):
        start, width, mask = head_window(h)
        v = qkv[:, 2 * D + start : 2 * D + start + width] * mask
        return dot_nt(do_ref[:, start : start + width], v)

    def spread(h, dp):
        start, width, mask = head_window(h)
        p_low = p_ref[h]
        p = p_low.astype(F32)
        t = p * dp
        ds = t - p * jnp.sum(t, -1, keepdims=True)
        ds_ref[...] = ds
        low = ds.astype(BF16)
        k = qkv[:, D + start : D + start + width] * mask
        q = qkv[:, start : start + width] * mask
        do = do_ref[:, start : start + width] * mask
        acc[:, start : start + width] += dot(low, k)
        acc[:, D + start : D + start + width] += dot_tn(low, q)
        acc[:, 2 * D + start : 2 * D + start + width] += dot_tn(p_low, do)
        mine = ds_ref[span(own_first, OWN, OWN)]
        fold[0, h] += mine * kind_ref[r, 0:1]
        fold[1, h] += mine * kind_ref[r, 1:2]

    ready = {}
    depth = 2
    for h in range(HEADS + depth):
        if h < HEADS:
            ready[h] = slopes(h)
        if h >= depth:
            spread(h - depth, ready.pop(h - depth))


def two_part_dot(a, b):
    high = a.astype(BF16)
    low = (a - high.astype(F32)).astype(BF16)
    return dot(high, b) + dot(low, b)


def fold_tables(fold, me):
    lane = lax.broadcasted_iota(jnp.int32, (ROW_LEN, 512), 0)
    place = lax.broadcasted_iota(jnp.int32, (ROW_LEN, 512), 1)
    wide = (place == (lane // GRID) * 32 + 15 - lane % GRID).astype(F32).astype(BF16)
    inner = lane % (SUB * SUB)
    narrow = (place == (inner // SUB) * 32 + 15 - inner % SUB).astype(F32).astype(BF16)
    rest = jnp.zeros((HEADS, 512), F32)
    out = jnp.zeros((HEADS, 1024), F32)
    for kind, (side, chosen) in enumerate(((GRID, wide), (SUB, narrow))):
        lines = []
        for n in range(2):
            sums = fold[kind, 8 * n : 8 * (n + 1)].reshape(8 * OWN, ROW_LEN)
            wider = two_part_dot(sums, chosen).reshape(8 * OWN // side, side, 512)
            line = wider[:, 0]
            for x in range(1, side):
                line = line + pltpu.roll(wider[:, x], x, 1)
            lines.append(line.reshape(8, OWN // side, 512))
        for i in range(OWN // side):
            line = jnp.concatenate([part[:, i] for part in lines], axis=0)
            y = 2 * me + i if side == GRID else lax.rem(me, 2) * 4 + i
            out = out + pltpu.roll(
                jnp.concatenate([line, rest], axis=1), (15 - y) * 32, 1
            )
    return out


def layers_kernel(
    gain_ref,
    shift_ref,
    bup_ref,
    bdown_ref,
    tp_ref,
    kind_ref,
    time_ref,
    x_hbm,
    cot_hbm,
    wqkv_hbm,
    wout_hbm,
    wup_hbm,
    wdown_hbm,
    wtime_hbm,
    bias_hbm,
    gtime_ref,
    gq_ref,
    gt_ref,
    go_ref,
    gup_ref,
    gdown_ref,
    ggain_ref,
    gshift_ref,
    gtable_ref,
    gbup_out,
    gbdown_out,
    dx_hbm,
    h_hbm,
    fsum_hbm,
    qkv_hbm,
    p_hbm,
    unit_hbm,
    inv_hbm,
    second_hbm,
    u_hbm,
    g_hbm,
    wqkv,
    wout,
    wup,
    wdown,
    bias_ref,
    p_ref,
    qkv,
    unit,
    inv,
    keep_ref,
    kept,
    second,
    u_ref,
    g_ref,
    total,
    part,
    recv,
    dy,
    dhl,
    dxl,
    do_ref,
    acc,
    dqkv,
    du_ref,
    ds_ref,
    x2,
    pair2,
    recv2,
    pair3,
    recv3,
    fold,
    dproj,
    pick_ref,
    timek_ref,
    small,
    small_out,
    small_recv,
    small_sum,
    small_pair,
    small_chip,
    load_sem,
    save_sem,
    hid_sems,
    dp_sems,
    chip_sems,
    free2,
    free3,
    small_sems,
    small_one,
):
    me = lax.axis_index("hid")
    own_first = me * OWN
    mine = span(own_first, OWN, OWN)
    sums = HidSums(part, recv, total, tuple(hid_sems.at[n] for n in range(4)))
    ff_sum = SteppedSums(
        x2,
        pair2,
        recv2,
        (dp_sems.at[0], dp_sems.at[1], chip_sems.at[0], chip_sems.at[1]),
        free2,
    )
    at_sum = DirectSums(
        x2.at[:, :, pl.ds(0, 64)],
        pair3,
        recv3,
        (dp_sems.at[2], dp_sems.at[3], chip_sems.at[2], chip_sems.at[3]),
        free3,
    )

    def load(n, src, dst):
        return pltpu.make_async_copy(src, dst, load_sem.at[n])

    def save(n, src, dst):
        return pltpu.make_async_copy(src, dst, save_sem.at[n])

    def load_weight(l, n):
        cols = pl.ds(n * D, D)
        return load(n, wqkv_hbm.at[l, :, cols], wqkv.at[:, cols])

    def load_time_weight(l):
        return load(3, wtime_hbm.at[l], wqkv)

    def load_out(l):
        return load(4, wout_hbm.at[l], wout)

    def load_feed_weights(l):
        return [load(5, wup_hbm.at[l], wup), load(6, wdown_hbm.at[l], wdown)]

    def load_bias(i):
        return load(7, bias_hbm.at[i // 2, lax.rem(i, 2)], bias_ref)

    def load_x():
        return load(8, x_hbm, dhl)

    def load_cot():
        return load(9, cot_hbm, dxl)

    def place_of(j):
        return 1 - j // 2, span(lax.rem(j, 2) * ROW_LEN, ROW_LEN, ROW_LEN)

    def load_p(j):
        return load(10, p_hbm.at[1 - j // 2, lax.rem(j, 2)], p_ref)

    def load_qkv(j):
        l, rows = place_of(j)
        return load(11, qkv_hbm.at[l, rows], qkv)

    def load_norm(which, j):
        l, rows = place_of(j)
        return [
            load(12 + 2 * which, unit_hbm.at[l, which, rows], unit.at[which]),
            load(13 + 2 * which, inv_hbm.at[l, which, rows], inv.at[which]),
        ]

    def load_u(r):
        return load(16, u_hbm.at[span(r * ROW_LEN, ROW_LEN, ROW_LEN)], u_ref)

    def load_feed():
        return [load(17, second_hbm, second), load(18, g_hbm, g_ref)]

    def save_qkv(l, rows):
        return save(0, qkv, qkv_hbm.at[l, rows])

    def save_p(l, r):
        return save(1, p_ref, p_hbm.at[l, r])

    def save_norm(which, l, rows):
        return [
            save(2 + 2 * which, unit.at[which], unit_hbm.at[l, which, rows]),
            save(3 + 2 * which, inv.at[which], inv_hbm.at[l, which, rows]),
        ]

    def save_u(r, rows):
        return save(10 + r, u_ref, u_hbm.at[rows])

    def save_feed(r, rows):
        return [
            save(6 + r, second.at[rows], second_hbm.at[rows]),
            save(8 + r, g_ref.at[rows], g_hbm.at[rows]),
        ]

    def save_h(r, rows):
        return save(12 + r, dy.at[rows], h_hbm.at[rows])

    def save_dx(r, rows):
        return save(14 + r, dy.at[rows], dx_hbm.at[rows])

    def save_fsum(r):
        return save(16 + r, total.at[2 + r], fsum_hbm.at[r])

    load_x().start()
    for n in range(3):
        load_weight(0, n).start()
    load_bias(0).start()
    load_out(0).start()
    for copy in load_feed_weights(0):
        copy.start()
    load_cot().start()
    barrier = pltpu.get_barrier_semaphore()
    greet_hid(barrier, me)
    pl.semaphore_signal(
        barrier, inc=1, device_id={"dp": ff_sum.partner}, device_id_type=MESH
    )
    for k in HID_ORDER:
        pl.semaphore_signal(barrier, inc=1, device_id=ff_sum.peer(k), device_id_type=MESH)
    small[...] = jnp.zeros_like(small)
    gtime_ref[...] = jnp.zeros_like(gtime_ref)
    keep_ref[...] = kept_matrix()
    tokens = [time_ref[r].astype(F32) for r in range(2)]
    timek_ref[...] = dot(
        jnp.concatenate(tokens, axis=0).astype(BF16), keep_ref[...]
    ).astype(BF16)
    quarter = lax.broadcasted_iota(jnp.int32, (8, ROW_LEN), 1) // 64
    owner = lax.broadcasted_iota(jnp.int32, (8, ROW_LEN), 0)
    for r in range(2):
        whole = (owner == 4 * r).astype(F32) * kind_ref[r, 0:1]
        parts = (owner == 4 * r + quarter).astype(F32) * kind_ref[r, 1:2]
        pick_ref[:, pl.ds(r * ROW_LEN, ROW_LEN)] = (whole + parts).astype(BF16)
    load_x().wait()
    pl.semaphore_wait(barrier, 15)

    def keep_features(l):
        for n in range(2):
            kept[l, n] = dot(dqkv[:, n * D : (n + 1) * D], keep_ref[...]).astype(BF16)

    def forward_step(i, _):
        l = i // 2
        r = lax.rem(i, 2)
        base = r * ROW_LEN
        rows = span(base, ROW_LEN, ROW_LEN)

        @pl.when(i > 0)
        def _():
            for which in range(2):
                for copy in save_norm(which, 0, rows):
                    copy.wait()
            save_qkv(0, rows).wait()

        @pl.when(l == 0)
        def _():
            dy[rows] = dhl[rows].astype(F32)

        @pl.when(l == 1)
        def _():
            pl.when(r == 0)(lambda: keep_features(0))
            for copy in save_feed(r, rows):
                copy.wait()
            sums.wait(r)
            dy[rows] = dy[rows] + (total[r].astype(F32) + bdown_ref[0:1])

        def norm(which):
            def body(c, _):
                here = span(c * CHUNK, CHUNK, CHUNK)
                rr = span(base + c * CHUNK, CHUNK, CHUNK)
                low, value, inverse = layer_norm_rows(
                    dy[rr], gain_ref[l, which : which + 1], shift_ref[l, which : which + 1]
                )
                if which == 0:
                    dqkv[rr, 0:D] = low
                else:
                    second[rr] = low
                unit[which, here] = value
                inv[which, here] = jnp.broadcast_to(inverse, (CHUNK, 128))
                return 0

            lax.fori_loop(0, ROW_LEN // CHUNK, body, 0)
            for copy in save_norm(which, l, rows):
                copy.start()

        norm(0)
        for n in range(3):

            @pl.when(r == 0)
            def _():
                load_weight(l, n).wait()

            cols = pl.ds(n * D, D)
            wide = dot(dqkv[rows, 0:D], wqkv[:, cols])
            for s in range(SLOTS):
                qkv[64 * s : 64 * (s + 1), cols] = (
                    wide[64 * s : 64 * (s + 1)] + tp_ref[l, pl.ds(4 * r + s, 1), cols]
                ).astype(BF16)

        @pl.when(i == 2)
        def _():
            sums.add_and_gather(1)

        save_qkv(l, rows).start()

        @pl.when(i == 1)
        def _():
            for n in range(3):
                load_weight(1, n).start()

        load_bias(i).wait()

        @pl.when(i > 0)
        def _():
            save_p(0, 0).wait()

        attend_forward(qkv, bias_ref, p_ref, acc)

        @pl.when((i == 1) | (i == 3))
        def _():
            sums.add_and_gather(0)

        save_p(l, r).start()

        @pl.when(i < 3)
        def _():
            load_bias(i + 1).start()

        dqkv[rows, D : 2 * D] = acc[:, 0:D].astype(BF16)

        @pl.when(r == 0)
        def _():
            load_out(l).wait()

        dy[rows] = dy[rows] + dot(dqkv[rows, D : 2 * D], wout[...])

        @pl.when(i == 1)
        def _():
            load_out(1).start()

        norm(1)

        @pl.when(r == 0)
        def _():
            for copy in load_feed_weights(l):
                copy.wait()

        @pl.when((i == 1) | (i == 2))
        def _():
            save_u(i - 1, pl.ds(0, ROW_LEN)).wait()

        u_ref[...] = dot_nt(second[rows], wup[...]) + bup_ref[pl.ds(l, 1)]
        g_ref[rows] = gelu(u_ref[...]).astype(BF16)

        @pl.when(l == 0)
        def _():
            part[r] = dot(g_ref[rows], wdown[...]).astype(BF16)
            sums.scatter(r)
            for copy in save_feed(r, rows):
                copy.start()
            save_u(r, rows).start()

        @pl.when(l == 1)
        def _():
            pl.when(r == 0)(lambda: load_cot().wait())
            gh = dot_nt(dxl[rows], wdown[...])
            du = (gh * gelu_slope(u_ref[...])).astype(BF16)
            du_ref[rows] = du
            sums.drain(r)
            part[r] = dot(du, wup[...]).astype(BF16)
            sums.scatter(r)
            save_h(r, rows).start()
            part[2 + r] = dot(g_ref[rows], wdown[...]).astype(BF16)

        @pl.when(i == 1)
        def _():
            for copy in load_feed_weights(1):
                copy.start()

        return 0

    lax.fori_loop(0, 4, forward_step, 0)

    both = pl.ds(0, ROW_LEN), pl.ds(ROW_LEN, ROW_LEN)
    save_p(0, 0).wait()
    load_p(0).start()
    save_qkv(0, both[1]).wait()
    load_qkv(0).start()
    for which in (1, 0):
        for copy in save_norm(which, 0, both[1]):
            copy.wait()
        for copy in load_norm(which, 0):
            copy.start()
    for copy in load_feed_weights(0):
        copy.start()
    load_u(0).start()
    write_ff_grads(
        x2,
        lambda a, b: dot_tn(second[...], du_ref[:, a:b]),
        lambda a, b: dot_tn(dxl[...], g_ref[:, a:b]),
    )
    ff_sum.start()
    for copy in load_feed():
        copy.start()
    keep_features(1)

    def bias_sums(l):
        odd = lax.rem(me, 2).astype(F32)
        value = jnp.sum(du_ref[...].astype(F32), 0, keepdims=True)
        small[pl.ds(42 + 4 * l + me // 2, 1)] = jnp.concatenate(
            [value * (1.0 - odd), value * odd], axis=1
        )
        for r in range(2):
            small[40 + l : 41 + l] += jnp.sum(
                dxl[span(r * ROW_LEN + own_first, OWN, OWN)].astype(F32), 0, keepdims=True
            )

    bias_sums(1)

    def attention_results(l, block):
        for j in range(KEPT):
            for n in range(7):
                at = 8 * n + j if j < 8 else 56 + n
                ref = gq_ref if n < 3 else gt_ref if n < 6 else go_ref
                ref[j, l : l + 1, pl.ds(n % 3 * D, D)] = block[at : at + 1]

    def feed_results(l, block):
        gup_ref[l] = block[0:72, 0:UNITS]
        gdown_ref[l] = block[0:72, UNITS : 2 * UNITS]

    def place(p, grad):
        half = lax.rem(p, 2)
        for c in range(DP):
            acc[span(16 * c + 8 * half, 8, 8), 0:D] = grad[8 * c : 8 * c + 8]
            acc[pl.ds(8 * c + p, 1), D : 2 * D] = grad[128 + c : 129 + c]

    def flush(pair):
        for c in range(DP):
            x2[c // 2, c % 2, span(16 * pair, 16, 16)] = acc[
                16 * c : 16 * (c + 1), 0:D
            ].astype(BF16)

    def attention_weights(l):
        acc[0:128, D : 2 * D] = jnp.zeros((128, D), F32)

        def project(n, _):
            cols = span(n * D, D, 128)
            dproj[l, :, cols] = dot(pick_ref[...], dqkv[:, cols])
            return 0

        lax.fori_loop(0, 3, project, 0)

        def token_piece(n, _):
            cols = span(n * D, D, 128)
            place(n, dot_tn(kept[l, 0, :, 0:144], dqkv[:, cols]))
            pl.when(n == 1)(lambda: flush(0))
            return 0

        lax.fori_loop(0, 3, token_piece, 0)

        def time_piece(n, _):
            cols = span(n * D, D, 128)
            place(3 + n, dot_tn(timek_ref[:, 0:144], dproj[l, :, cols].astype(BF16)))
            pl.when(n == 0)(lambda: flush(1))
            pl.when(n == 2)(lambda: flush(2))
            return 0

        lax.fori_loop(0, 3, time_piece, 0)
        place(6, dot_tn(kept[l, 1, :, 0:144], dhl[...]))
        for c in range(DP):
            acc[16 * c + 8 : 16 * c + 16, 0:D] = acc[8 * c : 8 * c + 8, D : 2 * D]
        flush(3)
        small[span(l * 16, 16, 16), 0:1024] = fold_tables(fold, me)

    def time_gradient(l):
        load_time_weight(l).wait()
        got = jnp.zeros((8, D), F32)
        for n in range(3):
            cols = pl.ds(n * D, D)
            got = got + dot_nt(dproj[l, :, cols].astype(BF16), wqkv[:, cols])
        for r in range(2):
            gtime_ref[r] += got[4 * r : 4 * r + 4]

    def backward_step(j, _):
        l = 1 - j // 2
        r = lax.rem(j, 2)
        base = r * ROW_LEN
        rows = span(base, ROW_LEN, ROW_LEN)
        more = j < 3

        for copy in load_norm(1, j):
            copy.wait()
        sums.wait(r)

        @pl.when(l == 1)
        def _():
            save_h(r, rows).wait()
            dy[rows] = dxl[rows].astype(F32)

        @pl.when(r == 0)
        def _():
            fold[...] = jnp.zeros_like(fold)

        def second_norm(c, _):
            here = span(c * CHUNK, CHUNK, CHUNK)
            rr = span(base + c * CHUNK, CHUNK, CHUNK)
            dn = total[r, here].astype(F32)
            dh = dy[rr] + norm_slope(
                dn, unit[1, here].astype(F32), inv[1, here, 0:1], gain_ref[l, 1:2]
            )
            dy[rr] = dh
            dhl[rr] = dh.astype(BF16)
            return 0

        lax.fori_loop(0, ROW_LEN // CHUNK, second_norm, 0)

        def norm_sums(which, dn):
            value = jnp.sum(dn * unit[which, mine].astype(F32), 0, keepdims=True)
            small[pl.ds(32 + 2 * l + which, 1)] += value
            small[pl.ds(36 + 2 * l + which, 1)] += jnp.sum(dn, 0, keepdims=True)

        norm_sums(1, total[r, mine].astype(F32))

        @pl.when(more)
        def _():
            for copy in load_norm(1, j + 1):
                copy.start()

        @pl.when(j == 2)
        def _():
            load_out(0).wait()

        do_ref[...] = dot_nt(dhl[rows], wout[...]).astype(BF16)

        @pl.when(j == 1)
        def _():
            load_out(0).start()

        @pl.when(j == 2)
        def _():
            ff_sum.acquire()
            ff_sum.start()

        load_qkv(j).wait()
        load_p(j).wait()
        attend_backward(qkv, r, do_ref, p_ref, acc, ds_ref, fold, kind_ref, own_first)

        @pl.when(j == 0)
        def _():
            sums.add_and_gather(1)
            ff_sum.exchange_y()

        @pl.when(j == 1)
        def _():
            sums.add_and_gather(0)

        @pl.when(j == 2)
        def _():
            sums.add_and_gather(1)
            sums.scatter(2)
            sums.scatter(3)
            ff_sum.exchange_y()

        @pl.when(j == 3)
        def _():
            attention_results(1, at_sum.finish())
            at_sum.release()

        @pl.when(more)
        def _():
            load_p(j + 1).start()
            load_qkv(j + 1).start()

        dqkv[rows, 0:D] = (acc[:, 0:D] * SCALE).astype(BF16)
        dqkv[rows, D : 2 * D] = (acc[:, D : 2 * D] * SCALE).astype(BF16)
        dqkv[rows, 2 * D :] = acc[:, 2 * D :].astype(BF16)

        @pl.when(r == 1)
        def _():
            attention_weights(l)
            pl.when(l == 0)(lambda: at_sum.acquire())
            at_sum.start()
            ff_sum.exchange_z()

        @pl.when(j == 3)
        def _():
            sums.add_and_gather(2)
            sums.add_and_gather(3)

        @pl.when(j == 2)
        def _():
            for n in range(3):
                load_weight(0, n).wait()

        def back(n, _):
            cols = span(n * D, D, 128)
            got = dot_nt(dqkv[rows, cols], wqkv[:, cols])

            @pl.when(n == 0)
            def _():
                acc[:, 0:D] = got

            @pl.when(n > 0)
            def _():
                acc[:, 0:D] += got

            return 0

        lax.fori_loop(0, 3, back, 0)

        @pl.when(j == 1)
        def _():
            for n in range(3):
                load_weight(0, n).start()

        @pl.when(j == 3)
        def _():
            load_time_weight(0).start()

        for copy in load_norm(0, j):
            copy.wait()

        def first_norm(c, _):
            here = span(c * CHUNK, CHUNK, CHUNK)
            rr = span(base + c * CHUNK, CHUNK, CHUNK)
            dn = acc[here, 0:D]
            dy[rr] = dy[rr] + norm_slope(
                dn, unit[0, here].astype(F32), inv[0, here, 0:1], gain_ref[l, 0:1]
            )
            return 0

        lax.fori_loop(0, ROW_LEN // CHUNK, first_norm, 0)
        norm_sums(0, acc[mine, 0:D])

        @pl.when(more)
        def _():
            for copy in load_norm(0, j + 1):
                copy.start()

        @pl.when(l == 0)
        def _():
            save_dx(r, rows).start()

        @pl.when(l == 1)
        def _():
            @pl.when(r == 0)
            def _():
                for copy in load_feed_weights(0) + load_feed():
                    copy.wait()

            dxl[rows] = dy[rows].astype(BF16)
            gh = dot_nt(dxl[rows], wdown[...])
            load_u(r).wait()
            du = (gh * gelu_slope(u_ref[...])).astype(BF16)
            pl.when(r == 0)(lambda: load_u(1).start())
            du_ref[rows] = du
            sums.drain(r)
            part[r] = dot(du, wup[...]).astype(BF16)
            sums.scatter(r)

        @pl.when(j == 1)
        def _():
            at_sum.exchange()
            feed_results(1, ff_sum.finish())
            ff_sum.release()
            write_ff_grads(
                x2,
                lambda a, b: dot_tn(second[...], du_ref[:, a:b]),
                lambda a, b: dot_tn(dxl[...], g_ref[:, a:b]),
            )
            bias_sums(0)

        return 0

    lax.fori_loop(0, 4, backward_step, 0)

    def small_scatter(k):
        peer = hid_peer(me, k)
        return pltpu.make_async_remote_copy(
            src_ref=small.at[span(peer * 8, 8, 8)],
            dst_ref=small_recv.at[k - 1],
            send_sem=small_sems.at[0, k - 1],
            recv_sem=small_sems.at[1, k - 1],
            device_id={"hid": peer},
            device_id_type=MESH,
        )

    def small_swap():
        return pltpu.make_async_remote_copy(
            src_ref=small_sum.at[0],
            dst_ref=small_pair,
            send_sem=small_one.at[0],
            recv_sem=small_one.at[1],
            device_id={"dp": ff_sum.partner},
            device_id_type=MESH,
        )

    def small_spread(k, outgoing):
        chip = ff_sum.chip
        if not outgoing:
            chip = lax.rem(ff_sum.y + 4 - k // 2, 4) * 2 + lax.rem(ff_sum.z + k, 2)
        return pltpu.make_async_remote_copy(
            src_ref=small_chip.at[chip],
            dst_ref=small_chip.at[chip],
            send_sem=small_sems.at[2, k - 1],
            recv_sem=small_sems.at[3, k - 1],
            device_id=ff_sum.peer(k),
            device_id_type=MESH,
        )

    def small_gather(k, outgoing):
        owner = me if outgoing else hid_source(me, k)
        rows = small_out.at[span(owner * 8, 8, 8)]
        return pltpu.make_async_remote_copy(
            src_ref=rows,
            dst_ref=rows,
            send_sem=small_sems.at[4, k - 1],
            recv_sem=small_sems.at[5, k - 1],
            device_id={"hid": hid_peer(me, k)},
            device_id_type=MESH,
        )

    for k in HID_ORDER:
        small_scatter(k).start()
    at_sum.exchange()
    for k in HID_ORDER:
        small_scatter(k).wait_recv()
    value = small[span(me * 8, 8, 8)]
    for k in range(HID - 1):
        value = value + small_recv[k]
    small_sum[0] = value
    small_swap().start()
    time_gradient(0)
    load_time_weight(1).start()
    small_swap().wait_recv()
    small_chip[ff_sum.chip] = small_sum[0] + small_pair[...]
    for k in HID_ORDER:
        small_spread(k, True).start()
    for e in range(2):
        sums.wait(2 + e)
        save_fsum(e).start()
    feed_results(0, ff_sum.finish())
    for k in HID_ORDER:
        small_spread(k, False).wait_recv()
    value = small_chip[0]
    for c in range(1, 8):
        value = value + small_chip[c]
    small_out[span(me * 8, 8, 8)] = value
    for k in HID_ORDER:
        small_gather(k, True).start()
    time_gradient(1)
    for k in HID_ORDER:
        small_gather(k, False).wait_recv()
    for l in range(LAYERS):
        for a in range(REL):
            at = (REL - 1 - a) * 32
            gtable_ref[l, a] = small_out[16 * l : 16 * l + 16, at : at + REL]
        for n in range(2):
            ggain_ref[l, n : n + 1] = small_out[32 + 2 * l + n : 33 + 2 * l + n]
            gshift_ref[l, n : n + 1] = small_out[36 + 2 * l + n : 37 + 2 * l + n]
        for n in range(4):
            gbup_out[l : l + 1, n * D : (n + 1) * D] = small_out[42 + 4 * l + n : 43 + 4 * l + n]
        gbdown_out[l : l + 1] = small_out[40 + l : 41 + l]
    attention_results(0, at_sum.finish())
    for k in HID_ORDER:
        small_scatter(k).wait_send()
        small_spread(k, True).wait_send()
        small_gather(k, True).wait_send()
    small_swap().wait_send()
    for r in range(2):
        save_dx(r, both[r]).wait()
        save_fsum(r).wait()
    for e in range(4):
        sums.drain(e)


def layers(vmem_args, hbm_args):
    s = jax.ShapeDtypeStruct
    v = pltpu.VMEM
    dma = pltpu.SemaphoreType.DMA
    return pl.pallas_call(
        layers_kernel,
        out_shape=[
            s((2, SLOTS, D), F32),
            s((KEPT, LAYERS, 3 * D), F32),
            s((KEPT, LAYERS, 3 * D), F32),
            s((KEPT, LAYERS, D), F32),
            s((LAYERS, 72, UNITS), F32),
            s((LAYERS, 72, UNITS), F32),
            s((LAYERS, 2, D), F32),
            s((LAYERS, 2, D), F32),
            s((LAYERS, REL, HEADS, REL), F32),
            s((LAYERS, FF), F32),
            s((LAYERS, D), F32),
            s((TOKENS, D), F32),
            s((TOKENS, D), F32),
            s((2, ROW_LEN, D), BF16),
            s((LAYERS, TOKENS, 3 * D), BF16),
            s((LAYERS, 2, HEADS, ROW_LEN, ROW_LEN), BF16),
            s((LAYERS, 2, TOKENS, D), BF16),
            s((LAYERS, 2, TOKENS, 128), F32),
            s((TOKENS, D), BF16),
            s((TOKENS, UNITS), F32),
            s((TOKENS, UNITS), BF16),
        ],
        in_specs=[IN_VMEM] * len(vmem_args) + [IN_ANY] * len(hbm_args),
        out_specs=[IN_VMEM] * 11 + [IN_ANY] * 10,
        scratch_shapes=[
            v((D, 3 * D), BF16),
            v((D, D), BF16),
            v((UNITS, D), BF16),
            v((UNITS, D), BF16),
            v((HEADS, ROW_LEN, ROW_LEN), BF16),
            v((HEADS, ROW_LEN, ROW_LEN), BF16),
            v((ROW_LEN, 3 * D), BF16),
            v((2, ROW_LEN, D), BF16),
            v((2, ROW_LEN, 128), F32),
            v((D, 256), BF16),
            v((LAYERS, 2, TOKENS, 256), BF16),
            v((TOKENS, D), BF16),
            v((ROW_LEN, UNITS), F32),
            v((TOKENS, UNITS), BF16),
            v((4, ROW_LEN, D), BF16),
            v((4, ROW_LEN, D), BF16),
            v((4, HID - 1, SLICE, D), BF16),
            v((TOKENS, D), F32),
            v((TOKENS, D), BF16),
            v((TOKENS, D), BF16),
            v((ROW_LEN, D), BF16),
            v((ROW_LEN, 3 * D), F32),
            v((TOKENS, 3 * D), BF16),
            v((TOKENS, UNITS), BF16),
            v((ROW_LEN, ROW_LEN), F32),
            v((8, 2, 80, D), BF16),
            v((8, 80, D), BF16),
            v((7, 80, D), BF16),
            v((8, 64, D), BF16),
            v((7, 64, D), BF16),
            v((2, HEADS, OWN, ROW_LEN), F32),
            v((LAYERS, 8, 3 * D), F32),
            v((8, TOKENS), BF16),
            v((8, 256), BF16),
            v((64, D), F32),
            v((64, D), F32),
            v((7, 8, D), F32),
            v((1, 8, D), F32),
            v((8, D), F32),
            v((8, 8, D), F32),
            dma((19,)),
            dma((18,)),
            dma((4, 4, HID - 1)),
            dma((4,)),
            dma((4, 7)),
            pltpu.SemaphoreType.REGULAR,
            pltpu.SemaphoreType.REGULAR,
            dma((6, HID - 1)),
            dma((2,)),
        ],
        compiler_params=pltpu.CompilerParams(
            collective_id=1, has_side_effects=True, vmem_limit_bytes=VMEM_LIMIT
        ),
        name="layers",
    )(*vmem_args, *hbm_args)


def finish_kernel(bdown_ref, h_ref, fsum_ref, dx_ref, *refs):
    out_ref, grad_ref = refs[11:13]
    out_ref[...] = h_ref[...] + (fsum_ref[...].astype(F32) + bdown_ref[1:2])
    grad_ref[...] = dx_ref[...]

    @pl.when(pl.program_id(0) == 0)
    def _():
        for n in range(11):
            refs[13 + n][...] = refs[n][...]


def finish(b_down, h, fsum, dx, rest):
    s = jax.ShapeDtypeStruct
    block = pl.BlockSpec((128, D), lambda i: (i, 0))
    whole = [pl.BlockSpec(a.shape, functools.partial(lambda n, i: (0,) * n, a.ndim)) for a in rest]
    return pl.pallas_call(
        finish_kernel,
        out_shape=[s((TOKENS, D), F32)] * 2 + [s(a.shape, F32) for a in rest],
        grid=(4,),
        in_specs=[pl.BlockSpec((LAYERS, D), lambda i: (0, 0))] + [block] * 3 + whole,
        out_specs=[block] * 2 + whole,
        compiler_params=pltpu.CompilerParams(vmem_limit_bytes=VMEM_LIMIT),
        name="finish",
    )(b_down, h, fsum.reshape(TOKENS, D), dx, *rest)


def shards(
    block_in,
    time_tokens,
    layout,
    norm_gain,
    norm_bias,
    w_qkv,
    w_time,
    rel_table,
    w_out,
    w_up,
    b_up,
    w_down,
    b_down,
    cotangent,
):
    bias, tp, kind = prepare(layout, rel_table, time_tokens, w_time)
    results = layers(
        (norm_gain, norm_bias, b_up, b_down, tp, kind, time_tokens),
        (
            block_in.reshape(TOKENS, D),
            cotangent.reshape(TOKENS, D),
            w_qkv,
            w_out,
            jnp.swapaxes(w_up, 1, 2),
            w_down,
            w_time,
            bias,
        ),
    )
    dx, h, fsum = results[11:14]
    block_out, grad_in, *rest = finish(b_down, h, fsum, dx, results[:11])
    gtime, gq, gt, go, gup, gdown, ggain, gshift, gtable, gbup, gbdown = rest
    return (
        block_out.reshape(2, ROW_LEN, D),
        grad_in.reshape(2, ROW_LEN, D),
        gtime,
        ggain,
        gshift,
        jnp.swapaxes(gq, 0, 1),
        jnp.swapaxes(gt, 0, 1),
        jnp.swapaxes(gtable, 1, 2),
        jnp.swapaxes(go, 0, 1),
        gup,
        gbup,
        jnp.swapaxes(gdown, 1, 2),
        gbdown,
    )


def solution(mesh):
    in_specs = (
        P("dp", None, None),
        P("dp", None, None),
        P("dp"),
        P(),
        P(),
        P(),
        P(),
        P(),
        P(),
        P(None, None, "hid"),
        P(None, "hid"),
        P(None, "hid", None),
        P(),
        P("dp", None, None),
    )
    out_specs = (
        P("dp", None, None),
        P("dp", None, None),
        P("dp", None, None),
        P(),
        P(),
        P(None, ("dp", "hid"), None),
        P(None, ("dp", "hid"), None),
        P(),
        P(None, ("dp", "hid"), None),
        P(None, "dp", "hid"),
        P(),
        P(None, "hid", "dp"),
        P(),
    )
    return jax.shard_map(shards, mesh=mesh, in_specs=in_specs, out_specs=out_specs, check_vma=False)
```

```python
import functools

import jax
import jax.numpy as jnp
from jax import lax
from jax.experimental import pallas as pl
from jax.experimental.pallas import tpu as pltpu
from jax.sharding import PartitionSpec as P

D = 1152
HEADS = 16
HEAD_DIM = 72
FF = 4608
LAYERS = 2
GRID = 16
SUB = 8
ROW_LEN = 256
SLOTS = 4
REL = 31
DP = 16
HID = 8
UNITS = FF // HID
KEPT = D // (DP * HID)
TOKENS = 512
OWN = ROW_LEN // HID
SCALE = HEAD_DIM ** (-0.5)
MASKED_LOGIT = -1e30
NORM_EPSILON = 1e-06
F32 = jnp.float32
BF16 = jnp.bfloat16
MESH = pl.DeviceIdType.MESH
VMEM_LIMIT = 63 * 1024 * 1024
HIGHEST = lax.Precision.HIGHEST


def contract(a, b, da, db, precision=None):
    return lax.dot_general(
        a, b, (((da,), (db,)), ((), ())), preferred_element_type=F32, precision=precision
    )


def dot(a, b):
    return contract(a, b, 1, 0)


def dot_nt(a, b):
    return contract(a, b, 1, 1)


def dot_tn(a, b):
    return contract(a, b, 0, 0)


def span(start, size, multiple):
    return pl.ds(pl.multiple_of(start, multiple), size)


def gelu_parts(v):
    c = 0.7978845608028654
    square = v * v
    t = jnp.tanh(c * v * (1.0 + 0.044715 * square))
    return t, square


def gelu(v):
    t, _ = gelu_parts(v)
    return 0.5 * v * (1.0 + t)


def gelu_slope(v):
    c = 0.7978845608028654
    t, square = gelu_parts(v)
    return 0.5 * (1.0 + t) + 0.5 * v * (1.0 - t * t) * (c * (1.0 + 3.0 * 0.044715 * square))


def prepare_kernel(
    layout_ref, rel_ref, time_ref, wtime_ref, bias_ref, tp_ref, kind_ref, rows_ref, skew_ref, turned_ref
):
    g = pl.program_id(1)
    first, second = layout_ref[0], layout_ref[1]

    @pl.when(g == 0)
    def _():
        tp_ref[...] = jnp.zeros_like(tp_ref)
        for r in range(2):
            four = jnp.where(layout_ref[r] == 1, 1.0, 0.0)
            kind_ref[r, 0:1] = jnp.full((1, ROW_LEN), 1.0 - four, F32)
            kind_ref[r, 1:2] = jnp.full((1, ROW_LEN), four, F32)

    @pl.when(g < 3)
    def _():
        cols = span(384 * g, 384, 128)
        tokens = [time_ref[r, :, cols].astype(F32) for r in range(2)]
        tp_ref[0] += dot(jnp.concatenate(tokens, axis=0).astype(BF16), wtime_ref[0])

    @pl.when(g == 3)
    def _():
        for r in range(2):

            @pl.when(layout_ref[r] != 1)
            def _():
                tp_ref[0, 4 * r : 4 * r + 4] = jnp.broadcast_to(
                    tp_ref[0, 4 * r : 4 * r + 1], (SLOTS, 3 * D)
                )

    rows_ref[...] = jnp.zeros_like(rows_ref)
    rows_ref[:, 0:4, 0:REL] = rel_ref[0, :, pl.ds(4 * g, 4), :]
    table = rows_ref[:, 0]
    for i in range(1, 4):
        table = table + pltpu.roll(rows_ref[:, i], 32 * i, 1)

    def skewed(side, count, top):
        skew_ref[...] = jnp.zeros_like(skew_ref)
        for j in range(count):
            block = jnp.broadcast_to(table[top - j : top - j + 1], (side, 128))
            skew_ref[pl.ds(side * j, side)] = pltpu.roll(
                block, 113, 1, stride=1, stride_axis=0
            )

    def single(r):
        skewed(GRID, REL, REL - 1)
        turned_ref[...] = skew_ref[...].T
        for i in range(4):
            w = turned_ref[32 * i : 32 * i + GRID]
            for m in range(8):
                moved = w if m == 0 else pltpu.roll(w, 512 - 16 * m, 1)
                for t in range(2):
                    y = 15 - 8 * t - m
                    bias_ref[0, r, i, pl.ds(GRID * y, GRID), :] = moved[
                        :, 128 * t : 128 * t + ROW_LEN
                    ].astype(BF16)

    def quad(r):
        skewed(SUB, 15, 22)
        turned_ref[:, 0:128] = skew_ref[0:128].T
        half = lax.broadcasted_iota(jnp.int32, (2 * SUB, 128), 1) // 64
        closed = jnp.full((2 * SUB, 128), MASKED_LOGIT, F32).astype(BF16)
        for i in range(4):
            w = turned_ref[32 * i : 32 * i + SUB, 0:128]
            for y in range(0, SUB, 2):
                for odd in range(2):
                    moved = jnp.concatenate(
                        [
                            pltpu.roll(w, (128 + 64 * odd - (7 - y - n) * SUB) % 128, 1)
                            for n in range(2)
                        ],
                        axis=0,
                    )
                    moved = jnp.where(half == odd, moved, MASKED_LOGIT).astype(BF16)
                    for tile in range(2):
                        rows = pl.ds(64 * (2 * tile + odd) + SUB * y, 2 * SUB)
                        bias_ref[0, r, i, rows, 128 * tile : 128 * tile + 128] = moved
                        bias_ref[0, r, i, rows, 128 - 128 * tile : 256 - 128 * tile] = closed

    pl.when(first != 1)(lambda: single(0))
    pl.when(first == 1)(lambda: quad(0))

    @pl.when(first == second)
    def _():
        for i in range(4):
            bias_ref[0, 1, i] = bias_ref[0, 0, i]

    pl.when((first != second) & (second != 1))(lambda: single(1))
    pl.when((first != second) & (second == 1))(lambda: quad(1))


def prepare(layout, rel_table, time_tokens, w_time):
    return pl.pallas_call(
        prepare_kernel,
        out_shape=[
            jax.ShapeDtypeStruct((LAYERS, 2, HEADS, ROW_LEN, ROW_LEN), BF16),
            jax.ShapeDtypeStruct((LAYERS, 8, 3 * D), F32),
            jax.ShapeDtypeStruct((2, 2, ROW_LEN), F32),
        ],
        grid_spec=pltpu.PrefetchScalarGridSpec(
            num_scalar_prefetch=1,
            grid=(LAYERS, 4),
            in_specs=[
                pl.BlockSpec((1, REL, HEADS, REL), lambda l, g, _: (l, 0, 0, 0)),
                pl.BlockSpec((2, SLOTS, D), lambda l, g, _: (0, 0, 0)),
                pl.BlockSpec((1, 384, 3 * D), lambda l, g, _: (l, jnp.minimum(g, 2), 0)),
            ],
            out_specs=[
                pl.BlockSpec((1, 2, 4, ROW_LEN, ROW_LEN), lambda l, g, _: (l, 0, g, 0, 0)),
                pl.BlockSpec((1, 8, 3 * D), lambda l, g, _: (l, 0, 0)),
                pl.BlockSpec((2, 2, ROW_LEN), lambda l, g, _: (0, 0, 0)),
            ],
            scratch_shapes=[
                pltpu.VMEM((REL, 8, 128), F32),
                pltpu.VMEM((512, 128), F32),
                pltpu.VMEM((128, 512), F32),
            ],
        ),
        compiler_params=pltpu.CompilerParams(vmem_limit_bytes=VMEM_LIMIT),
        name="prepare",
    )(layout, jnp.swapaxes(rel_table, 1, 2), time_tokens, w_time)


IN_VMEM = pl.BlockSpec(memory_space=pltpu.VMEM)
IN_ANY = pl.BlockSpec(memory_space=pl.ANY)
CHUNK = 128
HID_ORDER = (2, 6, 1, 4, 3, 7, 5)
SLICE = ROW_LEN // HID


def head_window(h):
    start = h * HEAD_DIM // 128 * 128
    offset = h * HEAD_DIM - start
    width = 128 if offset + HEAD_DIM <= 128 else 256
    lane = lax.broadcasted_iota(jnp.int32, (1, width), 1)
    mask = ((lane >= offset) & (lane < offset + HEAD_DIM)).astype(F32).astype(BF16)
    return start, width, mask


def hid_peer(me, k):
    return lax.rem(me // 2 + k // 2, 4) * 2 + lax.rem(me + k, 2)


def hid_source(me, k):
    return lax.rem(me // 2 + 4 - k // 2, 4) * 2 + lax.rem(me + k, 2)


def greet_hid(barrier, me):
    for k in HID_ORDER:
        pl.semaphore_signal(
            barrier, inc=1, device_id={"hid": hid_peer(me, k)}, device_id_type=MESH
        )


class HidSums:
    def __init__(self, part, recv, total, sems):
        self.part, self.recv, self.total = part, recv, total
        self.send1, self.recv1, self.send2, self.recv2 = sems
        self.me = lax.axis_index("hid")

    def scatter_copy(self, e, k):
        peer = hid_peer(self.me, k)
        return pltpu.make_async_remote_copy(
            src_ref=self.part.at[e, span(peer * SLICE, SLICE, SLICE)],
            dst_ref=self.recv.at[e, k - 1],
            send_sem=self.send1.at[e, k - 1],
            recv_sem=self.recv1.at[e, k - 1],
            device_id={"hid": peer},
            device_id_type=MESH,
        )

    def gather_copy(self, slot, e, k, outgoing):
        owner = self.me if outgoing else hid_source(self.me, k)
        rows = self.total.at[slot, span(owner * SLICE, SLICE, SLICE)]
        return pltpu.make_async_remote_copy(
            src_ref=rows,
            dst_ref=rows,
            send_sem=self.send2.at[e, k - 1],
            recv_sem=self.recv2.at[e, k - 1],
            device_id={"hid": hid_peer(self.me, k)},
            device_id_type=MESH,
        )

    def scatter(self, e):
        for k in HID_ORDER:
            self.scatter_copy(e, k).start()

    def add_and_gather(self, e):
        mine = span(self.me * SLICE, SLICE, SLICE)
        for k in HID_ORDER:
            self.scatter_copy(e, k).wait_recv()
        total = self.part[e, mine].astype(F32)
        for k in range(HID - 1):
            total = total + self.recv[e, k].astype(F32)
        self.total[e, mine] = total.astype(BF16)
        for k in HID_ORDER:
            self.gather_copy(e, e, k, True).start()

    def wait(self, e):
        for k in HID_ORDER:
            self.gather_copy(e, e, k, False).wait_recv()

    def drain(self, e):
        for k in HID_ORDER:
            self.scatter_copy(e, k).wait_send()
            self.gather_copy(e, e, k, True).wait_send()


def write_ff_grads(ffg, up_of, down_of):
    for n, of in enumerate((up_of, down_of)):
        for a, b in ((0, 128), (128, 256), (256, 384), (384, 512), (512, UNITS)):
            grad = of(a, b)
            for c in range(DP):
                ffg[c // 2, c % 2, 0:72, n * UNITS + a : n * UNITS + b] = grad[
                    72 * c : 72 * (c + 1)
                ].astype(BF16)


def layer_norm_rows(x, gain, shift):
    centre = x - jnp.mean(x, -1, keepdims=True)
    inverse = lax.rsqrt(jnp.mean(centre * centre, -1, keepdims=True) + NORM_EPSILON)
    unit = centre * inverse
    return (unit * gain + shift).astype(BF16), unit.astype(BF16), inverse


def kept_matrix():
    feature = lax.broadcasted_iota(jnp.int32, (D, 256), 0)
    column = lax.broadcasted_iota(jnp.int32, (D, 256), 1)
    low = column < 128
    owner = jnp.where(low, column // 8, column - 128)
    inner = jnp.where(low, column % 8, 8)
    chosen = (feature == owner * 72 + lax.axis_index("hid") * KEPT + inner) & (column < 144)
    return chosen.astype(F32).astype(BF16)


def attend_forward(qkv, bias_ref, p_ref, o_acc):
    o_acc[:, 0:D] = jnp.zeros((ROW_LEN, D), F32)

    def scores(h):
        start, width, mask = head_window(h)
        q = qkv[:, start : start + width] * mask
        return dot_nt(q, qkv[:, D + start : D + start + width])

    def mix(h, score):
        start, width, mask = head_window(h)
        logits = score * SCALE + bias_ref[h].astype(F32)
        expo = jnp.exp(logits - jnp.max(logits, -1, keepdims=True))
        p = (expo * (1.0 / jnp.sum(expo, -1, keepdims=True))).astype(BF16)
        p_ref[h] = p
        v = qkv[:, 2 * D + start : 2 * D + start + width] * mask
        o_acc[:, start : start + width] += dot(p, v)

    ready = {}
    for h in range(HEADS + 1):
        if h < HEADS:
            ready[h] = scores(h)
        if h:
            mix(h - 1, ready.pop(h - 1))


class DpSums:
    def __init__(self, x, pair, recv, sems, free):
        self.x, self.pair, self.recv, self.free = x, pair, recv, free
        self.pair_send, self.pair_recv, self.send, self.got = sems
        me = lax.axis_index("dp")
        self.y, self.z, self.core = me // 4, lax.rem(me // 2, 2), lax.rem(me, 2)
        self.chip = me // 2
        self.partner = self.chip * 2 + (1 - self.core)

    def other(self, k):
        return lax.rem(self.y + k // 2, 4) * 2 + lax.rem(self.z + k, 2)

    def peer(self, k):
        return {"dp": self.other(k) * 2 + self.core}

    def pair_copy(self):
        return pltpu.make_async_remote_copy(
            src_ref=self.x.at[:, 1 - self.core],
            dst_ref=self.pair,
            send_sem=self.pair_send,
            recv_sem=self.pair_recv,
            device_id={"dp": self.partner},
            device_id_type=MESH,
        )

    def start(self):
        self.pair_copy().start()

    def add_pair(self, c):
        both = self.x[c, self.core].astype(F32) + self.pair[c].astype(F32)
        self.pair[c] = both.astype(BF16)

    def release(self):
        pl.semaphore_signal(
            self.free, inc=1, device_id={"dp": self.partner}, device_id_type=MESH
        )
        for k in HID_ORDER:
            pl.semaphore_signal(self.free, inc=1, device_id=self.peer(k), device_id_type=MESH)

    def acquire(self):
        pl.semaphore_wait(self.free, 8)


class DirectSums(DpSums):
    def chip_copy(self, k):
        return pltpu.make_async_remote_copy(
            src_ref=self.pair.at[self.other(k)],
            dst_ref=self.recv.at[k - 1],
            send_sem=self.send.at[k - 1],
            recv_sem=self.got.at[k - 1],
            device_id=self.peer(k),
            device_id_type=MESH,
        )

    def exchange(self):
        self.pair_copy().wait_recv()
        for k in HID_ORDER + (0,):
            self.add_pair(self.other(k))
            if k:
                self.chip_copy(k).start()
        self.pair_copy().wait_send()

    def finish(self):
        total = self.pair[self.chip].astype(F32)
        for k in HID_ORDER:
            self.chip_copy(k).wait_recv()
            total = total + self.recv[k - 1].astype(F32)
        for k in HID_ORDER:
            self.chip_copy(k).wait_send()
        return total


class SteppedSums(DpSums):
    def y_copy(self, k):
        target = lax.rem(self.y + k, 4)
        return pltpu.make_async_remote_copy(
            src_ref=self.pair.at[pl.ds(2 * target, 2)],
            dst_ref=self.recv.at[pl.ds(2 * k - 2, 2)],
            send_sem=self.send.at[k - 1],
            recv_sem=self.got.at[k - 1],
            device_id=self.peer(2 * k),
            device_id_type=MESH,
        )

    def z_copy(self):
        return pltpu.make_async_remote_copy(
            src_ref=self.pair.at[2 * self.y + 1 - self.z],
            dst_ref=self.recv.at[6],
            send_sem=self.send.at[3],
            recv_sem=self.got.at[3],
            device_id=self.peer(1),
            device_id_type=MESH,
        )

    def exchange_y(self):
        self.pair_copy().wait_recv()
        for k in (2, 1, 3, 0):
            target = lax.rem(self.y + k, 4)
            for z in range(2):
                self.add_pair(2 * target + z)
            if k:
                self.y_copy(k).start()
        self.pair_copy().wait_send()

    def exchange_z(self):
        for k in (1, 3, 2):
            self.y_copy(k).wait_recv()
        for own in (False, True):
            z = self.z if own else 1 - self.z
            c = 2 * self.y + z
            block = self.pair[c].astype(F32)
            for k in (1, 2, 3):
                block = block + self.recv[2 * k - 2 + z].astype(F32)
            self.pair[c] = block.astype(BF16)
            if not own:
                self.z_copy().start()

    def finish(self):
        self.z_copy().wait_recv()
        total = self.pair[self.chip].astype(F32) + self.recv[6].astype(F32)
        for k in (1, 2, 3):
            self.y_copy(k).wait_send()
        self.z_copy().wait_send()
        return total


def norm_slope(dn, unit, inverse, gain):
    scaled = dn * gain
    return inverse * (
        scaled
        - jnp.mean(scaled, -1, keepdims=True)
        - unit * jnp.mean(scaled * unit, -1, keepdims=True)
    )


def attend_backward(qkv, r, do_ref, p_ref, acc, ds_ref, fold, kind_ref, own_first):
    acc[...] = jnp.zeros_like(acc)

    def slopes(h):
        start, width, mask = head_window(h)
        v = qkv[:, 2 * D + start : 2 * D + start + width] * mask
        return dot_nt(do_ref[:, start : start + width], v)

    def spread(h, dp):
        start, width, mask = head_window(h)
        p_low = p_ref[h]
        p = p_low.astype(F32)
        t = p * dp
        ds = t - p * jnp.sum(t, -1, keepdims=True)
        ds_ref[...] = ds
        low = ds.astype(BF16)
        k = qkv[:, D + start : D + start + width] * mask
        q = qkv[:, start : start + width] * mask
        do = do_ref[:, start : start + width] * mask
        acc[:, start : start + width] += dot(low, k)
        acc[:, D + start : D + start + width] += dot_tn(low, q)
        acc[:, 2 * D + start : 2 * D + start + width] += dot_tn(p_low, do)
        mine = ds_ref[span(own_first, OWN, OWN)]
        fold[0, h] += mine * kind_ref[r, 0:1]
        fold[1, h] += mine * kind_ref[r, 1:2]

    ready = {}
    depth = 2
    for h in range(HEADS + depth):
        if h < HEADS:
            ready[h] = slopes(h)
        if h >= depth:
            spread(h - depth, ready.pop(h - depth))


def two_part_dot(a, b):
    high = a.astype(BF16)
    low = (a - high.astype(F32)).astype(BF16)
    return dot(high, b) + dot(low, b)


def fold_tables(fold, me):
    lane = lax.broadcasted_iota(jnp.int32, (ROW_LEN, 512), 0)
    place = lax.broadcasted_iota(jnp.int32, (ROW_LEN, 512), 1)
    wide = (place == (lane // GRID) * 32 + 15 - lane % GRID).astype(F32).astype(BF16)
    inner = lane % (SUB * SUB)
    narrow = (place == (inner // SUB) * 32 + 15 - inner % SUB).astype(F32).astype(BF16)
    rest = jnp.zeros((HEADS, 512), F32)
    out = jnp.zeros((HEADS, 1024), F32)
    for kind, (side, chosen) in enumerate(((GRID, wide), (SUB, narrow))):
        lines = []
        for n in range(2):
            sums = fold[kind, 8 * n : 8 * (n + 1)].reshape(8 * OWN, ROW_LEN)
            wider = two_part_dot(sums, chosen).reshape(8 * OWN // side, side, 512)
            line = wider[:, 0]
            for x in range(1, side):
                line = line + pltpu.roll(wider[:, x], x, 1)
            lines.append(line.reshape(8, OWN // side, 512))
        for i in range(OWN // side):
            line = jnp.concatenate([part[:, i] for part in lines], axis=0)
            y = 2 * me + i if side == GRID else lax.rem(me, 2) * 4 + i
            out = out + pltpu.roll(
                jnp.concatenate([line, rest], axis=1), (15 - y) * 32, 1
            )
    return out


def layers_kernel(
    gain_ref,
    shift_ref,
    bup_ref,
    bdown_ref,
    tp_ref,
    kind_ref,
    time_ref,
    x_hbm,
    cot_hbm,
    wqkv_hbm,
    wout_hbm,
    wup_hbm,
    wdown_hbm,
    wtime_hbm,
    bias_hbm,
    gtime_ref,
    gq_ref,
    gt_ref,
    go_ref,
    gup_ref,
    gdown_ref,
    ggain_ref,
    gshift_ref,
    gtable_ref,
    gbup_out,
    gbdown_out,
    dx_hbm,
    h_hbm,
    fsum_hbm,
    qkv_hbm,
    p_hbm,
    unit_hbm,
    inv_hbm,
    second_hbm,
    u_hbm,
    g_hbm,
    wqkv,
    wout,
    wup,
    wdown,
    bias_ref,
    p_ref,
    qkv,
    unit,
    inv,
    keep_ref,
    kept,
    second,
    u_ref,
    g_ref,
    total,
    part,
    recv,
    dy,
    dhl,
    dxl,
    do_ref,
    acc,
    dqkv,
    du_ref,
    ds_ref,
    x2,
    pair2,
    recv2,
    pair3,
    recv3,
    fold,
    dproj,
    pick_ref,
    timek_ref,
    small,
    small_out,
    small_recv,
    small_sum,
    small_pair,
    small_chip,
    late,
    late_pair,
    late_chip,
    load_sem,
    save_sem,
    hid_sems,
    dp_sems,
    chip_sems,
    free2,
    free3,
    small_sems,
    small_one,
):
    me = lax.axis_index("hid")
    own_first = me * OWN
    mine = span(own_first, OWN, OWN)
    sums = HidSums(part, recv, total, tuple(hid_sems.at[n] for n in range(4)))
    ff_sum = SteppedSums(
        x2,
        pair2,
        recv2,
        (dp_sems.at[0], dp_sems.at[1], chip_sems.at[0], chip_sems.at[1]),
        free2,
    )
    at_sum, last_sum = (
        kind(
            x2.at[:, :, pl.ds(0, 64)],
            pair3,
            recv3,
            (dp_sems.at[2], dp_sems.at[3], chip_sems.at[2], chip_sems.at[3]),
            free3,
        )
        for kind in (SteppedSums, DirectSums)
    )

    def load(n, src, dst):
        return pltpu.make_async_copy(src, dst, load_sem.at[n])

    def save(n, src, dst):
        return pltpu.make_async_copy(src, dst, save_sem.at[n])

    def load_weight(l, n):
        cols = pl.ds(n * D, D)
        return load(n, wqkv_hbm.at[l, :, cols], wqkv.at[:, cols])

    def load_time_weight(l):
        return load(3, wtime_hbm.at[l], wqkv)

    def load_out(l):
        return load(4, wout_hbm.at[l], wout)

    def load_feed_weights(l):
        return [load(5, wup_hbm.at[l], wup), load(6, wdown_hbm.at[l], wdown)]

    def load_bias(i):
        return load(7, bias_hbm.at[i // 2, lax.rem(i, 2)], bias_ref)

    def load_x():
        return load(8, x_hbm, dhl)

    def load_cot():
        return load(9, cot_hbm, dxl)

    def place_of(j):
        return 1 - j // 2, span(lax.rem(j, 2) * ROW_LEN, ROW_LEN, ROW_LEN)

    def load_p(j):
        return load(10, p_hbm.at[1 - j // 2, lax.rem(j, 2)], p_ref)

    def load_qkv(j):
        l, rows = place_of(j)
        return load(11, qkv_hbm.at[l, rows], qkv)

    def load_norm(which, j):
        l, rows = place_of(j)
        return [
            load(12 + 2 * which, unit_hbm.at[l, which, rows], unit.at[which]),
            load(13 + 2 * which, inv_hbm.at[l, which, rows], inv.at[which]),
        ]

    def load_u(r):
        return load(16, u_hbm.at[span(r * ROW_LEN, ROW_LEN, ROW_LEN)], u_ref)

    def load_feed():
        return [load(17, second_hbm, second), load(18, g_hbm, g_ref)]

    def save_qkv(l, rows):
        return save(0, qkv, qkv_hbm.at[l, rows])

    def save_p(l, r):
        return save(1, p_ref, p_hbm.at[l, r])

    def save_norm(which, l, rows):
        return [
            save(2 + 2 * which, unit.at[which], unit_hbm.at[l, which, rows]),
            save(3 + 2 * which, inv.at[which], inv_hbm.at[l, which, rows]),
        ]

    def save_u(r, rows):
        return save(10 + r, u_ref, u_hbm.at[rows])

    def save_feed(r, rows):
        return [
            save(6 + r, second.at[rows], second_hbm.at[rows]),
            save(8 + r, g_ref.at[rows], g_hbm.at[rows]),
        ]

    def save_h(r, rows):
        return save(12 + r, dy.at[rows], h_hbm.at[rows])

    def save_dx(r, rows):
        return save(14 + r, dy.at[rows], dx_hbm.at[rows])

    def save_fsum(r):
        return save(16 + r, total.at[2 + r], fsum_hbm.at[r])

    load_x().start()
    for n in range(3):
        load_weight(0, n).start()
    load_bias(0).start()
    load_out(0).start()
    for copy in load_feed_weights(0):
        copy.start()
    load_cot().start()
    barrier = pltpu.get_barrier_semaphore()
    greet_hid(barrier, me)
    pl.semaphore_signal(
        barrier, inc=1, device_id={"dp": ff_sum.partner}, device_id_type=MESH
    )
    for k in HID_ORDER:
        pl.semaphore_signal(barrier, inc=1, device_id=ff_sum.peer(k), device_id_type=MESH)
    small[...] = jnp.zeros_like(small)
    late[...] = jnp.zeros_like(late)
    gtime_ref[...] = jnp.zeros_like(gtime_ref)
    keep_ref[...] = kept_matrix()
    tokens = [time_ref[r].astype(F32) for r in range(2)]
    timek_ref[...] = dot(
        jnp.concatenate(tokens, axis=0).astype(BF16), keep_ref[...]
    ).astype(BF16)
    quarter = lax.broadcasted_iota(jnp.int32, (8, ROW_LEN), 1) // 64
    owner = lax.broadcasted_iota(jnp.int32, (8, ROW_LEN), 0)
    for r in range(2):
        whole = (owner == 4 * r).astype(F32) * kind_ref[r, 0:1]
        parts = (owner == 4 * r + quarter).astype(F32) * kind_ref[r, 1:2]
        pick_ref[:, pl.ds(r * ROW_LEN, ROW_LEN)] = (whole + parts).astype(BF16)
    load_x().wait()
    pl.semaphore_wait(barrier, 15)

    def keep_features(l):
        for n in range(2):
            kept[l, n] = dot(dqkv[:, n * D : (n + 1) * D], keep_ref[...]).astype(BF16)

    def forward_step(i, _):
        l = i // 2
        r = lax.rem(i, 2)
        base = r * ROW_LEN
        rows = span(base, ROW_LEN, ROW_LEN)

        @pl.when(i > 0)
        def _():
            for which in range(2):
                for copy in save_norm(which, 0, rows):
                    copy.wait()
            save_qkv(0, rows).wait()

        @pl.when(l == 0)
        def _():
            dy[rows] = dhl[rows].astype(F32)

        @pl.when(l == 1)
        def _():
            pl.when(r == 0)(lambda: keep_features(0))
            for copy in save_feed(r, rows):
                copy.wait()
            sums.wait(r)
            dy[rows] = dy[rows] + (total[r].astype(F32) + bdown_ref[0:1])

        def norm(which):
            def body(c, _):
                here = span(c * CHUNK, CHUNK, CHUNK)
                rr = span(base + c * CHUNK, CHUNK, CHUNK)
                low, value, inverse = layer_norm_rows(
                    dy[rr], gain_ref[l, which : which + 1], shift_ref[l, which : which + 1]
                )
                if which == 0:
                    dqkv[rr, 0:D] = low
                else:
                    second[rr] = low
                unit[which, here] = value
                inv[which, here] = jnp.broadcast_to(inverse, (CHUNK, 128))
                return 0

            lax.fori_loop(0, ROW_LEN // CHUNK, body, 0)
            for copy in save_norm(which, l, rows):
                copy.start()

        norm(0)
        for n in range(3):

            @pl.when(r == 0)
            def _():
                load_weight(l, n).wait()

            cols = pl.ds(n * D, D)
            wide = dot(dqkv[rows, 0:D], wqkv[:, cols])
            for s in range(SLOTS):
                qkv[64 * s : 64 * (s + 1), cols] = (
                    wide[64 * s : 64 * (s + 1)] + tp_ref[l, pl.ds(4 * r + s, 1), cols]
                ).astype(BF16)

        @pl.when(i == 2)
        def _():
            sums.add_and_gather(1)

        save_qkv(l, rows).start()

        @pl.when(i == 1)
        def _():
            for n in range(3):
                load_weight(1, n).start()

        load_bias(i).wait()

        @pl.when(i > 0)
        def _():
            save_p(0, 0).wait()

        attend_forward(qkv, bias_ref, p_ref, acc)

        @pl.when((i == 1) | (i == 3))
        def _():
            sums.add_and_gather(0)

        save_p(l, r).start()

        @pl.when(i < 3)
        def _():
            load_bias(i + 1).start()

        dqkv[rows, D : 2 * D] = acc[:, 0:D].astype(BF16)

        @pl.when(r == 0)
        def _():
            load_out(l).wait()

        dy[rows] = dy[rows] + dot(dqkv[rows, D : 2 * D], wout[...])

        @pl.when(i == 1)
        def _():
            load_out(1).start()

        norm(1)

        @pl.when(r == 0)
        def _():
            for copy in load_feed_weights(l):
                copy.wait()

        @pl.when((i == 1) | (i == 2))
        def _():
            save_u(i - 1, pl.ds(0, ROW_LEN)).wait()

        u_ref[...] = dot_nt(second[rows], wup[...]) + bup_ref[pl.ds(l, 1)]
        g_ref[rows] = gelu(u_ref[...]).astype(BF16)

        @pl.when(l == 0)
        def _():
            part[r] = dot(g_ref[rows], wdown[...]).astype(BF16)
            sums.scatter(r)
            for copy in save_feed(r, rows):
                copy.start()
            save_u(r, rows).start()

        @pl.when(l == 1)
        def _():
            pl.when(r == 0)(lambda: load_cot().wait())
            gh = dot_nt(dxl[rows], wdown[...])
            du = (gh * gelu_slope(u_ref[...])).astype(BF16)
            du_ref[rows] = du
            sums.drain(r)
            part[r] = dot(du, wup[...]).astype(BF16)
            sums.scatter(r)
            save_h(r, rows).start()
            part[2 + r] = dot(g_ref[rows], wdown[...]).astype(BF16)

        @pl.when(i == 1)
        def _():
            for copy in load_feed_weights(1):
                copy.start()

        return 0

    lax.fori_loop(0, 4, forward_step, 0)

    both = pl.ds(0, ROW_LEN), pl.ds(ROW_LEN, ROW_LEN)
    save_p(0, 0).wait()
    load_p(0).start()
    save_qkv(0, both[1]).wait()
    load_qkv(0).start()
    for which in (1, 0):
        for copy in save_norm(which, 0, both[1]):
            copy.wait()
        for copy in load_norm(which, 0):
            copy.start()
    for copy in load_feed_weights(0):
        copy.start()
    load_u(0).start()
    write_ff_grads(
        x2,
        lambda a, b: dot_tn(second[...], du_ref[:, a:b]),
        lambda a, b: dot_tn(dxl[...], g_ref[:, a:b]),
    )
    ff_sum.start()
    for copy in load_feed():
        copy.start()
    keep_features(1)

    def bias_sums(l):
        odd = lax.rem(me, 2).astype(F32)
        value = jnp.sum(du_ref[...].astype(F32), 0, keepdims=True)
        small[pl.ds(42 + 4 * l + me // 2, 1)] = jnp.concatenate(
            [value * (1.0 - odd), value * odd], axis=1
        )
        for r in range(2):
            small[40 + l : 41 + l] += jnp.sum(
                dxl[span(r * ROW_LEN + own_first, OWN, OWN)].astype(F32), 0, keepdims=True
            )

    bias_sums(1)

    def attention_results(l, block):
        for j in range(KEPT):
            for n in range(7):
                at = 8 * n + j if j < 8 else 56 + n
                ref = gq_ref if n < 3 else gt_ref if n < 6 else go_ref
                ref[j, l : l + 1, pl.ds(n % 3 * D, D)] = block[at : at + 1]

    def feed_results(l, block):
        gup_ref[l] = block[0:72, 0:UNITS]
        gdown_ref[l] = block[0:72, UNITS : 2 * UNITS]

    def place(p, grad):
        half = lax.rem(p, 2)
        for c in range(DP):
            acc[span(16 * c + 8 * half, 8, 8), 0:D] = grad[8 * c : 8 * c + 8]
            acc[pl.ds(8 * c + p, 1), D : 2 * D] = grad[128 + c : 129 + c]

    def flush(pair):
        for c in range(DP):
            x2[c // 2, c % 2, span(16 * pair, 16, 16)] = acc[
                16 * c : 16 * (c + 1), 0:D
            ].astype(BF16)

    def attention_weights(l):
        acc[0:128, D : 2 * D] = jnp.zeros((128, D), F32)

        def project(n, _):
            cols = span(n * D, D, 128)
            dproj[l, :, cols] = dot(pick_ref[...], dqkv[:, cols])
            return 0

        lax.fori_loop(0, 3, project, 0)

        def token_piece(n, _):
            cols = span(n * D, D, 128)
            place(n, dot_tn(kept[l, 0, :, 0:144], dqkv[:, cols]))
            pl.when(n == 1)(lambda: flush(0))
            return 0

        lax.fori_loop(0, 3, token_piece, 0)

        def time_piece(n, _):
            cols = span(n * D, D, 128)
            place(3 + n, dot_tn(timek_ref[:, 0:144], dproj[l, :, cols].astype(BF16)))
            pl.when(n == 0)(lambda: flush(1))
            pl.when(n == 2)(lambda: flush(2))
            return 0

        lax.fori_loop(0, 3, time_piece, 0)
        place(6, dot_tn(kept[l, 1, :, 0:144], dhl[...]))
        for c in range(DP):
            acc[16 * c + 8 : 16 * c + 16, 0:D] = acc[8 * c : 8 * c + 8, D : 2 * D]
        flush(3)
        small[span(l * 16, 16, 16), 0:1024] = fold_tables(fold, me)

    def time_gradient(l):
        load_time_weight(l).wait()
        got = jnp.zeros((8, D), F32)
        for n in range(3):
            cols = pl.ds(n * D, D)
            got = got + dot_nt(dproj[l, :, cols].astype(BF16), wqkv[:, cols])
        for r in range(2):
            gtime_ref[r] += got[4 * r : 4 * r + 4]

    def small_scatter(k):
        peer = hid_peer(me, k)
        return pltpu.make_async_remote_copy(
            src_ref=small.at[span(peer * 8, 8, 8)],
            dst_ref=small_recv.at[k - 1],
            send_sem=small_sems.at[0, k - 1],
            recv_sem=small_sems.at[1, k - 1],
            device_id={"hid": peer},
            device_id_type=MESH,
        )

    def swap(src, dst, n):
        return pltpu.make_async_remote_copy(
            src_ref=src,
            dst_ref=dst,
            send_sem=small_one.at[n],
            recv_sem=small_one.at[n + 1],
            device_id={"dp": ff_sum.partner},
            device_id_type=MESH,
        )

    def spread(ref, n, k, outgoing):
        chip = ff_sum.chip
        if not outgoing:
            chip = lax.rem(ff_sum.y + 4 - k // 2, 4) * 2 + lax.rem(ff_sum.z + k, 2)
        return pltpu.make_async_remote_copy(
            src_ref=ref.at[chip],
            dst_ref=ref.at[chip],
            send_sem=small_sems.at[n, k - 1],
            recv_sem=small_sems.at[n + 1, k - 1],
            device_id=ff_sum.peer(k),
            device_id_type=MESH,
        )

    def small_gather(k, outgoing):
        owner = me if outgoing else hid_source(me, k)
        rows = small_out.at[span(owner * 8, 8, 8)]
        return pltpu.make_async_remote_copy(
            src_ref=rows,
            dst_ref=rows,
            send_sem=small_sems.at[4, k - 1],
            recv_sem=small_sems.at[5, k - 1],
            device_id={"hid": hid_peer(me, k)},
            device_id_type=MESH,
        )

    def backward_step(j, _):
        l = 1 - j // 2
        r = lax.rem(j, 2)
        base = r * ROW_LEN
        rows = span(base, ROW_LEN, ROW_LEN)
        more = j < 3

        for copy in load_norm(1, j):
            copy.wait()
        sums.wait(r)

        @pl.when(l == 1)
        def _():
            save_h(r, rows).wait()
            dy[rows] = dxl[rows].astype(F32)

        @pl.when(r == 0)
        def _():
            fold[...] = jnp.zeros_like(fold)

        def second_norm(c, _):
            here = span(c * CHUNK, CHUNK, CHUNK)
            rr = span(base + c * CHUNK, CHUNK, CHUNK)
            dn = total[r, here].astype(F32)
            dh = dy[rr] + norm_slope(
                dn, unit[1, here].astype(F32), inv[1, here, 0:1], gain_ref[l, 1:2]
            )
            dy[rr] = dh
            dhl[rr] = dh.astype(BF16)
            return 0

        lax.fori_loop(0, ROW_LEN // CHUNK, second_norm, 0)

        def norm_sums(which, dn):
            value = jnp.sum(dn * unit[which, mine].astype(F32), 0, keepdims=True)
            small[pl.ds(32 + 2 * l + which, 1)] += value
            small[pl.ds(36 + 2 * l + which, 1)] += jnp.sum(dn, 0, keepdims=True)

        norm_sums(1, total[r, mine].astype(F32))

        @pl.when(more)
        def _():
            for copy in load_norm(1, j + 1):
                copy.start()

        @pl.when(j == 2)
        def _():
            load_out(0).wait()

        do_ref[...] = dot_nt(dhl[rows], wout[...]).astype(BF16)

        @pl.when(j == 1)
        def _():
            load_out(0).start()

        load_qkv(j).wait()
        load_p(j).wait()
        attend_backward(qkv, r, do_ref, p_ref, acc, ds_ref, fold, kind_ref, own_first)

        @pl.when(j == 0)
        def _():
            sums.add_and_gather(1)
            ff_sum.exchange_y()

        @pl.when(j == 1)
        def _():
            sums.add_and_gather(0)

        @pl.when(j == 2)
        def _():
            sums.add_and_gather(1)
            ff_sum.acquire()
            ff_sum.start()
            sums.add_and_gather(2)

        @pl.when(j == 3)
        def _():
            sums.add_and_gather(3)
            attention_results(1, at_sum.finish())
            at_sum.release()

        @pl.when(more)
        def _():
            load_p(j + 1).start()
            load_qkv(j + 1).start()

        dqkv[rows, 0:D] = (acc[:, 0:D] * SCALE).astype(BF16)
        dqkv[rows, D : 2 * D] = (acc[:, D : 2 * D] * SCALE).astype(BF16)
        dqkv[rows, 2 * D :] = acc[:, 2 * D :].astype(BF16)

        @pl.when(r == 1)
        def _():
            attention_weights(l)
            pl.when(l == 0)(lambda: at_sum.acquire())
            at_sum.start()
            pl.when(l == 1)(lambda: ff_sum.exchange_z())

        @pl.when(j == 3)
        def _():
            for k in HID_ORDER:
                small_scatter(k).start()

        @pl.when(j == 2)
        def _():
            for n in range(3):
                load_weight(0, n).wait()

        def back(n, _):
            cols = span(n * D, D, 128)
            got = dot_nt(dqkv[rows, cols], wqkv[:, cols])

            @pl.when(n == 0)
            def _():
                acc[:, 0:D] = got

            @pl.when(n > 0)
            def _():
                acc[:, 0:D] += got

            return 0

        lax.fori_loop(0, 3, back, 0)

        @pl.when(j == 1)
        def _():
            for n in range(3):
                load_weight(0, n).start()

        @pl.when(j == 3)
        def _():
            load_time_weight(0).start()
            for k in HID_ORDER:
                small_scatter(k).wait_recv()
            value = small[span(me * 8, 8, 8)]
            for k in range(HID - 1):
                value = value + small_recv[k]
            small_sum[0] = value
            swap(small_sum.at[0], small_pair, 0).start()

        for copy in load_norm(0, j):
            copy.wait()

        def first_norm(c, _):
            here = span(c * CHUNK, CHUNK, CHUNK)
            rr = span(base + c * CHUNK, CHUNK, CHUNK)
            dn = acc[here, 0:D]
            dy[rr] = dy[rr] + norm_slope(
                dn, unit[0, here].astype(F32), inv[0, here, 0:1], gain_ref[l, 0:1]
            )
            return 0

        lax.fori_loop(0, ROW_LEN // CHUNK, first_norm, 0)
        @pl.when(l == 1)
        def _():
            norm_sums(0, acc[mine, 0:D])

        @pl.when(l == 0)
        def _():
            late[0:1] += jnp.sum(acc[:, 0:D] * unit[0].astype(F32), 0, keepdims=True)
            late[1:2] += jnp.sum(acc[:, 0:D], 0, keepdims=True)

        @pl.when(j == 3)
        def _():
            swap(small_sum.at[0], small_pair, 0).wait_recv()
            small_chip[ff_sum.chip] = small_sum[0] + small_pair[...]
            for k in HID_ORDER:
                spread(small_chip, 2, k, True).start()
            swap(late, late_pair, 2).start()

        @pl.when(more)
        def _():
            for copy in load_norm(0, j + 1):
                copy.start()

        @pl.when(l == 0)
        def _():
            save_dx(r, rows).start()

        @pl.when(j == 2)
        def _():
            at_sum.exchange_z()
            ff_sum.exchange_y()

        @pl.when(l == 1)
        def _():
            @pl.when(r == 0)
            def _():
                for copy in load_feed_weights(0) + load_feed():
                    copy.wait()

            dxl[rows] = dy[rows].astype(BF16)
            gh = dot_nt(dxl[rows], wdown[...])
            load_u(r).wait()
            du = (gh * gelu_slope(u_ref[...])).astype(BF16)
            pl.when(r == 0)(lambda: load_u(1).start())
            du_ref[rows] = du
            sums.drain(r)
            part[r] = dot(du, wup[...]).astype(BF16)
            sums.scatter(r)

        @pl.when(j == 0)
        def _():
            sums.scatter(2)

        @pl.when(j == 1)
        def _():
            sums.scatter(3)
            at_sum.exchange_y()
            feed_results(1, ff_sum.finish())
            ff_sum.release()
            write_ff_grads(
                x2,
                lambda a, b: dot_tn(second[...], du_ref[:, a:b]),
                lambda a, b: dot_tn(dxl[...], g_ref[:, a:b]),
            )
            bias_sums(0)

        return 0

    lax.fori_loop(0, 4, backward_step, 0)

    ff_sum.exchange_z()
    swap(late, late_pair, 2).wait_recv()
    late_chip[ff_sum.chip] = late[...] + late_pair[...]
    for k in HID_ORDER:
        spread(late_chip, 6, k, True).start()
    for k in HID_ORDER:
        spread(small_chip, 2, k, False).wait_recv()
    value = small_chip[0]
    for c in range(1, 8):
        value = value + small_chip[c]
    small_out[span(me * 8, 8, 8)] = value
    for k in HID_ORDER:
        small_gather(k, True).start()
    last_sum.exchange()
    time_gradient(0)
    load_time_weight(1).start()
    feed_results(0, ff_sum.finish())
    for e in range(2):
        sums.wait(2 + e)
        save_fsum(e).start()
    for k in HID_ORDER:
        spread(late_chip, 6, k, False).wait_recv()
    value = late_chip[0]
    for c in range(1, 8):
        value = value + late_chip[c]
    time_gradient(1)
    for k in HID_ORDER:
        small_gather(k, False).wait_recv()
    for l in range(LAYERS):
        for a in range(REL):
            at = (REL - 1 - a) * 32
            gtable_ref[l, a] = small_out[16 * l : 16 * l + 16, at : at + REL]
        for n in range(2):
            ggain_ref[l, n : n + 1] = small_out[32 + 2 * l + n : 33 + 2 * l + n]
            gshift_ref[l, n : n + 1] = small_out[36 + 2 * l + n : 37 + 2 * l + n]
        for n in range(4):
            gbup_out[l : l + 1, n * D : (n + 1) * D] = small_out[42 + 4 * l + n : 43 + 4 * l + n]
        gbdown_out[l : l + 1] = small_out[40 + l : 41 + l]
    ggain_ref[0, 0:1] = value[0:1]
    gshift_ref[0, 0:1] = value[1:2]
    attention_results(0, last_sum.finish())
    for k in HID_ORDER:
        small_scatter(k).wait_send()
        spread(small_chip, 2, k, True).wait_send()
        spread(late_chip, 6, k, True).wait_send()
        small_gather(k, True).wait_send()
    swap(small_sum.at[0], small_pair, 0).wait_send()
    swap(late, late_pair, 2).wait_send()
    for r in range(2):
        save_dx(r, both[r]).wait()
        save_fsum(r).wait()
    for e in range(4):
        sums.drain(e)


def layers(vmem_args, hbm_args):
    s = jax.ShapeDtypeStruct
    v = pltpu.VMEM
    dma = pltpu.SemaphoreType.DMA
    return pl.pallas_call(
        layers_kernel,
        out_shape=[
            s((2, SLOTS, D), F32),
            s((KEPT, LAYERS, 3 * D), F32),
            s((KEPT, LAYERS, 3 * D), F32),
            s((KEPT, LAYERS, D), F32),
            s((LAYERS, 72, UNITS), F32),
            s((LAYERS, 72, UNITS), F32),
            s((LAYERS, 2, D), F32),
            s((LAYERS, 2, D), F32),
            s((LAYERS, REL, HEADS, REL), F32),
            s((LAYERS, FF), F32),
            s((LAYERS, D), F32),
            s((TOKENS, D), F32),
            s((TOKENS, D), F32),
            s((2, ROW_LEN, D), BF16),
            s((LAYERS, TOKENS, 3 * D), BF16),
            s((LAYERS, 2, HEADS, ROW_LEN, ROW_LEN), BF16),
            s((LAYERS, 2, TOKENS, D), BF16),
            s((LAYERS, 2, TOKENS, 128), F32),
            s((TOKENS, D), BF16),
            s((TOKENS, UNITS), F32),
            s((TOKENS, UNITS), BF16),
        ],
        in_specs=[IN_VMEM] * len(vmem_args) + [IN_ANY] * len(hbm_args),
        out_specs=[IN_VMEM] * 11 + [IN_ANY] * 10,
        scratch_shapes=[
            v((D, 3 * D), BF16),
            v((D, D), BF16),
            v((UNITS, D), BF16),
            v((UNITS, D), BF16),
            v((HEADS, ROW_LEN, ROW_LEN), BF16),
            v((HEADS, ROW_LEN, ROW_LEN), BF16),
            v((ROW_LEN, 3 * D), BF16),
            v((2, ROW_LEN, D), BF16),
            v((2, ROW_LEN, 128), F32),
            v((D, 256), BF16),
            v((LAYERS, 2, TOKENS, 256), BF16),
            v((TOKENS, D), BF16),
            v((ROW_LEN, UNITS), F32),
            v((TOKENS, UNITS), BF16),
            v((4, ROW_LEN, D), BF16),
            v((4, ROW_LEN, D), BF16),
            v((4, HID - 1, SLICE, D), BF16),
            v((TOKENS, D), F32),
            v((TOKENS, D), BF16),
            v((TOKENS, D), BF16),
            v((ROW_LEN, D), BF16),
            v((ROW_LEN, 3 * D), F32),
            v((TOKENS, 3 * D), BF16),
            v((TOKENS, UNITS), BF16),
            v((ROW_LEN, ROW_LEN), F32),
            v((8, 2, 80, D), BF16),
            v((8, 80, D), BF16),
            v((7, 80, D), BF16),
            v((8, 64, D), BF16),
            v((7, 64, D), BF16),
            v((2, HEADS, OWN, ROW_LEN), F32),
            v((LAYERS, 8, 3 * D), F32),
            v((8, TOKENS), BF16),
            v((8, 256), BF16),
            v((64, D), F32),
            v((64, D), F32),
            v((7, 8, D), F32),
            v((1, 8, D), F32),
            v((8, D), F32),
            v((8, 8, D), F32),
            v((8, D), F32),
            v((8, D), F32),
            v((8, 8, D), F32),
            dma((19,)),
            dma((18,)),
            dma((4, 4, HID - 1)),
            dma((4,)),
            dma((4, 7)),
            pltpu.SemaphoreType.REGULAR,
            pltpu.SemaphoreType.REGULAR,
            dma((8, HID - 1)),
            dma((4,)),
        ],
        compiler_params=pltpu.CompilerParams(
            collective_id=1, has_side_effects=True, vmem_limit_bytes=VMEM_LIMIT
        ),
        name="layers",
    )(*vmem_args, *hbm_args)


def finish_kernel(bdown_ref, h_ref, fsum_ref, dx_ref, *refs):
    out_ref, grad_ref = refs[11:13]
    out_ref[...] = h_ref[...] + (fsum_ref[...].astype(F32) + bdown_ref[1:2])
    grad_ref[...] = dx_ref[...]

    @pl.when(pl.program_id(0) == 0)
    def _():
        for n in range(11):
            refs[13 + n][...] = refs[n][...]


def finish(b_down, h, fsum, dx, rest):
    s = jax.ShapeDtypeStruct
    block = pl.BlockSpec((128, D), lambda i: (i, 0))
    whole = [pl.BlockSpec(a.shape, functools.partial(lambda n, i: (0,) * n, a.ndim)) for a in rest]
    return pl.pallas_call(
        finish_kernel,
        out_shape=[s((TOKENS, D), F32)] * 2 + [s(a.shape, F32) for a in rest],
        grid=(4,),
        in_specs=[pl.BlockSpec((LAYERS, D), lambda i: (0, 0))] + [block] * 3 + whole,
        out_specs=[block] * 2 + whole,
        compiler_params=pltpu.CompilerParams(vmem_limit_bytes=VMEM_LIMIT),
        name="finish",
    )(b_down, h, fsum.reshape(TOKENS, D), dx, *rest)


def shards(
    block_in,
    time_tokens,
    layout,
    norm_gain,
    norm_bias,
    w_qkv,
    w_time,
    rel_table,
    w_out,
    w_up,
    b_up,
    w_down,
    b_down,
    cotangent,
):
    bias, tp, kind = prepare(layout, rel_table, time_tokens, w_time)
    results = layers(
        (norm_gain, norm_bias, b_up, b_down, tp, kind, time_tokens),
        (
            block_in.reshape(TOKENS, D),
            cotangent.reshape(TOKENS, D),
            w_qkv,
            w_out,
            jnp.swapaxes(w_up, 1, 2),
            w_down,
            w_time,
            bias,
        ),
    )
    dx, h, fsum = results[11:14]
    block_out, grad_in, *rest = finish(b_down, h, fsum, dx, results[:11])
    gtime, gq, gt, go, gup, gdown, ggain, gshift, gtable, gbup, gbdown = rest
    return (
        block_out.reshape(2, ROW_LEN, D),
        grad_in.reshape(2, ROW_LEN, D),
        gtime,
        ggain,
        gshift,
        jnp.swapaxes(gq, 0, 1),
        jnp.swapaxes(gt, 0, 1),
        jnp.swapaxes(gtable, 1, 2),
        jnp.swapaxes(go, 0, 1),
        gup,
        gbup,
        jnp.swapaxes(gdown, 1, 2),
        gbdown,
    )


def solution(mesh):
    in_specs = (
        P("dp", None, None),
        P("dp", None, None),
        P("dp"),
        P(),
        P(),
        P(),
        P(),
        P(),
        P(),
        P(None, None, "hid"),
        P(None, "hid"),
        P(None, "hid", None),
        P(),
        P("dp", None, None),
    )
    out_specs = (
        P("dp", None, None),
        P("dp", None, None),
        P("dp", None, None),
        P(),
        P(),
        P(None, ("dp", "hid"), None),
        P(None, ("dp", "hid"), None),
        P(),
        P(None, ("dp", "hid"), None),
        P(None, "dp", "hid"),
        P(),
        P(None, "hid", "dp"),
        P(),
    )
    return jax.shard_map(shards, mesh=mesh, in_specs=in_specs, out_specs=out_specs, check_vma=False)
```

```python
import functools

import jax
import jax.numpy as jnp
from jax import lax
from jax.experimental import pallas as pl
from jax.experimental.pallas import tpu as pltpu
from jax.sharding import PartitionSpec as P

D = 1152
HEADS = 16
HEAD_DIM = 72
FF = 4608
LAYERS = 2
GRID = 16
SUB = 8
ROW_LEN = 256
SLOTS = 4
REL = 31
DP = 16
HID = 8
UNITS = FF // HID
KEPT = D // (DP * HID)
TOKENS = 512
OWN = ROW_LEN // HID
SCALE = HEAD_DIM ** (-0.5)
MASKED_LOGIT = -1e30
NORM_EPSILON = 1e-06
F32 = jnp.float32
BF16 = jnp.bfloat16
MESH = pl.DeviceIdType.MESH
VMEM_LIMIT = 63 * 1024 * 1024
HIGHEST = lax.Precision.HIGHEST


def contract(a, b, da, db, precision=None):
    return lax.dot_general(
        a, b, (((da,), (db,)), ((), ())), preferred_element_type=F32, precision=precision
    )


def dot(a, b):
    return contract(a, b, 1, 0)


def dot_nt(a, b):
    return contract(a, b, 1, 1)


def dot_tn(a, b):
    return contract(a, b, 0, 0)


def span(start, size, multiple):
    return pl.ds(pl.multiple_of(start, multiple), size)


def gelu_parts(v):
    c = 0.7978845608028654
    square = v * v
    t = jnp.tanh(c * v * (1.0 + 0.044715 * square))
    return t, square


def gelu(v):
    t, _ = gelu_parts(v)
    return 0.5 * v * (1.0 + t)


def gelu_slope(v):
    c = 0.7978845608028654
    t, square = gelu_parts(v)
    return 0.5 * (1.0 + t) + 0.5 * v * (1.0 - t * t) * (c * (1.0 + 3.0 * 0.044715 * square))


def prepare_kernel(
    layout_ref, rel_ref, time_ref, wtime_ref, bias_ref, tp_ref, kind_ref, rows_ref, skew_ref, turned_ref
):
    g = pl.program_id(1)
    first, second = layout_ref[0], layout_ref[1]

    @pl.when(g == 0)
    def _():
        tp_ref[...] = jnp.zeros_like(tp_ref)
        for r in range(2):
            four = jnp.where(layout_ref[r] == 1, 1.0, 0.0)
            kind_ref[r, 0:1] = jnp.full((1, ROW_LEN), 1.0 - four, F32)
            kind_ref[r, 1:2] = jnp.full((1, ROW_LEN), four, F32)

    @pl.when(g < 3)
    def _():
        cols = span(384 * g, 384, 128)
        tokens = [time_ref[r, :, cols].astype(F32) for r in range(2)]
        tp_ref[0] += dot(jnp.concatenate(tokens, axis=0).astype(BF16), wtime_ref[0])

    @pl.when(g == 3)
    def _():
        for r in range(2):

            @pl.when(layout_ref[r] != 1)
            def _():
                tp_ref[0, 4 * r : 4 * r + 4] = jnp.broadcast_to(
                    tp_ref[0, 4 * r : 4 * r + 1], (SLOTS, 3 * D)
                )

    rows_ref[...] = jnp.zeros_like(rows_ref)
    rows_ref[:, 0:4, 0:REL] = rel_ref[0, :, pl.ds(4 * g, 4), :]
    table = rows_ref[:, 0]
    for i in range(1, 4):
        table = table + pltpu.roll(rows_ref[:, i], 32 * i, 1)

    def skewed(side, count, top):
        skew_ref[...] = jnp.zeros_like(skew_ref)
        for j in range(count):
            block = jnp.broadcast_to(table[top - j : top - j + 1], (side, 128))
            skew_ref[pl.ds(side * j, side)] = pltpu.roll(
                block, 113, 1, stride=1, stride_axis=0
            )

    def single(r):
        skewed(GRID, REL, REL - 1)
        turned_ref[...] = skew_ref[...].T
        for i in range(4):
            w = turned_ref[32 * i : 32 * i + GRID]
            for m in range(8):
                moved = w if m == 0 else pltpu.roll(w, 512 - 16 * m, 1)
                for t in range(2):
                    y = 15 - 8 * t - m
                    bias_ref[0, r, i, pl.ds(GRID * y, GRID), :] = moved[
                        :, 128 * t : 128 * t + ROW_LEN
                    ].astype(BF16)

    def quad(r):
        skewed(SUB, 15, 22)
        turned_ref[:, 0:128] = skew_ref[0:128].T
        half = lax.broadcasted_iota(jnp.int32, (2 * SUB, 128), 1) // 64
        closed = jnp.full((2 * SUB, 128), MASKED_LOGIT, F32).astype(BF16)
        for i in range(4):
            w = turned_ref[32 * i : 32 * i + SUB, 0:128]
            for y in range(0, SUB, 2):
                for odd in range(2):
                    moved = jnp.concatenate(
                        [
                            pltpu.roll(w, (128 + 64 * odd - (7 - y - n) * SUB) % 128, 1)
                            for n in range(2)
                        ],
                        axis=0,
                    )
                    moved = jnp.where(half == odd, moved, MASKED_LOGIT).astype(BF16)
                    for tile in range(2):
                        rows = pl.ds(64 * (2 * tile + odd) + SUB * y, 2 * SUB)
                        bias_ref[0, r, i, rows, 128 * tile : 128 * tile + 128] = moved
                        bias_ref[0, r, i, rows, 128 - 128 * tile : 256 - 128 * tile] = closed

    pl.when(first != 1)(lambda: single(0))
    pl.when(first == 1)(lambda: quad(0))

    @pl.when(first == second)
    def _():
        for i in range(4):
            bias_ref[0, 1, i] = bias_ref[0, 0, i]

    pl.when((first != second) & (second != 1))(lambda: single(1))
    pl.when((first != second) & (second == 1))(lambda: quad(1))


def prepare(layout, rel_table, time_tokens, w_time):
    return pl.pallas_call(
        prepare_kernel,
        out_shape=[
            jax.ShapeDtypeStruct((LAYERS, 2, HEADS, ROW_LEN, ROW_LEN), BF16),
            jax.ShapeDtypeStruct((LAYERS, 8, 3 * D), F32),
            jax.ShapeDtypeStruct((2, 2, ROW_LEN), F32),
        ],
        grid_spec=pltpu.PrefetchScalarGridSpec(
            num_scalar_prefetch=1,
            grid=(LAYERS, 4),
            in_specs=[
                pl.BlockSpec((1, REL, HEADS, REL), lambda l, g, _: (l, 0, 0, 0)),
                pl.BlockSpec((2, SLOTS, D), lambda l, g, _: (0, 0, 0)),
                pl.BlockSpec((1, 384, 3 * D), lambda l, g, _: (l, jnp.minimum(g, 2), 0)),
            ],
            out_specs=[
                pl.BlockSpec((1, 2, 4, ROW_LEN, ROW_LEN), lambda l, g, _: (l, 0, g, 0, 0)),
                pl.BlockSpec((1, 8, 3 * D), lambda l, g, _: (l, 0, 0)),
                pl.BlockSpec((2, 2, ROW_LEN), lambda l, g, _: (0, 0, 0)),
            ],
            scratch_shapes=[
                pltpu.VMEM((REL, 8, 128), F32),
                pltpu.VMEM((512, 128), F32),
                pltpu.VMEM((128, 512), F32),
            ],
        ),
        compiler_params=pltpu.CompilerParams(vmem_limit_bytes=VMEM_LIMIT),
        name="prepare",
    )(layout, jnp.swapaxes(rel_table, 1, 2), time_tokens, w_time)


IN_VMEM = pl.BlockSpec(memory_space=pltpu.VMEM)
IN_ANY = pl.BlockSpec(memory_space=pl.ANY)
CHUNK = 128
HID_ORDER = (2, 6, 1, 4, 3, 7, 5)
SLICE = ROW_LEN // HID


def head_window(h):
    start = h * HEAD_DIM // 128 * 128
    offset = h * HEAD_DIM - start
    width = 128 if offset + HEAD_DIM <= 128 else 256
    lane = lax.broadcasted_iota(jnp.int32, (1, width), 1)
    mask = ((lane >= offset) & (lane < offset + HEAD_DIM)).astype(F32).astype(BF16)
    return start, width, mask


def hid_peer(me, k):
    return lax.rem(me // 2 + k // 2, 4) * 2 + lax.rem(me + k, 2)


def hid_source(me, k):
    return lax.rem(me // 2 + 4 - k // 2, 4) * 2 + lax.rem(me + k, 2)


def greet_hid(barrier, me):
    for k in HID_ORDER:
        pl.semaphore_signal(
            barrier, inc=1, device_id={"hid": hid_peer(me, k)}, device_id_type=MESH
        )


class HidSums:
    def __init__(self, part, recv, total, sems):
        self.part, self.recv, self.total = part, recv, total
        self.send1, self.recv1, self.send2, self.recv2 = sems
        self.me = lax.axis_index("hid")

    def scatter_copy(self, e, k):
        peer = hid_peer(self.me, k)
        return pltpu.make_async_remote_copy(
            src_ref=self.part.at[e, span(peer * SLICE, SLICE, SLICE)],
            dst_ref=self.recv.at[e, k - 1],
            send_sem=self.send1.at[e, k - 1],
            recv_sem=self.recv1.at[e, k - 1],
            device_id={"hid": peer},
            device_id_type=MESH,
        )

    def gather_copy(self, slot, e, k, outgoing):
        owner = self.me if outgoing else hid_source(self.me, k)
        rows = self.total.at[slot, span(owner * SLICE, SLICE, SLICE)]
        return pltpu.make_async_remote_copy(
            src_ref=rows,
            dst_ref=rows,
            send_sem=self.send2.at[e, k - 1],
            recv_sem=self.recv2.at[e, k - 1],
            device_id={"hid": hid_peer(self.me, k)},
            device_id_type=MESH,
        )

    def scatter(self, e):
        for k in HID_ORDER:
            self.scatter_copy(e, k).start()

    def add_and_gather(self, e):
        mine = span(self.me * SLICE, SLICE, SLICE)
        for k in HID_ORDER:
            self.scatter_copy(e, k).wait_recv()
        total = self.part[e, mine].astype(F32)
        for k in range(HID - 1):
            total = total + self.recv[e, k].astype(F32)
        self.total[e, mine] = total.astype(BF16)
        for k in HID_ORDER:
            self.gather_copy(e, e, k, True).start()

    def wait(self, e):
        for k in HID_ORDER:
            self.gather_copy(e, e, k, False).wait_recv()

    def drain(self, e):
        for k in HID_ORDER:
            self.scatter_copy(e, k).wait_send()
            self.gather_copy(e, e, k, True).wait_send()


def write_ff_grads(ffg, up_of, down_of):
    for n, of in enumerate((up_of, down_of)):
        for a, b in ((0, 128), (128, 256), (256, 384), (384, 512), (512, UNITS)):
            grad = of(a, b)
            for c in range(DP):
                ffg[c // 2, c % 2, 0:72, n * UNITS + a : n * UNITS + b] = grad[
                    72 * c : 72 * (c + 1)
                ].astype(BF16)


def layer_norm_rows(x, gain, shift):
    centre = x - jnp.mean(x, -1, keepdims=True)
    inverse = lax.rsqrt(jnp.mean(centre * centre, -1, keepdims=True) + NORM_EPSILON)
    unit = centre * inverse
    return (unit * gain + shift).astype(BF16), unit.astype(BF16), inverse


def kept_matrix():
    feature = lax.broadcasted_iota(jnp.int32, (D, 256), 0)
    column = lax.broadcasted_iota(jnp.int32, (D, 256), 1)
    low = column < 128
    owner = jnp.where(low, column // 8, column - 128)
    inner = jnp.where(low, column % 8, 8)
    chosen = (feature == owner * 72 + lax.axis_index("hid") * KEPT + inner) & (column < 144)
    return chosen.astype(F32).astype(BF16)


def attend_forward(qkv, bias_ref, p_ref, o_acc):
    o_acc[:, 0:D] = jnp.zeros((ROW_LEN, D), F32)

    def scores(h):
        start, width, mask = head_window(h)
        q = qkv[:, start : start + width] * mask
        return dot_nt(q, qkv[:, D + start : D + start + width])

    def mix(h, score):
        start, width, mask = head_window(h)
        logits = score * SCALE + bias_ref[h].astype(F32)
        expo = jnp.exp(logits - jnp.max(logits, -1, keepdims=True))
        p = (expo * (1.0 / jnp.sum(expo, -1, keepdims=True))).astype(BF16)
        p_ref[h] = p
        v = qkv[:, 2 * D + start : 2 * D + start + width] * mask
        o_acc[:, start : start + width] += dot(p, v)

    ready = {}
    for h in range(HEADS + 1):
        if h < HEADS:
            ready[h] = scores(h)
        if h:
            mix(h - 1, ready.pop(h - 1))


class DpSums:
    def __init__(self, x, pair, recv, sems, free):
        self.x, self.pair, self.recv, self.free = x, pair, recv, free
        self.pair_send, self.pair_recv, self.send, self.got = sems
        me = lax.axis_index("dp")
        self.y, self.z, self.core = me // 4, lax.rem(me // 2, 2), lax.rem(me, 2)
        self.chip = me // 2
        self.partner = self.chip * 2 + (1 - self.core)

    def other(self, k):
        return lax.rem(self.y + k // 2, 4) * 2 + lax.rem(self.z + k, 2)

    def peer(self, k):
        return {"dp": self.other(k) * 2 + self.core}

    def pair_copy(self):
        return pltpu.make_async_remote_copy(
            src_ref=self.x.at[:, 1 - self.core],
            dst_ref=self.pair,
            send_sem=self.pair_send,
            recv_sem=self.pair_recv,
            device_id={"dp": self.partner},
            device_id_type=MESH,
        )

    def start(self):
        self.pair_copy().start()

    def add_pair(self, c):
        both = self.x[c, self.core].astype(F32) + self.pair[c].astype(F32)
        self.pair[c] = both.astype(BF16)

    def release(self):
        pl.semaphore_signal(
            self.free, inc=1, device_id={"dp": self.partner}, device_id_type=MESH
        )
        for k in HID_ORDER:
            pl.semaphore_signal(self.free, inc=1, device_id=self.peer(k), device_id_type=MESH)

    def acquire(self):
        pl.semaphore_wait(self.free, 8)


class DirectSums(DpSums):
    def chip_copy(self, k):
        return pltpu.make_async_remote_copy(
            src_ref=self.pair.at[self.other(k)],
            dst_ref=self.recv.at[k - 1],
            send_sem=self.send.at[k - 1],
            recv_sem=self.got.at[k - 1],
            device_id=self.peer(k),
            device_id_type=MESH,
        )

    def exchange(self):
        self.pair_copy().wait_recv()
        for k in HID_ORDER + (0,):
            self.add_pair(self.other(k))
            if k:
                self.chip_copy(k).start()
        self.pair_copy().wait_send()

    def finish(self):
        total = self.pair[self.chip].astype(F32)
        for k in HID_ORDER:
            self.chip_copy(k).wait_recv()
            total = total + self.recv[k - 1].astype(F32)
        for k in HID_ORDER:
            self.chip_copy(k).wait_send()
        return total


class SteppedSums(DpSums):
    def y_copy(self, k):
        target = lax.rem(self.y + k, 4)
        return pltpu.make_async_remote_copy(
            src_ref=self.pair.at[pl.ds(2 * target, 2)],
            dst_ref=self.recv.at[pl.ds(2 * k - 2, 2)],
            send_sem=self.send.at[k - 1],
            recv_sem=self.got.at[k - 1],
            device_id=self.peer(2 * k),
            device_id_type=MESH,
        )

    def z_copy(self):
        return pltpu.make_async_remote_copy(
            src_ref=self.pair.at[2 * self.y + 1 - self.z],
            dst_ref=self.recv.at[6],
            send_sem=self.send.at[3],
            recv_sem=self.got.at[3],
            device_id=self.peer(1),
            device_id_type=MESH,
        )

    def exchange_y(self):
        self.pair_copy().wait_recv()
        for k in (2, 1, 3, 0):
            target = lax.rem(self.y + k, 4)
            for z in range(2):
                self.add_pair(2 * target + z)
            if k:
                self.y_copy(k).start()
        self.pair_copy().wait_send()

    def exchange_z(self):
        for k in (1, 3, 2):
            self.y_copy(k).wait_recv()
        for own in (False, True):
            z = self.z if own else 1 - self.z
            c = 2 * self.y + z
            block = self.pair[c].astype(F32)
            for k in (1, 2, 3):
                block = block + self.recv[2 * k - 2 + z].astype(F32)
            self.pair[c] = block.astype(BF16)
            if not own:
                self.z_copy().start()

    def finish(self):
        self.z_copy().wait_recv()
        total = self.pair[self.chip].astype(F32) + self.recv[6].astype(F32)
        for k in (1, 2, 3):
            self.y_copy(k).wait_send()
        self.z_copy().wait_send()
        return total


def norm_slope(dn, unit, inverse, gain):
    scaled = dn * gain
    return inverse * (
        scaled
        - jnp.mean(scaled, -1, keepdims=True)
        - unit * jnp.mean(scaled * unit, -1, keepdims=True)
    )


def attend_backward(qkv, r, do_ref, p_ref, acc, ds_ref, fold, kind_ref, own_first):
    acc[...] = jnp.zeros_like(acc)

    def slopes(h):
        start, width, mask = head_window(h)
        v = qkv[:, 2 * D + start : 2 * D + start + width] * mask
        return dot_nt(do_ref[:, start : start + width], v)

    def spread(h, dp):
        start, width, mask = head_window(h)
        p_low = p_ref[h]
        p = p_low.astype(F32)
        t = p * dp
        ds = t - p * jnp.sum(t, -1, keepdims=True)
        ds_ref[...] = ds
        low = ds.astype(BF16)
        k = qkv[:, D + start : D + start + width] * mask
        q = qkv[:, start : start + width] * mask
        do = do_ref[:, start : start + width] * mask
        acc[:, start : start + width] += dot(low, k)
        acc[:, D + start : D + start + width] += dot_tn(low, q)
        acc[:, 2 * D + start : 2 * D + start + width] += dot_tn(p_low, do)
        mine = ds_ref[span(own_first, OWN, OWN)]
        fold[0, h] += mine * kind_ref[r, 0:1]
        fold[1, h] += mine * kind_ref[r, 1:2]

    ready = {}
    depth = 2
    for h in range(HEADS + depth):
        if h < HEADS:
            ready[h] = slopes(h)
        if h >= depth:
            spread(h - depth, ready.pop(h - depth))


def two_part_dot(a, b):
    high = a.astype(BF16)
    low = (a - high.astype(F32)).astype(BF16)
    return dot(high, b) + dot(low, b)


def fold_tables(fold, me):
    lane = lax.broadcasted_iota(jnp.int32, (ROW_LEN, 512), 0)
    place = lax.broadcasted_iota(jnp.int32, (ROW_LEN, 512), 1)
    wide = (place == (lane // GRID) * 32 + 15 - lane % GRID).astype(F32).astype(BF16)
    inner = lane % (SUB * SUB)
    narrow = (place == (inner // SUB) * 32 + 15 - inner % SUB).astype(F32).astype(BF16)
    rest = jnp.zeros((HEADS, 512), F32)
    out = jnp.zeros((HEADS, 1024), F32)
    for kind, (side, chosen) in enumerate(((GRID, wide), (SUB, narrow))):
        lines = []
        for n in range(2):
            sums = fold[kind, 8 * n : 8 * (n + 1)].reshape(8 * OWN, ROW_LEN)
            wider = two_part_dot(sums, chosen).reshape(8 * OWN // side, side, 512)
            line = wider[:, 0]
            for x in range(1, side):
                line = line + pltpu.roll(wider[:, x], x, 1)
            lines.append(line.reshape(8, OWN // side, 512))
        for i in range(OWN // side):
            line = jnp.concatenate([part[:, i] for part in lines], axis=0)
            y = 2 * me + i if side == GRID else lax.rem(me, 2) * 4 + i
            out = out + pltpu.roll(
                jnp.concatenate([line, rest], axis=1), (15 - y) * 32, 1
            )
    return out


def layers_kernel(
    gain_ref,
    shift_ref,
    bup_ref,
    bdown_ref,
    tp_ref,
    kind_ref,
    time_ref,
    x_hbm,
    cot_hbm,
    wqkv_hbm,
    wout_hbm,
    wup_hbm,
    wdown_hbm,
    wtime_hbm,
    bias_hbm,
    gtime_ref,
    gq_ref,
    gt_ref,
    go_ref,
    gup_ref,
    gdown_ref,
    ggain_ref,
    gshift_ref,
    gtable_ref,
    gbup_out,
    gbdown_out,
    dx_hbm,
    h_hbm,
    fsum_hbm,
    qkv_hbm,
    p_hbm,
    unit_hbm,
    inv_hbm,
    second_hbm,
    u_hbm,
    g_hbm,
    wqkv,
    wout,
    wup,
    wdown,
    bias_ref,
    p_ref,
    qkv,
    unit,
    inv,
    keep_ref,
    kept,
    second,
    u_ref,
    g_ref,
    total,
    part,
    recv,
    dy,
    dhl,
    dxl,
    do_ref,
    acc,
    dqkv,
    du_ref,
    ds_ref,
    x2,
    pair2,
    recv2,
    pair3,
    recv3,
    fold,
    dproj,
    pick_ref,
    timek_ref,
    small,
    small_out,
    small_recv,
    small_sum,
    small_pair,
    small_chip,
    late,
    late_pair,
    late_chip,
    load_sem,
    save_sem,
    hid_sems,
    dp_sems,
    chip_sems,
    free2,
    free3,
    small_sems,
    small_one,
):
    me = lax.axis_index("hid")
    own_first = me * OWN
    mine = span(own_first, OWN, OWN)
    sums = HidSums(part, recv, total, tuple(hid_sems.at[n] for n in range(4)))
    ff_sum = SteppedSums(
        x2,
        pair2,
        recv2,
        (dp_sems.at[0], dp_sems.at[1], chip_sems.at[0], chip_sems.at[1]),
        free2,
    )
    at_sum, last_sum = (
        kind(
            x2.at[:, :, pl.ds(0, 64)],
            pair3,
            recv3,
            (dp_sems.at[2], dp_sems.at[3], chip_sems.at[2], chip_sems.at[3]),
            free3,
        )
        for kind in (SteppedSums, DirectSums)
    )

    def load(n, src, dst):
        return pltpu.make_async_copy(src, dst, load_sem.at[n])

    def save(n, src, dst):
        return pltpu.make_async_copy(src, dst, save_sem.at[n])

    def load_weight(l, n):
        cols = pl.ds(n * D, D)
        return load(n, wqkv_hbm.at[l, :, cols], wqkv.at[:, cols])

    def load_time_weight(l):
        return load(3, wtime_hbm.at[l], wqkv)

    def load_out(l):
        return load(4, wout_hbm.at[l], wout)

    def load_feed_weights(l):
        return [load(5, wup_hbm.at[l], wup), load(6, wdown_hbm.at[l], wdown)]

    def load_bias(i):
        return load(7, bias_hbm.at[i // 2, lax.rem(i, 2)], bias_ref)

    def load_x():
        return load(8, x_hbm, dhl)

    def load_cot():
        return load(9, cot_hbm, dxl)

    def place_of(j):
        return 1 - j // 2, span(lax.rem(j, 2) * ROW_LEN, ROW_LEN, ROW_LEN)

    def load_p(j):
        return load(10, p_hbm.at[1 - j // 2, lax.rem(j, 2)], p_ref)

    def load_qkv(j):
        l, rows = place_of(j)
        return load(11, qkv_hbm.at[l, rows], qkv)

    def load_norm(which, j):
        l, rows = place_of(j)
        return [
            load(12 + 2 * which, unit_hbm.at[l, which, rows], unit.at[which]),
            load(13 + 2 * which, inv_hbm.at[l, which, rows], inv.at[which]),
        ]

    def load_u(r):
        return load(16, u_hbm.at[span(r * ROW_LEN, ROW_LEN, ROW_LEN)], u_ref)

    def load_feed():
        return [load(17, second_hbm, second), load(18, g_hbm, g_ref)]

    def save_qkv(l, rows):
        return save(0, qkv, qkv_hbm.at[l, rows])

    def save_p(l, r):
        return save(1, p_ref, p_hbm.at[l, r])

    def save_norm(which, l, rows):
        return [
            save(2 + 2 * which, unit.at[which], unit_hbm.at[l, which, rows]),
            save(3 + 2 * which, inv.at[which], inv_hbm.at[l, which, rows]),
        ]

    def save_u(r, rows):
        return save(10 + r, u_ref, u_hbm.at[rows])

    def save_feed(r, rows):
        return [
            save(6 + r, second.at[rows], second_hbm.at[rows]),
            save(8 + r, g_ref.at[rows], g_hbm.at[rows]),
        ]

    def save_h(r, rows):
        return save(12 + r, dy.at[rows], h_hbm.at[rows])

    def save_dx(r, rows):
        return save(14 + r, dy.at[rows], dx_hbm.at[rows])

    def save_fsum(r):
        return save(16 + r, total.at[2 + r], fsum_hbm.at[r])

    load_x().start()
    for n in range(3):
        load_weight(0, n).start()
    load_bias(0).start()
    load_out(0).start()
    for copy in load_feed_weights(0):
        copy.start()
    load_cot().start()
    barrier = pltpu.get_barrier_semaphore()
    greet_hid(barrier, me)
    pl.semaphore_signal(
        barrier, inc=1, device_id={"dp": ff_sum.partner}, device_id_type=MESH
    )
    for k in HID_ORDER:
        pl.semaphore_signal(barrier, inc=1, device_id=ff_sum.peer(k), device_id_type=MESH)
    small[...] = jnp.zeros_like(small)
    late[...] = jnp.zeros_like(late)
    gtime_ref[...] = jnp.zeros_like(gtime_ref)
    keep_ref[...] = kept_matrix()
    tokens = [time_ref[r].astype(F32) for r in range(2)]
    timek_ref[...] = dot(
        jnp.concatenate(tokens, axis=0).astype(BF16), keep_ref[...]
    ).astype(BF16)
    quarter = lax.broadcasted_iota(jnp.int32, (8, ROW_LEN), 1) // 64
    owner = lax.broadcasted_iota(jnp.int32, (8, ROW_LEN), 0)
    for r in range(2):
        whole = (owner == 4 * r).astype(F32) * kind_ref[r, 0:1]
        parts = (owner == 4 * r + quarter).astype(F32) * kind_ref[r, 1:2]
        pick_ref[:, pl.ds(r * ROW_LEN, ROW_LEN)] = (whole + parts).astype(BF16)
    load_x().wait()
    pl.semaphore_wait(barrier, 15)

    def keep_features(l):
        for n in range(2):
            kept[l, n] = dot(dqkv[:, n * D : (n + 1) * D], keep_ref[...]).astype(BF16)

    def forward_step(i, _):
        l = i // 2
        r = lax.rem(i, 2)
        base = r * ROW_LEN
        rows = span(base, ROW_LEN, ROW_LEN)

        @pl.when(i > 0)
        def _():
            for which in range(2):
                for copy in save_norm(which, 0, rows):
                    copy.wait()
            save_qkv(0, rows).wait()

        @pl.when(l == 0)
        def _():
            dy[rows] = dhl[rows].astype(F32)

        @pl.when(l == 1)
        def _():
            pl.when(r == 0)(lambda: keep_features(0))
            for copy in save_feed(r, rows):
                copy.wait()
            sums.wait(r)
            dy[rows] = dy[rows] + (total[r].astype(F32) + bdown_ref[0:1])

        def norm(which):
            def body(c, _):
                here = span(c * CHUNK, CHUNK, CHUNK)
                rr = span(base + c * CHUNK, CHUNK, CHUNK)
                low, value, inverse = layer_norm_rows(
                    dy[rr], gain_ref[l, which : which + 1], shift_ref[l, which : which + 1]
                )
                if which == 0:
                    dqkv[rr, 0:D] = low
                else:
                    second[rr] = low
                unit[which, here] = value
                inv[which, here] = jnp.broadcast_to(inverse, (CHUNK, 128))
                return 0

            lax.fori_loop(0, ROW_LEN // CHUNK, body, 0)
            for copy in save_norm(which, l, rows):
                copy.start()

        norm(0)
        for n in range(3):

            @pl.when(r == 0)
            def _():
                load_weight(l, n).wait()

            cols = pl.ds(n * D, D)
            wide = dot(dqkv[rows, 0:D], wqkv[:, cols])
            for s in range(SLOTS):
                qkv[64 * s : 64 * (s + 1), cols] = (
                    wide[64 * s : 64 * (s + 1)] + tp_ref[l, pl.ds(4 * r + s, 1), cols]
                ).astype(BF16)

        @pl.when(i == 2)
        def _():
            sums.add_and_gather(1)

        save_qkv(l, rows).start()

        @pl.when(i == 1)
        def _():
            for n in range(3):
                load_weight(1, n).start()

        load_bias(i).wait()

        @pl.when(i > 0)
        def _():
            save_p(0, 0).wait()

        attend_forward(qkv, bias_ref, p_ref, acc)

        @pl.when((i == 1) | (i == 3))
        def _():
            sums.add_and_gather(0)

        save_p(l, r).start()

        @pl.when(i < 3)
        def _():
            load_bias(i + 1).start()

        dqkv[rows, D : 2 * D] = acc[:, 0:D].astype(BF16)

        @pl.when(r == 0)
        def _():
            load_out(l).wait()

        dy[rows] = dy[rows] + dot(dqkv[rows, D : 2 * D], wout[...])

        @pl.when(i == 1)
        def _():
            load_out(1).start()

        norm(1)

        @pl.when(r == 0)
        def _():
            for copy in load_feed_weights(l):
                copy.wait()

        @pl.when((i == 1) | (i == 2))
        def _():
            save_u(i - 1, pl.ds(0, ROW_LEN)).wait()

        u_ref[...] = dot_nt(second[rows], wup[...]) + bup_ref[pl.ds(l, 1)]
        g_ref[rows] = gelu(u_ref[...]).astype(BF16)

        @pl.when(l == 0)
        def _():
            part[r] = dot(g_ref[rows], wdown[...]).astype(BF16)
            sums.scatter(r)
            for copy in save_feed(r, rows):
                copy.start()
            save_u(r, rows).start()

        @pl.when(l == 1)
        def _():
            pl.when(r == 0)(lambda: load_cot().wait())
            gh = dot_nt(dxl[rows], wdown[...])
            du = (gh * gelu_slope(u_ref[...])).astype(BF16)
            du_ref[rows] = du
            sums.drain(r)
            part[r] = dot(du, wup[...]).astype(BF16)
            sums.scatter(r)
            save_h(r, rows).start()
            part[2 + r] = dot(g_ref[rows], wdown[...]).astype(BF16)

        @pl.when(i == 1)
        def _():
            for copy in load_feed_weights(1):
                copy.start()

        return 0

    lax.fori_loop(0, 4, forward_step, 0)

    both = pl.ds(0, ROW_LEN), pl.ds(ROW_LEN, ROW_LEN)
    save_p(0, 0).wait()
    load_p(0).start()
    save_qkv(0, both[1]).wait()
    load_qkv(0).start()
    for which in (1, 0):
        for copy in save_norm(which, 0, both[1]):
            copy.wait()
        for copy in load_norm(which, 0):
            copy.start()
    for copy in load_feed_weights(0):
        copy.start()
    load_u(0).start()
    write_ff_grads(
        x2,
        lambda a, b: dot_tn(second[...], du_ref[:, a:b]),
        lambda a, b: dot_tn(dxl[...], g_ref[:, a:b]),
    )
    ff_sum.start()
    for copy in load_feed():
        copy.start()
    keep_features(1)

    def bias_sums(l):
        odd = lax.rem(me, 2).astype(F32)
        value = jnp.sum(du_ref[...].astype(F32), 0, keepdims=True)
        small[pl.ds(42 + 4 * l + me // 2, 1)] = jnp.concatenate(
            [value * (1.0 - odd), value * odd], axis=1
        )
        for r in range(2):
            small[40 + l : 41 + l] += jnp.sum(
                dxl[span(r * ROW_LEN + own_first, OWN, OWN)].astype(F32), 0, keepdims=True
            )

    bias_sums(1)

    def attention_results(l, block):
        for j in range(KEPT):
            for n in range(7):
                at = 8 * n + j if j < 8 else 56 + n
                ref = gq_ref if n < 3 else gt_ref if n < 6 else go_ref
                ref[j, l : l + 1, pl.ds(n % 3 * D, D)] = block[at : at + 1]

    def feed_results(l, block):
        gup_ref[l] = block[0:72, 0:UNITS]
        gdown_ref[l] = block[0:72, UNITS : 2 * UNITS]

    def place(p, grad):
        half = lax.rem(p, 2)
        for c in range(DP):
            acc[span(16 * c + 8 * half, 8, 8), 0:D] = grad[8 * c : 8 * c + 8]
            acc[pl.ds(8 * c + p, 1), D : 2 * D] = grad[128 + c : 129 + c]

    def flush(pair):
        for c in range(DP):
            x2[c // 2, c % 2, span(16 * pair, 16, 16)] = acc[
                16 * c : 16 * (c + 1), 0:D
            ].astype(BF16)

    def attention_weights(l):
        acc[0:128, D : 2 * D] = jnp.zeros((128, D), F32)

        def project(n, _):
            cols = span(n * D, D, 128)
            dproj[l, :, cols] = dot(pick_ref[...], dqkv[:, cols])
            return 0

        lax.fori_loop(0, 3, project, 0)

        def token_piece(n, _):
            cols = span(n * D, D, 128)
            place(n, dot_tn(kept[l, 0, :, 0:144], dqkv[:, cols]))
            pl.when(n == 1)(lambda: flush(0))
            return 0

        lax.fori_loop(0, 3, token_piece, 0)

        def time_piece(n, _):
            cols = span(n * D, D, 128)
            place(3 + n, dot_tn(timek_ref[:, 0:144], dproj[l, :, cols].astype(BF16)))
            pl.when(n == 0)(lambda: flush(1))
            pl.when(n == 2)(lambda: flush(2))
            return 0

        lax.fori_loop(0, 3, time_piece, 0)
        place(6, dot_tn(kept[l, 1, :, 0:144], dhl[...]))
        for c in range(DP):
            acc[16 * c + 8 : 16 * c + 16, 0:D] = acc[8 * c : 8 * c + 8, D : 2 * D]
        flush(3)
        small[span(l * 16, 16, 16), 0:1024] = fold_tables(fold, me)

    def time_gradient(l):
        load_time_weight(l).wait()
        got = jnp.zeros((8, D), F32)
        for n in range(3):
            cols = pl.ds(n * D, D)
            got = got + dot_nt(dproj[l, :, cols].astype(BF16), wqkv[:, cols])
        for r in range(2):
            gtime_ref[r] += got[4 * r : 4 * r + 4]

    def small_scatter(k):
        peer = hid_peer(me, k)
        return pltpu.make_async_remote_copy(
            src_ref=small.at[span(peer * 8, 8, 8)],
            dst_ref=small_recv.at[k - 1],
            send_sem=small_sems.at[0, k - 1],
            recv_sem=small_sems.at[1, k - 1],
            device_id={"hid": peer},
            device_id_type=MESH,
        )

    def swap(src, dst, n):
        return pltpu.make_async_remote_copy(
            src_ref=src,
            dst_ref=dst,
            send_sem=small_one.at[n],
            recv_sem=small_one.at[n + 1],
            device_id={"dp": ff_sum.partner},
            device_id_type=MESH,
        )

    def spread(ref, n, k, outgoing):
        chip = ff_sum.chip
        if not outgoing:
            chip = lax.rem(ff_sum.y + 4 - k // 2, 4) * 2 + lax.rem(ff_sum.z + k, 2)
        return pltpu.make_async_remote_copy(
            src_ref=ref.at[chip],
            dst_ref=ref.at[chip],
            send_sem=small_sems.at[n, k - 1],
            recv_sem=small_sems.at[n + 1, k - 1],
            device_id=ff_sum.peer(k),
            device_id_type=MESH,
        )

    def small_gather(k, outgoing):
        owner = me if outgoing else hid_source(me, k)
        rows = small_out.at[span(owner * 8, 8, 8)]
        return pltpu.make_async_remote_copy(
            src_ref=rows,
            dst_ref=rows,
            send_sem=small_sems.at[4, k - 1],
            recv_sem=small_sems.at[5, k - 1],
            device_id={"hid": hid_peer(me, k)},
            device_id_type=MESH,
        )

    def backward_step(j, _):
        l = 1 - j // 2
        r = lax.rem(j, 2)
        base = r * ROW_LEN
        rows = span(base, ROW_LEN, ROW_LEN)
        more = j < 3

        for copy in load_norm(1, j):
            copy.wait()
        sums.wait(r)

        @pl.when(l == 1)
        def _():
            save_h(r, rows).wait()
            dy[rows] = dxl[rows].astype(F32)

        @pl.when(r == 0)
        def _():
            fold[...] = jnp.zeros_like(fold)

        def second_norm(c, _):
            here = span(c * CHUNK, CHUNK, CHUNK)
            rr = span(base + c * CHUNK, CHUNK, CHUNK)
            dn = total[r, here].astype(F32)
            dh = dy[rr] + norm_slope(
                dn, unit[1, here].astype(F32), inv[1, here, 0:1], gain_ref[l, 1:2]
            )
            dy[rr] = dh
            dhl[rr] = dh.astype(BF16)
            return 0

        lax.fori_loop(0, ROW_LEN // CHUNK, second_norm, 0)

        def norm_sums(which, dn):
            value = jnp.sum(dn * unit[which, mine].astype(F32), 0, keepdims=True)
            small[pl.ds(32 + 2 * l + which, 1)] += value
            small[pl.ds(36 + 2 * l + which, 1)] += jnp.sum(dn, 0, keepdims=True)

        norm_sums(1, total[r, mine].astype(F32))

        @pl.when(more)
        def _():
            for copy in load_norm(1, j + 1):
                copy.start()

        @pl.when(j == 2)
        def _():
            load_out(0).wait()

        do_ref[...] = dot_nt(dhl[rows], wout[...]).astype(BF16)

        @pl.when(j == 1)
        def _():
            load_out(0).start()

        load_qkv(j).wait()
        load_p(j).wait()
        attend_backward(qkv, r, do_ref, p_ref, acc, ds_ref, fold, kind_ref, own_first)

        @pl.when(j == 0)
        def _():
            sums.add_and_gather(1)
            ff_sum.exchange_y()

        @pl.when(j == 1)
        def _():
            sums.add_and_gather(0)

        @pl.when(j == 2)
        def _():
            sums.add_and_gather(1)
            ff_sum.acquire()
            ff_sum.start()
            sums.add_and_gather(2)

        @pl.when(j == 3)
        def _():
            sums.add_and_gather(3)
            attention_results(1, at_sum.finish())
            at_sum.release()

        @pl.when(more)
        def _():
            load_p(j + 1).start()
            load_qkv(j + 1).start()

        dqkv[rows, 0:D] = (acc[:, 0:D] * SCALE).astype(BF16)
        dqkv[rows, D : 2 * D] = (acc[:, D : 2 * D] * SCALE).astype(BF16)
        dqkv[rows, 2 * D :] = acc[:, 2 * D :].astype(BF16)

        @pl.when(r == 1)
        def _():
            attention_weights(l)
            pl.when(l == 0)(lambda: at_sum.acquire())
            at_sum.start()
            pl.when(l == 1)(lambda: ff_sum.exchange_z())

        @pl.when(j == 3)
        def _():
            for k in HID_ORDER:
                small_scatter(k).start()

        @pl.when(j == 2)
        def _():
            for n in range(3):
                load_weight(0, n).wait()

        def back(n, _):
            cols = span(n * D, D, 128)
            got = dot_nt(dqkv[rows, cols], wqkv[:, cols])

            @pl.when(n == 0)
            def _():
                acc[:, 0:D] = got

            @pl.when(n > 0)
            def _():
                acc[:, 0:D] += got

            return 0

        lax.fori_loop(0, 3, back, 0)

        @pl.when(j == 1)
        def _():
            for n in range(3):
                load_weight(0, n).start()

        @pl.when(j == 3)
        def _():
            load_time_weight(0).start()
            for k in HID_ORDER:
                small_scatter(k).wait_recv()
            value = small[span(me * 8, 8, 8)]
            for k in range(HID - 1):
                value = value + small_recv[k]
            small_sum[0] = value
            swap(small_sum.at[0], small_pair, 0).start()

        for copy in load_norm(0, j):
            copy.wait()

        def first_norm(c, _):
            here = span(c * CHUNK, CHUNK, CHUNK)
            rr = span(base + c * CHUNK, CHUNK, CHUNK)
            dn = acc[here, 0:D]
            dy[rr] = dy[rr] + norm_slope(
                dn, unit[0, here].astype(F32), inv[0, here, 0:1], gain_ref[l, 0:1]
            )
            return 0

        lax.fori_loop(0, ROW_LEN // CHUNK, first_norm, 0)
        @pl.when(l == 1)
        def _():
            norm_sums(0, acc[mine, 0:D])

        @pl.when(l == 0)
        def _():
            late[0:1] += jnp.sum(acc[:, 0:D] * unit[0].astype(F32), 0, keepdims=True)
            late[1:2] += jnp.sum(acc[:, 0:D], 0, keepdims=True)

        @pl.when(j == 3)
        def _():
            swap(small_sum.at[0], small_pair, 0).wait_recv()
            small_chip[ff_sum.chip] = small_sum[0] + small_pair[...]
            for k in HID_ORDER:
                spread(small_chip, 2, k, True).start()
            swap(late, late_pair, 2).start()

        @pl.when(more)
        def _():
            for copy in load_norm(0, j + 1):
                copy.start()

        @pl.when(l == 0)
        def _():
            save_dx(r, rows).start()

        @pl.when(j == 2)
        def _():
            at_sum.exchange_z()
            ff_sum.exchange_y()

        @pl.when(l == 1)
        def _():
            @pl.when(r == 0)
            def _():
                for copy in load_feed_weights(0) + load_feed():
                    copy.wait()

            dxl[rows] = dy[rows].astype(BF16)
            gh = dot_nt(dxl[rows], wdown[...])
            load_u(r).wait()
            du = (gh * gelu_slope(u_ref[...])).astype(BF16)
            pl.when(r == 0)(lambda: load_u(1).start())
            du_ref[rows] = du
            sums.drain(r)
            part[r] = dot(du, wup[...]).astype(BF16)
            sums.scatter(r)

        @pl.when(j == 0)
        def _():
            sums.scatter(2)

        @pl.when(j == 1)
        def _():
            sums.scatter(3)
            at_sum.exchange_y()
            feed_results(1, ff_sum.finish())
            ff_sum.release()
            write_ff_grads(
                x2,
                lambda a, b: dot_tn(second[...], du_ref[:, a:b]),
                lambda a, b: dot_tn(dxl[...], g_ref[:, a:b]),
            )
            bias_sums(0)

        return 0

    lax.fori_loop(0, 4, backward_step, 0)

    ff_sum.exchange_z()
    swap(late, late_pair, 2).wait_recv()
    late_chip[ff_sum.chip] = late[...] + late_pair[...]
    for k in HID_ORDER:
        spread(late_chip, 6, k, True).start()
    for k in HID_ORDER:
        spread(small_chip, 2, k, False).wait_recv()
    value = small_chip[0]
    for c in range(1, 8):
        value = value + small_chip[c]
    small_out[span(me * 8, 8, 8)] = value
    for k in HID_ORDER:
        small_gather(k, True).start()
    at_sum.exchange_y()
    time_gradient(0)
    load_time_weight(1).start()
    feed_results(0, ff_sum.finish())
    for e in range(2):
        sums.wait(2 + e)
        save_fsum(e).start()
    for k in HID_ORDER:
        spread(late_chip, 6, k, False).wait_recv()
    value = late_chip[0]
    for c in range(1, 8):
        value = value + late_chip[c]
    at_sum.exchange_z()
    time_gradient(1)
    for k in HID_ORDER:
        small_gather(k, False).wait_recv()
    for l in range(LAYERS):
        for a in range(REL):
            at = (REL - 1 - a) * 32
            gtable_ref[l, a] = small_out[16 * l : 16 * l + 16, at : at + REL]
        for n in range(2):
            ggain_ref[l, n : n + 1] = small_out[32 + 2 * l + n : 33 + 2 * l + n]
            gshift_ref[l, n : n + 1] = small_out[36 + 2 * l + n : 37 + 2 * l + n]
        for n in range(4):
            gbup_out[l : l + 1, n * D : (n + 1) * D] = small_out[42 + 4 * l + n : 43 + 4 * l + n]
        gbdown_out[l : l + 1] = small_out[40 + l : 41 + l]
    ggain_ref[0, 0:1] = value[0:1]
    gshift_ref[0, 0:1] = value[1:2]
    attention_results(0, at_sum.finish())
    for k in HID_ORDER:
        small_scatter(k).wait_send()
        spread(small_chip, 2, k, True).wait_send()
        spread(late_chip, 6, k, True).wait_send()
        small_gather(k, True).wait_send()
    swap(small_sum.at[0], small_pair, 0).wait_send()
    swap(late, late_pair, 2).wait_send()
    for r in range(2):
        save_dx(r, both[r]).wait()
        save_fsum(r).wait()
    for e in range(4):
        sums.drain(e)


def layers(vmem_args, hbm_args):
    s = jax.ShapeDtypeStruct
    v = pltpu.VMEM
    dma = pltpu.SemaphoreType.DMA
    return pl.pallas_call(
        layers_kernel,
        out_shape=[
            s((2, SLOTS, D), F32),
            s((KEPT, LAYERS, 3 * D), F32),
            s((KEPT, LAYERS, 3 * D), F32),
            s((KEPT, LAYERS, D), F32),
            s((LAYERS, 72, UNITS), F32),
            s((LAYERS, 72, UNITS), F32),
            s((LAYERS, 2, D), F32),
            s((LAYERS, 2, D), F32),
            s((LAYERS, REL, HEADS, REL), F32),
            s((LAYERS, FF), F32),
            s((LAYERS, D), F32),
            s((TOKENS, D), F32),
            s((TOKENS, D), F32),
            s((2, ROW_LEN, D), BF16),
            s((LAYERS, TOKENS, 3 * D), BF16),
            s((LAYERS, 2, HEADS, ROW_LEN, ROW_LEN), BF16),
            s((LAYERS, 2, TOKENS, D), BF16),
            s((LAYERS, 2, TOKENS, 128), F32),
            s((TOKENS, D), BF16),
            s((TOKENS, UNITS), F32),
            s((TOKENS, UNITS), BF16),
        ],
        in_specs=[IN_VMEM] * len(vmem_args) + [IN_ANY] * len(hbm_args),
        out_specs=[IN_VMEM] * 11 + [IN_ANY] * 10,
        scratch_shapes=[
            v((D, 3 * D), BF16),
            v((D, D), BF16),
            v((UNITS, D), BF16),
            v((UNITS, D), BF16),
            v((HEADS, ROW_LEN, ROW_LEN), BF16),
            v((HEADS, ROW_LEN, ROW_LEN), BF16),
            v((ROW_LEN, 3 * D), BF16),
            v((2, ROW_LEN, D), BF16),
            v((2, ROW_LEN, 128), F32),
            v((D, 256), BF16),
            v((LAYERS, 2, TOKENS, 256), BF16),
            v((TOKENS, D), BF16),
            v((ROW_LEN, UNITS), F32),
            v((TOKENS, UNITS), BF16),
            v((4, ROW_LEN, D), BF16),
            v((4, ROW_LEN, D), BF16),
            v((4, HID - 1, SLICE, D), BF16),
            v((TOKENS, D), F32),
            v((TOKENS, D), BF16),
            v((TOKENS, D), BF16),
            v((ROW_LEN, D), BF16),
            v((ROW_LEN, 3 * D), F32),
            v((TOKENS, 3 * D), BF16),
            v((TOKENS, UNITS), BF16),
            v((ROW_LEN, ROW_LEN), F32),
            v((8, 2, 80, D), BF16),
            v((8, 80, D), BF16),
            v((7, 80, D), BF16),
            v((8, 64, D), BF16),
            v((7, 64, D), BF16),
            v((2, HEADS, OWN, ROW_LEN), F32),
            v((LAYERS, 8, 3 * D), F32),
            v((8, TOKENS), BF16),
            v((8, 256), BF16),
            v((64, D), F32),
            v((64, D), F32),
            v((7, 8, D), F32),
            v((1, 8, D), F32),
            v((8, D), F32),
            v((8, 8, D), F32),
            v((8, D), F32),
            v((8, D), F32),
            v((8, 8, D), F32),
            dma((19,)),
            dma((18,)),
            dma((4, 4, HID - 1)),
            dma((4,)),
            dma((4, 7)),
            pltpu.SemaphoreType.REGULAR,
            pltpu.SemaphoreType.REGULAR,
            dma((8, HID - 1)),
            dma((4,)),
        ],
        compiler_params=pltpu.CompilerParams(
            collective_id=1, has_side_effects=True, vmem_limit_bytes=VMEM_LIMIT
        ),
        name="layers",
    )(*vmem_args, *hbm_args)


def finish_kernel(bdown_ref, h_ref, fsum_ref, dx_ref, *refs):
    out_ref, grad_ref = refs[11:13]
    out_ref[...] = h_ref[...] + (fsum_ref[...].astype(F32) + bdown_ref[1:2])
    grad_ref[...] = dx_ref[...]

    @pl.when(pl.program_id(0) == 0)
    def _():
        for n in range(11):
            refs[13 + n][...] = refs[n][...]


def finish(b_down, h, fsum, dx, rest):
    s = jax.ShapeDtypeStruct
    block = pl.BlockSpec((256, D), lambda i: (i, 0))
    whole = [pl.BlockSpec(a.shape, functools.partial(lambda n, i: (0,) * n, a.ndim)) for a in rest]
    return pl.pallas_call(
        finish_kernel,
        out_shape=[s((TOKENS, D), F32)] * 2 + [s(a.shape, F32) for a in rest],
        grid=(2,),
        in_specs=[pl.BlockSpec((LAYERS, D), lambda i: (0, 0))] + [block] * 3 + whole,
        out_specs=[block] * 2 + whole,
        compiler_params=pltpu.CompilerParams(vmem_limit_bytes=VMEM_LIMIT),
        name="finish",
    )(b_down, h, fsum.reshape(TOKENS, D), dx, *rest)


def shards(
    block_in,
    time_tokens,
    layout,
    norm_gain,
    norm_bias,
    w_qkv,
    w_time,
    rel_table,
    w_out,
    w_up,
    b_up,
    w_down,
    b_down,
    cotangent,
):
    bias, tp, kind = prepare(layout, rel_table, time_tokens, w_time)
    results = layers(
        (norm_gain, norm_bias, b_up, b_down, tp, kind, time_tokens),
        (
            block_in.reshape(TOKENS, D),
            cotangent.reshape(TOKENS, D),
            w_qkv,
            w_out,
            jnp.swapaxes(w_up, 1, 2),
            w_down,
            w_time,
            bias,
        ),
    )
    dx, h, fsum = results[11:14]
    block_out, grad_in, *rest = finish(b_down, h, fsum, dx, results[:11])
    gtime, gq, gt, go, gup, gdown, ggain, gshift, gtable, gbup, gbdown = rest
    return (
        block_out.reshape(2, ROW_LEN, D),
        grad_in.reshape(2, ROW_LEN, D),
        gtime,
        ggain,
        gshift,
        jnp.swapaxes(gq, 0, 1),
        jnp.swapaxes(gt, 0, 1),
        jnp.swapaxes(gtable, 1, 2),
        jnp.swapaxes(go, 0, 1),
        gup,
        gbup,
        jnp.swapaxes(gdown, 1, 2),
        gbdown,
    )


def solution(mesh):
    in_specs = (
        P("dp", None, None),
        P("dp", None, None),
        P("dp"),
        P(),
        P(),
        P(),
        P(),
        P(),
        P(),
        P(None, None, "hid"),
        P(None, "hid"),
        P(None, "hid", None),
        P(),
        P("dp", None, None),
    )
    out_specs = (
        P("dp", None, None),
        P("dp", None, None),
        P("dp", None, None),
        P(),
        P(),
        P(None, ("dp", "hid"), None),
        P(None, ("dp", "hid"), None),
        P(),
        P(None, ("dp", "hid"), None),
        P(None, "dp", "hid"),
        P(),
        P(None, "hid", "dp"),
        P(),
    )
    return jax.shard_map(shards, mesh=mesh, in_specs=in_specs, out_specs=out_specs, check_vma=False)
```

```python
import functools

import jax
import jax.numpy as jnp
from jax import lax
from jax.experimental import pallas as pl
from jax.experimental.pallas import tpu as pltpu
from jax.sharding import PartitionSpec as P

D = 1152
HEADS = 16
HEAD_DIM = 72
FF = 4608
LAYERS = 2
GRID = 16
SUB = 8
ROW_LEN = 256
SLOTS = 4
REL = 31
DP = 16
HID = 8
UNITS = FF // HID
KEPT = D // (DP * HID)
TOKENS = 512
OWN = ROW_LEN // HID
SCALE = HEAD_DIM ** (-0.5)
MASKED_LOGIT = -1e30
NORM_EPSILON = 1e-06
F32 = jnp.float32
BF16 = jnp.bfloat16
MESH = pl.DeviceIdType.MESH
VMEM_LIMIT = 63 * 1024 * 1024
HIGHEST = lax.Precision.HIGHEST


def contract(a, b, da, db, precision=None):
    return lax.dot_general(
        a, b, (((da,), (db,)), ((), ())), preferred_element_type=F32, precision=precision
    )


def dot(a, b):
    return contract(a, b, 1, 0)


def dot_nt(a, b):
    return contract(a, b, 1, 1)


def dot_tn(a, b):
    return contract(a, b, 0, 0)


def span(start, size, multiple):
    return pl.ds(pl.multiple_of(start, multiple), size)


def gelu_parts(v):
    c = 0.7978845608028654
    square = v * v
    t = jnp.tanh(c * v * (1.0 + 0.044715 * square))
    return t, square


def gelu(v):
    t, _ = gelu_parts(v)
    return 0.5 * v * (1.0 + t)


def gelu_slope(v):
    c = 0.7978845608028654
    t, square = gelu_parts(v)
    return 0.5 * (1.0 + t) + 0.5 * v * (1.0 - t * t) * (c * (1.0 + 3.0 * 0.044715 * square))


def prepare_kernel(
    layout_ref, rel_ref, time_ref, wtime_ref, bias_ref, tp_ref, kind_ref, rows_ref, skew_ref, turned_ref
):
    g = pl.program_id(1)

    @pl.when(g == 0)
    def _():
        tp_ref[...] = jnp.zeros_like(tp_ref)
        for r in range(2):
            four = jnp.where(layout_ref[r] == 1, 1.0, 0.0)
            kind_ref[r, 0:1] = jnp.full((1, ROW_LEN), 1.0 - four, F32)
            kind_ref[r, 1:2] = jnp.full((1, ROW_LEN), four, F32)

    for part in range(2):

        @pl.when(g == part)
        def _():
            cols = slice(576 * part, 576 * (part + 1))
            tokens = [time_ref[r, :, cols].astype(F32) for r in range(2)]
            tp_ref[0] += dot(jnp.concatenate(tokens, axis=0).astype(BF16), wtime_ref[0])

    @pl.when(g == 1)
    def _():
        for r in range(2):

            @pl.when(layout_ref[r] != 1)
            def _():
                tp_ref[0, 4 * r : 4 * r + 4] = jnp.broadcast_to(
                    tp_ref[0, 4 * r : 4 * r + 1], (SLOTS, 3 * D)
                )

    for n in range(2):
        rows_ref[...] = jnp.zeros_like(rows_ref)
        rows_ref[:, 0:4, 0:REL] = rel_ref[0, :, pl.ds(8 * g + 4 * n, 4), :]
        table = rows_ref[:, 0]
        for i in range(1, 4):
            table = table + pltpu.roll(rows_ref[:, i], 32 * i, 1)
        four_heads(table, n, layout_ref, bias_ref, skew_ref, turned_ref)


def four_heads(table, n, layout_ref, bias_ref, skew_ref, turned_ref):
    first, second = layout_ref[0], layout_ref[1]

    def skewed(side, count, top):
        skew_ref[...] = jnp.zeros_like(skew_ref)
        for j in range(count):
            block = jnp.broadcast_to(table[top - j : top - j + 1], (side, 128))
            skew_ref[pl.ds(side * j, side)] = pltpu.roll(
                block, 113, 1, stride=1, stride_axis=0
            )

    def single(r):
        skewed(GRID, REL, REL - 1)
        turned_ref[...] = skew_ref[...].T
        for i in range(4):
            w = turned_ref[32 * i : 32 * i + GRID]
            for m in range(8):
                moved = w if m == 0 else pltpu.roll(w, 512 - 16 * m, 1)
                for t in range(2):
                    y = 15 - 8 * t - m
                    bias_ref[0, r, 4 * n + i, pl.ds(GRID * y, GRID), :] = moved[
                        :, 128 * t : 128 * t + ROW_LEN
                    ].astype(BF16)

    def quad(r):
        skewed(SUB, 15, 22)
        turned_ref[:, 0:128] = skew_ref[0:128].T
        half = lax.broadcasted_iota(jnp.int32, (2 * SUB, 128), 1) // 64
        closed = jnp.full((2 * SUB, 128), MASKED_LOGIT, F32).astype(BF16)
        for i in range(4):
            w = turned_ref[32 * i : 32 * i + SUB, 0:128]
            for y in range(0, SUB, 2):
                for odd in range(2):
                    moved = jnp.concatenate(
                        [
                            pltpu.roll(w, (128 + 64 * odd - (7 - y - m) * SUB) % 128, 1)
                            for m in range(2)
                        ],
                        axis=0,
                    )
                    moved = jnp.where(half == odd, moved, MASKED_LOGIT).astype(BF16)
                    for tile in range(2):
                        rows = pl.ds(64 * (2 * tile + odd) + SUB * y, 2 * SUB)
                        bias_ref[0, r, 4 * n + i, rows, 128 * tile : 128 * tile + 128] = moved
                        bias_ref[0, r, 4 * n + i, rows, 128 - 128 * tile : 256 - 128 * tile] = closed

    pl.when(first != 1)(lambda: single(0))
    pl.when(first == 1)(lambda: quad(0))

    @pl.when(first == second)
    def _():
        for i in range(4):
            bias_ref[0, 1, 4 * n + i] = bias_ref[0, 0, 4 * n + i]

    pl.when((first != second) & (second != 1))(lambda: single(1))
    pl.when((first != second) & (second == 1))(lambda: quad(1))


def prepare(layout, rel_table, time_tokens, w_time):
    return pl.pallas_call(
        prepare_kernel,
        out_shape=[
            jax.ShapeDtypeStruct((LAYERS, 2, HEADS, ROW_LEN, ROW_LEN), BF16),
            jax.ShapeDtypeStruct((LAYERS, 8, 3 * D), F32),
            jax.ShapeDtypeStruct((2, 2, ROW_LEN), F32),
        ],
        grid_spec=pltpu.PrefetchScalarGridSpec(
            num_scalar_prefetch=1,
            grid=(LAYERS, 2),
            in_specs=[
                pl.BlockSpec((1, REL, HEADS, REL), lambda l, g, _: (l, 0, 0, 0)),
                pl.BlockSpec((2, SLOTS, D), lambda l, g, _: (0, 0, 0)),
                pl.BlockSpec((1, 576, 3 * D), lambda l, g, _: (l, g, 0)),
            ],
            out_specs=[
                pl.BlockSpec((1, 2, 8, ROW_LEN, ROW_LEN), lambda l, g, _: (l, 0, g, 0, 0)),
                pl.BlockSpec((1, 8, 3 * D), lambda l, g, _: (l, 0, 0)),
                pl.BlockSpec((2, 2, ROW_LEN), lambda l, g, _: (0, 0, 0)),
            ],
            scratch_shapes=[
                pltpu.VMEM((REL, 8, 128), F32),
                pltpu.VMEM((512, 128), F32),
                pltpu.VMEM((128, 512), F32),
            ],
        ),
        compiler_params=pltpu.CompilerParams(vmem_limit_bytes=VMEM_LIMIT),
        name="prepare",
    )(layout, jnp.swapaxes(rel_table, 1, 2), time_tokens, w_time)


IN_VMEM = pl.BlockSpec(memory_space=pltpu.VMEM)
IN_ANY = pl.BlockSpec(memory_space=pl.ANY)
CHUNK = 128
HID_ORDER = (2, 6, 1, 4, 3, 7, 5)
SLICE = ROW_LEN // HID


def head_window(h):
    start = h * HEAD_DIM // 128 * 128
    offset = h * HEAD_DIM - start
    width = 128 if offset + HEAD_DIM <= 128 else 256
    lane = lax.broadcasted_iota(jnp.int32, (1, width), 1)
    mask = ((lane >= offset) & (lane < offset + HEAD_DIM)).astype(F32).astype(BF16)
    return start, width, mask


def hid_peer(me, k):
    return lax.rem(me // 2 + k // 2, 4) * 2 + lax.rem(me + k, 2)


def hid_source(me, k):
    return lax.rem(me // 2 + 4 - k // 2, 4) * 2 + lax.rem(me + k, 2)


def greet_hid(barrier, me):
    for k in HID_ORDER:
        pl.semaphore_signal(
            barrier, inc=1, device_id={"hid": hid_peer(me, k)}, device_id_type=MESH
        )


class HidSums:
    def __init__(self, part, recv, total, sems):
        self.part, self.recv, self.total = part, recv, total
        self.send1, self.recv1, self.send2, self.recv2 = sems
        self.me = lax.axis_index("hid")

    def scatter_copy(self, e, k):
        peer = hid_peer(self.me, k)
        return pltpu.make_async_remote_copy(
            src_ref=self.part.at[e, span(peer * SLICE, SLICE, SLICE)],
            dst_ref=self.recv.at[e, k - 1],
            send_sem=self.send1.at[e, k - 1],
            recv_sem=self.recv1.at[e, k - 1],
            device_id={"hid": peer},
            device_id_type=MESH,
        )

    def gather_copy(self, slot, e, k, outgoing):
        owner = self.me if outgoing else hid_source(self.me, k)
        rows = self.total.at[slot, span(owner * SLICE, SLICE, SLICE)]
        return pltpu.make_async_remote_copy(
            src_ref=rows,
            dst_ref=rows,
            send_sem=self.send2.at[e, k - 1],
            recv_sem=self.recv2.at[e, k - 1],
            device_id={"hid": hid_peer(self.me, k)},
            device_id_type=MESH,
        )

    def scatter(self, e):
        for k in HID_ORDER:
            self.scatter_copy(e, k).start()

    def add_and_gather(self, e):
        mine = span(self.me * SLICE, SLICE, SLICE)
        for k in HID_ORDER:
            self.scatter_copy(e, k).wait_recv()
        total = self.part[e, mine].astype(F32)
        for k in range(HID - 1):
            total = total + self.recv[e, k].astype(F32)
        self.total[e, mine] = total.astype(BF16)
        for k in HID_ORDER:
            self.gather_copy(e, e, k, True).start()

    def wait(self, e):
        for k in HID_ORDER:
            self.gather_copy(e, e, k, False).wait_recv()

    def drain(self, e):
        for k in HID_ORDER:
            self.scatter_copy(e, k).wait_send()
            self.gather_copy(e, e, k, True).wait_send()


def write_ff_grads(ffg, up_of, down_of):
    for n, of in enumerate((up_of, down_of)):
        for a, b in ((0, 128), (128, 256), (256, 384), (384, 512), (512, UNITS)):
            grad = of(a, b)
            for c in range(DP):
                ffg[c // 2, c % 2, 0:72, n * UNITS + a : n * UNITS + b] = grad[
                    72 * c : 72 * (c + 1)
                ].astype(BF16)


def layer_norm_rows(x, gain, shift):
    centre = x - jnp.mean(x, -1, keepdims=True)
    inverse = lax.rsqrt(jnp.mean(centre * centre, -1, keepdims=True) + NORM_EPSILON)
    unit = centre * inverse
    return (unit * gain + shift).astype(BF16), unit.astype(BF16), inverse


def kept_matrix():
    feature = lax.broadcasted_iota(jnp.int32, (D, 256), 0)
    column = lax.broadcasted_iota(jnp.int32, (D, 256), 1)
    low = column < 128
    owner = jnp.where(low, column // 8, column - 128)
    inner = jnp.where(low, column % 8, 8)
    chosen = (feature == owner * 72 + lax.axis_index("hid") * KEPT + inner) & (column < 144)
    return chosen.astype(F32).astype(BF16)


def attend_forward(qkv, bias_ref, p_ref, o_acc):
    o_acc[:, 0:D] = jnp.zeros((ROW_LEN, D), F32)

    def scores(h):
        start, width, mask = head_window(h)
        q = qkv[:, start : start + width] * mask
        return dot_nt(q, qkv[:, D + start : D + start + width])

    def mix(h, score):
        start, width, mask = head_window(h)
        logits = score * SCALE + bias_ref[h].astype(F32)
        expo = jnp.exp(logits - jnp.max(logits, -1, keepdims=True))
        p = (expo * (1.0 / jnp.sum(expo, -1, keepdims=True))).astype(BF16)
        p_ref[h] = p
        v = qkv[:, 2 * D + start : 2 * D + start + width] * mask
        o_acc[:, start : start + width] += dot(p, v)

    ready = {}
    for h in range(HEADS + 1):
        if h < HEADS:
            ready[h] = scores(h)
        if h:
            mix(h - 1, ready.pop(h - 1))


class DpSums:
    def __init__(self, x, pair, recv, sems, free):
        self.x, self.pair, self.recv, self.free = x, pair, recv, free
        self.pair_send, self.pair_recv, self.send, self.got = sems
        me = lax.axis_index("dp")
        self.y, self.z, self.core = me // 4, lax.rem(me // 2, 2), lax.rem(me, 2)
        self.chip = me // 2
        self.partner = self.chip * 2 + (1 - self.core)

    def other(self, k):
        return lax.rem(self.y + k // 2, 4) * 2 + lax.rem(self.z + k, 2)

    def peer(self, k):
        return {"dp": self.other(k) * 2 + self.core}

    def pair_copy(self):
        return pltpu.make_async_remote_copy(
            src_ref=self.x.at[:, 1 - self.core],
            dst_ref=self.pair,
            send_sem=self.pair_send,
            recv_sem=self.pair_recv,
            device_id={"dp": self.partner},
            device_id_type=MESH,
        )

    def start(self):
        self.pair_copy().start()

    def add_pair(self, c):
        both = self.x[c, self.core].astype(F32) + self.pair[c].astype(F32)
        self.pair[c] = both.astype(BF16)

    def release(self):
        pl.semaphore_signal(
            self.free, inc=1, device_id={"dp": self.partner}, device_id_type=MESH
        )
        for k in HID_ORDER:
            pl.semaphore_signal(self.free, inc=1, device_id=self.peer(k), device_id_type=MESH)

    def acquire(self):
        pl.semaphore_wait(self.free, 8)


class DirectSums(DpSums):
    def chip_copy(self, k):
        return pltpu.make_async_remote_copy(
            src_ref=self.pair.at[self.other(k)],
            dst_ref=self.recv.at[k - 1],
            send_sem=self.send.at[k - 1],
            recv_sem=self.got.at[k - 1],
            device_id=self.peer(k),
            device_id_type=MESH,
        )

    def exchange(self):
        self.pair_copy().wait_recv()
        for k in HID_ORDER + (0,):
            self.add_pair(self.other(k))
            if k:
                self.chip_copy(k).start()
        self.pair_copy().wait_send()

    def finish(self):
        total = self.pair[self.chip].astype(F32)
        for k in HID_ORDER:
            self.chip_copy(k).wait_recv()
            total = total + self.recv[k - 1].astype(F32)
        for k in HID_ORDER:
            self.chip_copy(k).wait_send()
        return total


class SteppedSums(DpSums):
    def y_copy(self, k):
        target = lax.rem(self.y + k, 4)
        return pltpu.make_async_remote_copy(
            src_ref=self.pair.at[pl.ds(2 * target, 2)],
            dst_ref=self.recv.at[pl.ds(2 * k - 2, 2)],
            send_sem=self.send.at[k - 1],
            recv_sem=self.got.at[k - 1],
            device_id=self.peer(2 * k),
            device_id_type=MESH,
        )

    def z_copy(self):
        return pltpu.make_async_remote_copy(
            src_ref=self.pair.at[2 * self.y + 1 - self.z],
            dst_ref=self.recv.at[6],
            send_sem=self.send.at[3],
            recv_sem=self.got.at[3],
            device_id=self.peer(1),
            device_id_type=MESH,
        )

    def exchange_y(self):
        self.pair_copy().wait_recv()
        for k in (2, 1, 3, 0):
            target = lax.rem(self.y + k, 4)
            for z in range(2):
                self.add_pair(2 * target + z)
            if k:
                self.y_copy(k).start()
        self.pair_copy().wait_send()

    def exchange_z(self):
        for k in (1, 3, 2):
            self.y_copy(k).wait_recv()
        for own in (False, True):
            z = self.z if own else 1 - self.z
            c = 2 * self.y + z
            block = self.pair[c].astype(F32)
            for k in (1, 2, 3):
                block = block + self.recv[2 * k - 2 + z].astype(F32)
            self.pair[c] = block.astype(BF16)
            if not own:
                self.z_copy().start()

    def finish(self):
        self.z_copy().wait_recv()
        total = self.pair[self.chip].astype(F32) + self.recv[6].astype(F32)
        for k in (1, 2, 3):
            self.y_copy(k).wait_send()
        self.z_copy().wait_send()
        return total


def norm_slope(dn, unit, inverse, gain):
    scaled = dn * gain
    return inverse * (
        scaled
        - jnp.mean(scaled, -1, keepdims=True)
        - unit * jnp.mean(scaled * unit, -1, keepdims=True)
    )


def attend_backward(qkv, r, do_ref, p_ref, acc, ds_ref, fold, kind_ref, own_first):
    acc[...] = jnp.zeros_like(acc)

    def slopes(h):
        start, width, mask = head_window(h)
        v = qkv[:, 2 * D + start : 2 * D + start + width] * mask
        return dot_nt(do_ref[:, start : start + width], v)

    def spread(h, dp):
        start, width, mask = head_window(h)
        p_low = p_ref[h]
        p = p_low.astype(F32)
        t = p * dp
        ds = t - p * jnp.sum(t, -1, keepdims=True)
        ds_ref[...] = ds
        low = ds.astype(BF16)
        k = qkv[:, D + start : D + start + width] * mask
        q = qkv[:, start : start + width] * mask
        do = do_ref[:, start : start + width] * mask
        acc[:, start : start + width] += dot(low, k)
        acc[:, D + start : D + start + width] += dot_tn(low, q)
        acc[:, 2 * D + start : 2 * D + start + width] += dot_tn(p_low, do)
        mine = ds_ref[span(own_first, OWN, OWN)]
        fold[0, h] += mine * kind_ref[r, 0:1]
        fold[1, h] += mine * kind_ref[r, 1:2]

    ready = {}
    depth = 2
    for h in range(HEADS + depth):
        if h < HEADS:
            ready[h] = slopes(h)
        if h >= depth:
            spread(h - depth, ready.pop(h - depth))


def two_part_dot(a, b):
    high = a.astype(BF16)
    low = (a - high.astype(F32)).astype(BF16)
    return dot(high, b) + dot(low, b)


def fold_tables(fold, me):
    lane = lax.broadcasted_iota(jnp.int32, (ROW_LEN, 512), 0)
    place = lax.broadcasted_iota(jnp.int32, (ROW_LEN, 512), 1)
    wide = (place == (lane // GRID) * 32 + 15 - lane % GRID).astype(F32).astype(BF16)
    inner = lane % (SUB * SUB)
    narrow = (place == (inner // SUB) * 32 + 15 - inner % SUB).astype(F32).astype(BF16)
    rest = jnp.zeros((HEADS, 512), F32)
    out = jnp.zeros((HEADS, 1024), F32)
    for kind, (side, chosen) in enumerate(((GRID, wide), (SUB, narrow))):
        lines = []
        for n in range(2):
            sums = fold[kind, 8 * n : 8 * (n + 1)].reshape(8 * OWN, ROW_LEN)
            wider = two_part_dot(sums, chosen).reshape(8 * OWN // side, side, 512)
            line = wider[:, 0]
            for x in range(1, side):
                line = line + pltpu.roll(wider[:, x], x, 1)
            lines.append(line.reshape(8, OWN // side, 512))
        for i in range(OWN // side):
            line = jnp.concatenate([part[:, i] for part in lines], axis=0)
            y = 2 * me + i if side == GRID else lax.rem(me, 2) * 4 + i
            out = out + pltpu.roll(
                jnp.concatenate([line, rest], axis=1), (15 - y) * 32, 1
            )
    return out


def layers_kernel(
    gain_ref,
    shift_ref,
    bup_ref,
    bdown_ref,
    tp_ref,
    kind_ref,
    time_ref,
    x_hbm,
    cot_hbm,
    wqkv_hbm,
    wout_hbm,
    wup_hbm,
    wdown_hbm,
    wtime_hbm,
    bias_hbm,
    gtime_ref,
    gq_ref,
    gt_ref,
    go_ref,
    gup_ref,
    gdown_ref,
    ggain_ref,
    gshift_ref,
    gtable_ref,
    gbup_out,
    gbdown_out,
    dx_hbm,
    h_hbm,
    fsum_hbm,
    qkv_hbm,
    p_hbm,
    unit_hbm,
    inv_hbm,
    second_hbm,
    u_hbm,
    g_hbm,
    wqkv,
    wout,
    wup,
    wdown,
    bias_ref,
    p_ref,
    qkv,
    unit,
    inv,
    keep_ref,
    kept,
    second,
    u_ref,
    g_ref,
    total,
    part,
    recv,
    dy,
    dhl,
    dxl,
    do_ref,
    acc,
    dqkv,
    du_ref,
    ds_ref,
    x2,
    pair2,
    recv2,
    pair3,
    recv3,
    fold,
    dproj,
    pick_ref,
    timek_ref,
    small,
    small_out,
    small_recv,
    small_sum,
    small_pair,
    small_chip,
    late,
    late_pair,
    late_chip,
    load_sem,
    save_sem,
    hid_sems,
    dp_sems,
    chip_sems,
    free2,
    free3,
    small_sems,
    small_one,
):
    me = lax.axis_index("hid")
    own_first = me * OWN
    mine = span(own_first, OWN, OWN)
    sums = HidSums(part, recv, total, tuple(hid_sems.at[n] for n in range(4)))
    ff_sum = SteppedSums(
        x2,
        pair2,
        recv2,
        (dp_sems.at[0], dp_sems.at[1], chip_sems.at[0], chip_sems.at[1]),
        free2,
    )
    at_sum, last_sum = (
        kind(
            x2.at[:, :, pl.ds(0, 64)],
            pair3,
            recv3,
            (dp_sems.at[2], dp_sems.at[3], chip_sems.at[2], chip_sems.at[3]),
            free3,
        )
        for kind in (SteppedSums, DirectSums)
    )

    def load(n, src, dst):
        return pltpu.make_async_copy(src, dst, load_sem.at[n])

    def save(n, src, dst):
        return pltpu.make_async_copy(src, dst, save_sem.at[n])

    def load_weight(l, n):
        cols = pl.ds(n * D, D)
        return load(n, wqkv_hbm.at[l, :, cols], wqkv.at[:, cols])

    def load_time_weight(l):
        return load(3, wtime_hbm.at[l], wqkv)

    def load_out(l):
        return load(4, wout_hbm.at[l], wout)

    def load_feed_weights(l):
        return [load(5, wup_hbm.at[l], wup), load(6, wdown_hbm.at[l], wdown)]

    def load_bias(i):
        return load(7, bias_hbm.at[i // 2, lax.rem(i, 2)], bias_ref)

    def load_x():
        return load(8, x_hbm, dhl)

    def load_cot():
        return load(9, cot_hbm, dxl)

    def place_of(j):
        return 1 - j // 2, span(lax.rem(j, 2) * ROW_LEN, ROW_LEN, ROW_LEN)

    def load_p(j):
        return load(10, p_hbm.at[1 - j // 2, lax.rem(j, 2)], p_ref)

    def load_qkv(j):
        l, rows = place_of(j)
        return load(11, qkv_hbm.at[l, rows], qkv)

    def load_norm(which, j):
        l, rows = place_of(j)
        return [
            load(12 + 2 * which, unit_hbm.at[l, which, rows], unit.at[which]),
            load(13 + 2 * which, inv_hbm.at[l, which, rows], inv.at[which]),
        ]

    def load_u(r):
        return load(16, u_hbm.at[span(r * ROW_LEN, ROW_LEN, ROW_LEN)], u_ref)

    def load_feed():
        return [load(17, second_hbm, second), load(18, g_hbm, g_ref)]

    def save_qkv(l, rows):
        return save(0, qkv, qkv_hbm.at[l, rows])

    def save_p(l, r):
        return save(1, p_ref, p_hbm.at[l, r])

    def save_norm(which, l, rows):
        return [
            save(2 + 2 * which, unit.at[which], unit_hbm.at[l, which, rows]),
            save(3 + 2 * which, inv.at[which], inv_hbm.at[l, which, rows]),
        ]

    def save_u(r, rows):
        return save(10 + r, u_ref, u_hbm.at[rows])

    def save_feed(r, rows):
        return [
            save(6 + r, second.at[rows], second_hbm.at[rows]),
            save(8 + r, g_ref.at[rows], g_hbm.at[rows]),
        ]

    def save_h(r, rows):
        return save(12 + r, dy.at[rows], h_hbm.at[rows])

    def save_dx(r, rows):
        return save(14 + r, dy.at[rows], dx_hbm.at[rows])

    def save_fsum(r):
        return save(16 + r, total.at[2 + r], fsum_hbm.at[r])

    load_x().start()
    for n in range(3):
        load_weight(0, n).start()
    load_bias(0).start()
    load_out(0).start()
    for copy in load_feed_weights(0):
        copy.start()
    load_cot().start()
    barrier = pltpu.get_barrier_semaphore()
    greet_hid(barrier, me)
    pl.semaphore_signal(
        barrier, inc=1, device_id={"dp": ff_sum.partner}, device_id_type=MESH
    )
    for k in HID_ORDER:
        pl.semaphore_signal(barrier, inc=1, device_id=ff_sum.peer(k), device_id_type=MESH)
    small[...] = jnp.zeros_like(small)
    late[...] = jnp.zeros_like(late)
    gtime_ref[...] = jnp.zeros_like(gtime_ref)
    keep_ref[...] = kept_matrix()
    tokens = [time_ref[r].astype(F32) for r in range(2)]
    timek_ref[...] = dot(
        jnp.concatenate(tokens, axis=0).astype(BF16), keep_ref[...]
    ).astype(BF16)
    quarter = lax.broadcasted_iota(jnp.int32, (8, ROW_LEN), 1) // 64
    owner = lax.broadcasted_iota(jnp.int32, (8, ROW_LEN), 0)
    for r in range(2):
        whole = (owner == 4 * r).astype(F32) * kind_ref[r, 0:1]
        parts = (owner == 4 * r + quarter).astype(F32) * kind_ref[r, 1:2]
        pick_ref[:, pl.ds(r * ROW_LEN, ROW_LEN)] = (whole + parts).astype(BF16)
    load_x().wait()
    pl.semaphore_wait(barrier, 15)

    def keep_features(l):
        for n in range(2):
            kept[l, n] = dot(dqkv[:, n * D : (n + 1) * D], keep_ref[...]).astype(BF16)

    def forward_step(i, _):
        l = i // 2
        r = lax.rem(i, 2)
        base = r * ROW_LEN
        rows = span(base, ROW_LEN, ROW_LEN)

        @pl.when(i > 0)
        def _():
            for which in range(2):
                for copy in save_norm(which, 0, rows):
                    copy.wait()
            save_qkv(0, rows).wait()

        @pl.when(l == 0)
        def _():
            dy[rows] = dhl[rows].astype(F32)

        @pl.when(l == 1)
        def _():
            pl.when(r == 0)(lambda: keep_features(0))
            for copy in save_feed(r, rows):
                copy.wait()
            sums.wait(r)
            dy[rows] = dy[rows] + (total[r].astype(F32) + bdown_ref[0:1])

        def norm(which):
            def body(c, _):
                here = span(c * CHUNK, CHUNK, CHUNK)
                rr = span(base + c * CHUNK, CHUNK, CHUNK)
                low, value, inverse = layer_norm_rows(
                    dy[rr], gain_ref[l, which : which + 1], shift_ref[l, which : which + 1]
                )
                if which == 0:
                    dqkv[rr, 0:D] = low
                else:
                    second[rr] = low
                unit[which, here] = value
                inv[which, here] = jnp.broadcast_to(inverse, (CHUNK, 128))
                return 0

            lax.fori_loop(0, ROW_LEN // CHUNK, body, 0)
            for copy in save_norm(which, l, rows):
                copy.start()

        norm(0)
        for n in range(3):

            @pl.when(r == 0)
            def _():
                load_weight(l, n).wait()

            cols = pl.ds(n * D, D)
            wide = dot(dqkv[rows, 0:D], wqkv[:, cols])
            for s in range(SLOTS):
                qkv[64 * s : 64 * (s + 1), cols] = (
                    wide[64 * s : 64 * (s + 1)] + tp_ref[l, pl.ds(4 * r + s, 1), cols]
                ).astype(BF16)

        @pl.when(i == 2)
        def _():
            sums.add_and_gather(1)

        save_qkv(l, rows).start()

        @pl.when(i == 1)
        def _():
            for n in range(3):
                load_weight(1, n).start()

        load_bias(i).wait()

        @pl.when(i > 0)
        def _():
            save_p(0, 0).wait()

        attend_forward(qkv, bias_ref, p_ref, acc)

        @pl.when((i == 1) | (i == 3))
        def _():
            sums.add_and_gather(0)

        save_p(l, r).start()

        @pl.when(i < 3)
        def _():
            load_bias(i + 1).start()

        dqkv[rows, D : 2 * D] = acc[:, 0:D].astype(BF16)

        @pl.when(r == 0)
        def _():
            load_out(l).wait()

        dy[rows] = dy[rows] + dot(dqkv[rows, D : 2 * D], wout[...])

        @pl.when(i == 1)
        def _():
            load_out(1).start()

        norm(1)

        @pl.when(r == 0)
        def _():
            for copy in load_feed_weights(l):
                copy.wait()

        @pl.when((i == 1) | (i == 2))
        def _():
            save_u(i - 1, pl.ds(0, ROW_LEN)).wait()

        u_ref[...] = dot_nt(second[rows], wup[...]) + bup_ref[pl.ds(l, 1)]
        g_ref[rows] = gelu(u_ref[...]).astype(BF16)

        @pl.when(l == 0)
        def _():
            part[r] = dot(g_ref[rows], wdown[...]).astype(BF16)
            sums.scatter(r)
            for copy in save_feed(r, rows):
                copy.start()
            save_u(r, rows).start()

        @pl.when(l == 1)
        def _():
            pl.when(r == 0)(lambda: load_cot().wait())
            gh = dot_nt(dxl[rows], wdown[...])
            du = (gh * gelu_slope(u_ref[...])).astype(BF16)
            du_ref[rows] = du
            sums.drain(r)
            part[r] = dot(du, wup[...]).astype(BF16)
            sums.scatter(r)
            save_h(r, rows).start()
            part[2 + r] = dot(g_ref[rows], wdown[...]).astype(BF16)

        @pl.when(i == 1)
        def _():
            for copy in load_feed_weights(1):
                copy.start()

        return 0

    lax.fori_loop(0, 4, forward_step, 0)

    both = pl.ds(0, ROW_LEN), pl.ds(ROW_LEN, ROW_LEN)
    save_p(0, 0).wait()
    load_p(0).start()
    save_qkv(0, both[1]).wait()
    load_qkv(0).start()
    for which in (1, 0):
        for copy in save_norm(which, 0, both[1]):
            copy.wait()
        for copy in load_norm(which, 0):
            copy.start()
    for copy in load_feed_weights(0):
        copy.start()
    load_u(0).start()
    write_ff_grads(
        x2,
        lambda a, b: dot_tn(second[...], du_ref[:, a:b]),
        lambda a, b: dot_tn(dxl[...], g_ref[:, a:b]),
    )
    ff_sum.start()
    for copy in load_feed():
        copy.start()
    keep_features(1)

    def bias_sums(l):
        odd = lax.rem(me, 2).astype(F32)
        value = jnp.sum(du_ref[...].astype(F32), 0, keepdims=True)
        small[pl.ds(42 + 4 * l + me // 2, 1)] = jnp.concatenate(
            [value * (1.0 - odd), value * odd], axis=1
        )
        for r in range(2):
            small[40 + l : 41 + l] += jnp.sum(
                dxl[span(r * ROW_LEN + own_first, OWN, OWN)].astype(F32), 0, keepdims=True
            )

    bias_sums(1)

    def attention_results(l, block):
        for j in range(KEPT):
            for n in range(7):
                at = 8 * n + j if j < 8 else 56 + n
                ref = gq_ref if n < 3 else gt_ref if n < 6 else go_ref
                ref[j, l : l + 1, pl.ds(n % 3 * D, D)] = block[at : at + 1]

    def feed_results(l, block):
        gup_ref[l] = block[0:72, 0:UNITS]
        gdown_ref[l] = block[0:72, UNITS : 2 * UNITS]

    def place(p, grad):
        half = lax.rem(p, 2)
        for c in range(DP):
            acc[span(16 * c + 8 * half, 8, 8), 0:D] = grad[8 * c : 8 * c + 8]
            acc[pl.ds(8 * c + p, 1), D : 2 * D] = grad[128 + c : 129 + c]

    def flush(pair):
        for c in range(DP):
            x2[c // 2, c % 2, span(16 * pair, 16, 16)] = acc[
                16 * c : 16 * (c + 1), 0:D
            ].astype(BF16)

    def attention_weights(l):
        acc[0:128, D : 2 * D] = jnp.zeros((128, D), F32)

        def project(n, _):
            cols = span(n * D, D, 128)
            dproj[l, :, cols] = dot(pick_ref[...], dqkv[:, cols])
            return 0

        lax.fori_loop(0, 3, project, 0)

        def token_piece(n, _):
            cols = span(n * D, D, 128)
            place(n, dot_tn(kept[l, 0, :, 0:144], dqkv[:, cols]))
            pl.when(n == 1)(lambda: flush(0))
            return 0

        lax.fori_loop(0, 3, token_piece, 0)

        def time_piece(n, _):
            cols = span(n * D, D, 128)
            place(3 + n, dot_tn(timek_ref[:, 0:144], dproj[l, :, cols].astype(BF16)))
            pl.when(n == 0)(lambda: flush(1))
            pl.when(n == 2)(lambda: flush(2))
            return 0

        lax.fori_loop(0, 3, time_piece, 0)
        place(6, dot_tn(kept[l, 1, :, 0:144], dhl[...]))
        for c in range(DP):
            acc[16 * c + 8 : 16 * c + 16, 0:D] = acc[8 * c : 8 * c + 8, D : 2 * D]
        flush(3)
        small[span(l * 16, 16, 16), 0:1024] = fold_tables(fold, me)

    def time_gradient(l):
        load_time_weight(l).wait()
        got = jnp.zeros((8, D), F32)
        for n in range(3):
            cols = pl.ds(n * D, D)
            got = got + dot_nt(dproj[l, :, cols].astype(BF16), wqkv[:, cols])
        for r in range(2):
            gtime_ref[r] += got[4 * r : 4 * r + 4]

    def small_scatter(k):
        peer = hid_peer(me, k)
        return pltpu.make_async_remote_copy(
            src_ref=small.at[span(peer * 8, 8, 8)],
            dst_ref=small_recv.at[k - 1],
            send_sem=small_sems.at[0, k - 1],
            recv_sem=small_sems.at[1, k - 1],
            device_id={"hid": peer},
            device_id_type=MESH,
        )

    def swap(src, dst, n):
        return pltpu.make_async_remote_copy(
            src_ref=src,
            dst_ref=dst,
            send_sem=small_one.at[n],
            recv_sem=small_one.at[n + 1],
            device_id={"dp": ff_sum.partner},
            device_id_type=MESH,
        )

    def spread(ref, n, k, outgoing):
        chip = ff_sum.chip
        if not outgoing:
            chip = lax.rem(ff_sum.y + 4 - k // 2, 4) * 2 + lax.rem(ff_sum.z + k, 2)
        return pltpu.make_async_remote_copy(
            src_ref=ref.at[chip],
            dst_ref=ref.at[chip],
            send_sem=small_sems.at[n, k - 1],
            recv_sem=small_sems.at[n + 1, k - 1],
            device_id=ff_sum.peer(k),
            device_id_type=MESH,
        )

    def small_gather(k, outgoing):
        owner = me if outgoing else hid_source(me, k)
        rows = small_out.at[span(owner * 8, 8, 8)]
        return pltpu.make_async_remote_copy(
            src_ref=rows,
            dst_ref=rows,
            send_sem=small_sems.at[4, k - 1],
            recv_sem=small_sems.at[5, k - 1],
            device_id={"hid": hid_peer(me, k)},
            device_id_type=MESH,
        )

    def backward_step(j, _):
        l = 1 - j // 2
        r = lax.rem(j, 2)
        base = r * ROW_LEN
        rows = span(base, ROW_LEN, ROW_LEN)
        more = j < 3

        for copy in load_norm(1, j):
            copy.wait()
        sums.wait(r)

        @pl.when(l == 1)
        def _():
            save_h(r, rows).wait()
            dy[rows] = dxl[rows].astype(F32)

        @pl.when(r == 0)
        def _():
            fold[...] = jnp.zeros_like(fold)

        def second_norm(c, _):
            here = span(c * CHUNK, CHUNK, CHUNK)
            rr = span(base + c * CHUNK, CHUNK, CHUNK)
            dn = total[r, here].astype(F32)
            dh = dy[rr] + norm_slope(
                dn, unit[1, here].astype(F32), inv[1, here, 0:1], gain_ref[l, 1:2]
            )
            dy[rr] = dh
            dhl[rr] = dh.astype(BF16)
            return 0

        lax.fori_loop(0, ROW_LEN // CHUNK, second_norm, 0)

        def norm_sums(which, dn):
            value = jnp.sum(dn * unit[which, mine].astype(F32), 0, keepdims=True)
            small[pl.ds(32 + 2 * l + which, 1)] += value
            small[pl.ds(36 + 2 * l + which, 1)] += jnp.sum(dn, 0, keepdims=True)

        norm_sums(1, total[r, mine].astype(F32))

        @pl.when(more)
        def _():
            for copy in load_norm(1, j + 1):
                copy.start()

        @pl.when(j == 2)
        def _():
            load_out(0).wait()

        do_ref[...] = dot_nt(dhl[rows], wout[...]).astype(BF16)

        @pl.when(j == 1)
        def _():
            load_out(0).start()

        load_qkv(j).wait()
        load_p(j).wait()
        attend_backward(qkv, r, do_ref, p_ref, acc, ds_ref, fold, kind_ref, own_first)

        @pl.when(j == 0)
        def _():
            sums.add_and_gather(1)
            ff_sum.exchange_y()

        @pl.when(j == 1)
        def _():
            sums.add_and_gather(0)

        @pl.when(j == 2)
        def _():
            sums.add_and_gather(1)
            ff_sum.acquire()
            ff_sum.start()
            sums.add_and_gather(2)

        @pl.when(j == 3)
        def _():
            sums.add_and_gather(3)
            attention_results(1, at_sum.finish())
            at_sum.release()

        @pl.when(more)
        def _():
            load_p(j + 1).start()
            load_qkv(j + 1).start()

        dqkv[rows, 0:D] = (acc[:, 0:D] * SCALE).astype(BF16)
        dqkv[rows, D : 2 * D] = (acc[:, D : 2 * D] * SCALE).astype(BF16)
        dqkv[rows, 2 * D :] = acc[:, 2 * D :].astype(BF16)

        @pl.when(r == 1)
        def _():
            attention_weights(l)
            pl.when(l == 0)(lambda: at_sum.acquire())
            at_sum.start()
            pl.when(l == 1)(lambda: ff_sum.exchange_z())

        @pl.when(j == 3)
        def _():
            for k in HID_ORDER:
                small_scatter(k).start()

        @pl.when(j == 2)
        def _():
            for n in range(3):
                load_weight(0, n).wait()

        def back(n, _):
            cols = span(n * D, D, 128)
            got = dot_nt(dqkv[rows, cols], wqkv[:, cols])

            @pl.when(n == 0)
            def _():
                acc[:, 0:D] = got

            @pl.when(n > 0)
            def _():
                acc[:, 0:D] += got

            return 0

        lax.fori_loop(0, 3, back, 0)

        @pl.when(j == 1)
        def _():
            for n in range(3):
                load_weight(0, n).start()

        @pl.when(j == 3)
        def _():
            load_time_weight(0).start()
            for k in HID_ORDER:
                small_scatter(k).wait_recv()
            value = small[span(me * 8, 8, 8)]
            for k in range(HID - 1):
                value = value + small_recv[k]
            small_sum[0] = value
            swap(small_sum.at[0], small_pair, 0).start()

        for copy in load_norm(0, j):
            copy.wait()

        def first_norm(c, _):
            here = span(c * CHUNK, CHUNK, CHUNK)
            rr = span(base + c * CHUNK, CHUNK, CHUNK)
            dn = acc[here, 0:D]
            dy[rr] = dy[rr] + norm_slope(
                dn, unit[0, here].astype(F32), inv[0, here, 0:1], gain_ref[l, 0:1]
            )
            return 0

        lax.fori_loop(0, ROW_LEN // CHUNK, first_norm, 0)
        @pl.when(l == 1)
        def _():
            norm_sums(0, acc[mine, 0:D])

        @pl.when(l == 0)
        def _():
            late[0:1] += jnp.sum(acc[:, 0:D] * unit[0].astype(F32), 0, keepdims=True)
            late[1:2] += jnp.sum(acc[:, 0:D], 0, keepdims=True)

        @pl.when(j == 3)
        def _():
            swap(small_sum.at[0], small_pair, 0).wait_recv()
            small_chip[ff_sum.chip] = small_sum[0] + small_pair[...]
            for k in HID_ORDER:
                spread(small_chip, 2, k, True).start()
            swap(late, late_pair, 2).start()

        @pl.when(more)
        def _():
            for copy in load_norm(0, j + 1):
                copy.start()

        @pl.when(l == 0)
        def _():
            save_dx(r, rows).start()

        @pl.when(j == 2)
        def _():
            at_sum.exchange_z()
            ff_sum.exchange_y()

        @pl.when(l == 1)
        def _():
            @pl.when(r == 0)
            def _():
                for copy in load_feed_weights(0) + load_feed():
                    copy.wait()

            dxl[rows] = dy[rows].astype(BF16)
            gh = dot_nt(dxl[rows], wdown[...])
            load_u(r).wait()
            du = (gh * gelu_slope(u_ref[...])).astype(BF16)
            pl.when(r == 0)(lambda: load_u(1).start())
            du_ref[rows] = du
            sums.drain(r)
            part[r] = dot(du, wup[...]).astype(BF16)
            sums.scatter(r)

        @pl.when(j == 0)
        def _():
            sums.scatter(2)

        @pl.when(j == 1)
        def _():
            sums.scatter(3)
            at_sum.exchange_y()
            feed_results(1, ff_sum.finish())
            ff_sum.release()
            write_ff_grads(
                x2,
                lambda a, b: dot_tn(second[...], du_ref[:, a:b]),
                lambda a, b: dot_tn(dxl[...], g_ref[:, a:b]),
            )
            bias_sums(0)

        return 0

    lax.fori_loop(0, 4, backward_step, 0)

    ff_sum.exchange_z()
    swap(late, late_pair, 2).wait_recv()
    late_chip[ff_sum.chip] = late[...] + late_pair[...]
    for k in HID_ORDER:
        spread(late_chip, 6, k, True).start()
    for k in HID_ORDER:
        spread(small_chip, 2, k, False).wait_recv()
    value = small_chip[0]
    for c in range(1, 8):
        value = value + small_chip[c]
    small_out[span(me * 8, 8, 8)] = value
    for k in HID_ORDER:
        small_gather(k, True).start()
    last_sum.exchange()
    time_gradient(0)
    load_time_weight(1).start()
    feed_results(0, ff_sum.finish())
    for e in range(2):
        sums.wait(2 + e)
        save_fsum(e).start()
    for k in HID_ORDER:
        spread(late_chip, 6, k, False).wait_recv()
    value = late_chip[0]
    for c in range(1, 8):
        value = value + late_chip[c]
    time_gradient(1)
    for k in HID_ORDER:
        small_gather(k, False).wait_recv()
    for l in range(LAYERS):
        for a in range(REL):
            at = (REL - 1 - a) * 32
            gtable_ref[l, a] = small_out[16 * l : 16 * l + 16, at : at + REL]
        for n in range(2):
            ggain_ref[l, n : n + 1] = small_out[32 + 2 * l + n : 33 + 2 * l + n]
            gshift_ref[l, n : n + 1] = small_out[36 + 2 * l + n : 37 + 2 * l + n]
        for n in range(4):
            gbup_out[l : l + 1, n * D : (n + 1) * D] = small_out[42 + 4 * l + n : 43 + 4 * l + n]
        gbdown_out[l : l + 1] = small_out[40 + l : 41 + l]
    ggain_ref[0, 0:1] = value[0:1]
    gshift_ref[0, 0:1] = value[1:2]
    attention_results(0, last_sum.finish())
    for k in HID_ORDER:
        small_scatter(k).wait_send()
        spread(small_chip, 2, k, True).wait_send()
        spread(late_chip, 6, k, True).wait_send()
        small_gather(k, True).wait_send()
    swap(small_sum.at[0], small_pair, 0).wait_send()
    swap(late, late_pair, 2).wait_send()
    for r in range(2):
        save_dx(r, both[r]).wait()
        save_fsum(r).wait()
    for e in range(4):
        sums.drain(e)


def layers(vmem_args, hbm_args):
    s = jax.ShapeDtypeStruct
    v = pltpu.VMEM
    dma = pltpu.SemaphoreType.DMA
    return pl.pallas_call(
        layers_kernel,
        out_shape=[
            s((2, SLOTS, D), F32),
            s((KEPT, LAYERS, 3 * D), F32),
            s((KEPT, LAYERS, 3 * D), F32),
            s((KEPT, LAYERS, D), F32),
            s((LAYERS, 72, UNITS), F32),
            s((LAYERS, 72, UNITS), F32),
            s((LAYERS, 2, D), F32),
            s((LAYERS, 2, D), F32),
            s((LAYERS, REL, HEADS, REL), F32),
            s((LAYERS, FF), F32),
            s((LAYERS, D), F32),
            s((TOKENS, D), F32),
            s((TOKENS, D), F32),
            s((2, ROW_LEN, D), BF16),
            s((LAYERS, TOKENS, 3 * D), BF16),
            s((LAYERS, 2, HEADS, ROW_LEN, ROW_LEN), BF16),
            s((LAYERS, 2, TOKENS, D), BF16),
            s((LAYERS, 2, TOKENS, 128), F32),
            s((TOKENS, D), BF16),
            s((TOKENS, UNITS), F32),
            s((TOKENS, UNITS), BF16),
        ],
        in_specs=[IN_VMEM] * len(vmem_args) + [IN_ANY] * len(hbm_args),
        out_specs=[IN_VMEM] * 11 + [IN_ANY] * 10,
        scratch_shapes=[
            v((D, 3 * D), BF16),
            v((D, D), BF16),
            v((UNITS, D), BF16),
            v((UNITS, D), BF16),
            v((HEADS, ROW_LEN, ROW_LEN), BF16),
            v((HEADS, ROW_LEN, ROW_LEN), BF16),
            v((ROW_LEN, 3 * D), BF16),
            v((2, ROW_LEN, D), BF16),
            v((2, ROW_LEN, 128), F32),
            v((D, 256), BF16),
            v((LAYERS, 2, TOKENS, 256), BF16),
            v((TOKENS, D), BF16),
            v((ROW_LEN, UNITS), F32),
            v((TOKENS, UNITS), BF16),
            v((4, ROW_LEN, D), BF16),
            v((4, ROW_LEN, D), BF16),
            v((4, HID - 1, SLICE, D), BF16),
            v((TOKENS, D), F32),
            v((TOKENS, D), BF16),
            v((TOKENS, D), BF16),
            v((ROW_LEN, D), BF16),
            v((ROW_LEN, 3 * D), F32),
            v((TOKENS, 3 * D), BF16),
            v((TOKENS, UNITS), BF16),
            v((ROW_LEN, ROW_LEN), F32),
            v((8, 2, 80, D), BF16),
            v((8, 80, D), BF16),
            v((7, 80, D), BF16),
            v((8, 64, D), BF16),
            v((7, 64, D), BF16),
            v((2, HEADS, OWN, ROW_LEN), F32),
            v((LAYERS, 8, 3 * D), F32),
            v((8, TOKENS), BF16),
            v((8, 256), BF16),
            v((64, D), F32),
            v((64, D), F32),
            v((7, 8, D), F32),
            v((1, 8, D), F32),
            v((8, D), F32),
            v((8, 8, D), F32),
            v((8, D), F32),
            v((8, D), F32),
            v((8, 8, D), F32),
            dma((19,)),
            dma((18,)),
            dma((4, 4, HID - 1)),
            dma((4,)),
            dma((4, 7)),
            pltpu.SemaphoreType.REGULAR,
            pltpu.SemaphoreType.REGULAR,
            dma((8, HID - 1)),
            dma((4,)),
        ],
        compiler_params=pltpu.CompilerParams(
            collective_id=1, has_side_effects=True, vmem_limit_bytes=VMEM_LIMIT
        ),
        name="layers",
    )(*vmem_args, *hbm_args)


def finish_kernel(bdown_ref, h_ref, fsum_ref, dx_ref, *refs):
    out_ref, grad_ref = refs[11:13]
    out_ref[...] = h_ref[...] + (fsum_ref[...].astype(F32) + bdown_ref[1:2])
    grad_ref[...] = dx_ref[...]

    @pl.when(pl.program_id(0) == 0)
    def _():
        for n in range(11):
            refs[13 + n][...] = refs[n][...]


def finish(b_down, h, fsum, dx, rest):
    s = jax.ShapeDtypeStruct
    block = pl.BlockSpec((256, D), lambda i: (i, 0))
    whole = [pl.BlockSpec(a.shape, functools.partial(lambda n, i: (0,) * n, a.ndim)) for a in rest]
    return pl.pallas_call(
        finish_kernel,
        out_shape=[s((TOKENS, D), F32)] * 2 + [s(a.shape, F32) for a in rest],
        grid=(2,),
        in_specs=[pl.BlockSpec((LAYERS, D), lambda i: (0, 0))] + [block] * 3 + whole,
        out_specs=[block] * 2 + whole,
        compiler_params=pltpu.CompilerParams(vmem_limit_bytes=VMEM_LIMIT),
        name="finish",
    )(b_down, h, fsum.reshape(TOKENS, D), dx, *rest)


def shards(
    block_in,
    time_tokens,
    layout,
    norm_gain,
    norm_bias,
    w_qkv,
    w_time,
    rel_table,
    w_out,
    w_up,
    b_up,
    w_down,
    b_down,
    cotangent,
):
    bias, tp, kind = prepare(layout, rel_table, time_tokens, w_time)
    results = layers(
        (norm_gain, norm_bias, b_up, b_down, tp, kind, time_tokens),
        (
            block_in.reshape(TOKENS, D),
            cotangent.reshape(TOKENS, D),
            w_qkv,
            w_out,
            jnp.swapaxes(w_up, 1, 2),
            w_down,
            w_time,
            bias,
        ),
    )
    dx, h, fsum = results[11:14]
    block_out, grad_in, *rest = finish(b_down, h, fsum, dx, results[:11])
    gtime, gq, gt, go, gup, gdown, ggain, gshift, gtable, gbup, gbdown = rest
    return (
        block_out.reshape(2, ROW_LEN, D),
        grad_in.reshape(2, ROW_LEN, D),
        gtime,
        ggain,
        gshift,
        jnp.swapaxes(gq, 0, 1),
        jnp.swapaxes(gt, 0, 1),
        jnp.swapaxes(gtable, 1, 2),
        jnp.swapaxes(go, 0, 1),
        gup,
        gbup,
        jnp.swapaxes(gdown, 1, 2),
        gbdown,
    )


def solution(mesh):
    in_specs = (
        P("dp", None, None),
        P("dp", None, None),
        P("dp"),
        P(),
        P(),
        P(),
        P(),
        P(),
        P(),
        P(None, None, "hid"),
        P(None, "hid"),
        P(None, "hid", None),
        P(),
        P("dp", None, None),
    )
    out_specs = (
        P("dp", None, None),
        P("dp", None, None),
        P("dp", None, None),
        P(),
        P(),
        P(None, ("dp", "hid"), None),
        P(None, ("dp", "hid"), None),
        P(),
        P(None, ("dp", "hid"), None),
        P(None, "dp", "hid"),
        P(),
        P(None, "hid", "dp"),
        P(),
    )
    return jax.shard_map(shards, mesh=mesh, in_specs=in_specs, out_specs=out_specs, check_vma=False)
```
